128 devices in a mesh: group: 4 (over y), fsdp: 8 (over x_lo, z), tp: 4 (over x_hi, core).
Axes of the slice: x: 4 (x_hi: 2, x_lo: 2; x = x_hi * 2 + x_lo), y: 4, z: 4, core: 2. Of those that a mesh axis runs over, the one named last changes fastest.
Arguments:
- noise_in: bfloat16 [256, 5120], P('fsdp'), may hold values from -6 to 6
- noise: bfloat16 [256, 5120], P('fsdp'), may hold values from -6 to 6
- timesteps: int32 [8], P('fsdp'), may hold values from 20 to 979
- up_weight: bfloat16 [4, 6912, 5120], P('group', ('fsdp', 'tp')), may hold values from -0.078125 to 0.078125
- down_weight: bfloat16 [4, 6912, 5120], P('group', ('fsdp', 'tp')), may hold values from -0.0546875 to 0.0546875
- small_params: float32 [3, 5, 5120], replicated, may hold values from -3 to 3
Outputs:
- score_gap: float32 [256, 5120], P('fsdp')
- up_grads: float32 [4, 6912, 5120], P('group', ('fsdp', 'tp'))
- down_grads: float32 [4, 6912, 5120], P('group', ('fsdp', 'tp'))
- small_grads: float32 [4, 5, 5120], P('group', None, ('fsdp', 'tp'))
The draws below stay inside these ranges and needn't reach their ends.
All inputs are finite; a program needn't handle non-finite values.
Results may differ from the reference program's by a relative error of at most 0.019.
Values may be sent and summed in bfloat16 or wider, within the bound.
A program may use at most 128 MiB of HBM per device.

```python
import math
import jax
import jax.numpy as jnp
from jax import lax

D = 5120
FF = 13824
FH = 6912
LTOK = 32
LATENTS = 8
TOKENS = 256


def set_ends(values, stream_key, low, high):
    dims = values.shape
    index_at = [jax.random.randint(jax.random.fold_in(stream_key, axis), (), 0, dims[axis]) for axis in range(len(dims))]
    values = values.at[tuple(index_at)].set(low)
    longest = dims.index(max(dims))
    index_at[longest] = (index_at[longest] + 1) % dims[longest]
    return values.at[tuple(index_at)].set(high)


def block_scale(own_key, shape, pieces, low, high):
    level, own = 1.0, jax.random.fold_in(own_key, 6)
    for dim, blocks in pieces:
        steps = jnp.exp(jax.random.uniform(jax.random.fold_in(own, dim), (blocks,), jnp.float32, low / len(pieces), high / len(pieces)))
        level = level * jnp.repeat(steps, shape[dim] // blocks).reshape([-1 if axis == dim else 1 for axis in range(len(shape))])
    return level


def normal_values(stream_key, shape, scale, most, cuts=(), kind=jnp.bfloat16):
    entries = scale * jax.random.normal(stream_key, shape, jnp.float32)
    if cuts:
        entries = entries * block_scale(stream_key, shape, cuts, -0.22, 0.18)
    return jnp.clip(entries, -most, most).astype(kind)


def setup_inputs(seed: int = 0) -> dict:
    keys = jax.random.split(jax.random.key(seed), 7)
    return {
        "noise_in": normal_values(keys[0], (TOKENS, D), 1.0, 6.0, ((0, 8),)),
        "noise": normal_values(keys[1], (TOKENS, D), 1.0, 6.0, ((0, 8),)),
        "timesteps": set_ends(jax.random.randint(keys[2], (LATENTS,), 20, 980), jax.random.fold_in(keys[2], 1), 20, 979).astype(jnp.int32),
        "up_weight": normal_values(keys[3], (4, FH, D), D ** -0.5, 0.078125, ((0, 4), (1, 32))),
        "down_weight": normal_values(keys[4], (4, FH, D), FF ** -0.5, 0.0546875, ((0, 4), (1, 32))),
        "small_params": normal_values(keys[5], (3, 5, D), 0.5, 3.0, (), jnp.float32),
    }


gen_time = 999.0
epsilon_norm = 1e-06
epsilon_gap = 1e-05

def gelu_tanh(inputs):
    return jax.nn.gelu(inputs, approximate=True)

def embedding(step_value, feature_width):
    half_width = feature_width // 2
    freqs = jnp.exp(-math.log(10000.0) * jnp.arange(half_width, dtype=jnp.float32) / half_width)
    angles = step_value[..., None] * freqs
    return jnp.concatenate([jnp.cos(angles), jnp.sin(angles)], axis=-1)

def forward(inputs, time_vec, params, up_rows, down_rows):
    values = inputs.astype(jnp.float32)
    center = lax.optimization_barrier(jnp.mean(values, axis=1, keepdims=True))
    spread = lax.optimization_barrier(jnp.mean(jnp.square(values - center), axis=1, keepdims=True))
    normed = (values - center) * lax.rsqrt(spread + epsilon_norm)
    layered = normed * (1.0 + params[0]) + params[1]
    scale_vec = params[3] + time_vec
    shift_vec = params[2] + time_vec
    gate_vec = params[4] + time_vec
    modulated = (layered * (1.0 + scale_vec) + shift_vec).astype(jnp.bfloat16)
    hidden_pre = jnp.dot(modulated, up_rows.T, preferred_element_type=jnp.float32)
    active = gelu_tanh(hidden_pre).astype(jnp.bfloat16)
    mixed_sum = jnp.dot(active, down_rows, preferred_element_type=jnp.float32)
    output = (values + gate_vec * mixed_sum).astype(jnp.bfloat16)
    return (output, (normed, layered, scale_vec, gate_vec, modulated, hidden_pre, active, mixed_sum))

def backward(cotangent, saved, up_rows, down_rows):
    normed, layered, scale_vec, gate_vec, modulated, hidden_pre, active, mixed_sum = saved
    gate_grad = lax.optimization_barrier(jnp.sum(cotangent * mixed_sum, axis=0))
    mixed_grad = (cotangent * gate_vec).astype(jnp.bfloat16)
    active_grad = jnp.dot(mixed_grad, down_rows.T, preferred_element_type=jnp.float32)
    hidden_grad = jax.vjp(gelu_tanh, hidden_pre)[1](active_grad)[0].astype(jnp.bfloat16)
    down_grad = jnp.dot(active.T, mixed_grad, preferred_element_type=jnp.float32)
    up_grad = jnp.dot(hidden_grad.T, modulated, preferred_element_type=jnp.float32)
    input_grad = jnp.dot(hidden_grad, up_rows, preferred_element_type=jnp.float32)
    layer_grad = input_grad * (1.0 + scale_vec)
    stacked = jnp.stack([lax.optimization_barrier(jnp.sum(layer_grad * normed, axis=0)), lax.optimization_barrier(jnp.sum(layer_grad, axis=0)), lax.optimization_barrier(jnp.sum(input_grad, axis=0)), lax.optimization_barrier(jnp.sum(input_grad * layered, axis=0)), gate_grad])
    return (up_grad, down_grad, stacked)

def reference(noise_in, noise, timesteps, up_weight, down_weight, small_params):
    step_values = timesteps.astype(jnp.float32)
    data_vec = jnp.repeat(embedding(step_values, D), LTOK, axis=0)
    gen_vec = embedding(jnp.full((1,), gen_time, jnp.float32), D)
    gen_up = jnp.concatenate([up_weight[0], up_weight[1]], axis=0)
    gen_down = jnp.concatenate([down_weight[0], down_weight[1]], axis=0)
    samples, gen_saved = forward(noise_in, gen_vec, small_params[0], gen_up, gen_down)
    noise_angle = jnp.repeat(0.5 * math.pi * step_values / 1000.0, LTOK)[:, None]
    sample_values = samples.astype(jnp.float32)
    noisy = (jnp.cos(noise_angle) * sample_values + jnp.sin(noise_angle) * noise.astype(jnp.float32)).astype(jnp.bfloat16)
    fake_out, critic_saved = forward(noisy, data_vec, small_params[1], up_weight[2], down_weight[2])
    real_out, teacher_saved = forward(noisy, data_vec, small_params[2], up_weight[3], down_weight[3])
    fake_pred = fake_out.astype(jnp.float32)
    real_pred = real_out.astype(jnp.float32)
    distance = jnp.abs(sample_values - real_pred).reshape(LATENTS, LTOK * D)
    scale_gap = jnp.repeat(lax.optimization_barrier(jnp.mean(distance, axis=1)) + epsilon_gap, LTOK)[:, None]
    score_gap = (fake_pred - real_pred) / scale_gap
    gen_up_grad, gen_down_grad, gen_small = backward(score_gap / LATENTS, gen_saved, gen_up, gen_down)
    critic_cot = (fake_pred - sample_values) / LATENTS
    critic_up_grad, critic_down_grad, critic_small = backward(critic_cot, critic_saved, up_weight[2], down_weight[2])
    empty_rows = jnp.zeros((FH, D), jnp.float32)
    up_grads = jnp.stack([gen_up_grad[:FH], gen_up_grad[FH:], critic_up_grad, empty_rows])
    down_grads = jnp.stack([gen_down_grad[:FH], gen_down_grad[FH:], critic_down_grad, empty_rows])
    small_grads = jnp.stack([gen_small, gen_small, critic_small, jnp.zeros((5, D), jnp.float32)])
    return (score_gap, up_grads, down_grads, small_grads)
```

```python
import functools
import math

import jax
import jax.numpy as jnp
from jax import lax
from jax.experimental import pallas as pl
from jax.experimental.pallas import tpu as pltpu
from jax.sharding import PartitionSpec as P

MESH = pl.DeviceIdType.MESH
bf16, f32 = jnp.bfloat16, jnp.float32
gen_time = 999.0
epsilon_norm = 1e-06
epsilon_gap = 1e-05

D = 5120
HU = 216
HP = 256
RB = 16
PW = 1280
SW = 160
CW = 512
NT = (((1,), (1,)), ((), ()))
FAR = (1, 3, 2)


def embedding(step_value, feature_width):
    half_width = feature_width // 2
    freqs = jnp.exp(-math.log(10000.0) * jnp.arange(half_width, dtype=f32) / half_width)
    angles = step_value * freqs
    return jnp.concatenate([jnp.cos(angles), jnp.sin(angles)], axis=-1)


def device(x, y, z, c):
    return (y, lax.rem(x, 2) * 4 + z, lax.div(x, 2) * 2 + c)


def turn(value, steps):
    return lax.rem(value + (steps % 4), 4)


def gelu_parts(h):
    k = math.sqrt(2.0 / math.pi)
    t = jnp.tanh(k * (h + 0.044715 * (h * h * h)))
    value = 0.5 * h * (1.0 + t)
    slope = 0.5 * (1.0 + t) + 0.5 * h * (1.0 - t * t) * (k * (1.0 + 3.0 * 0.044715 * (h * h)))
    return value, slope


def chain_kernel(
    up_ref, down_ref, nin_ref, noi_ref, vec_ref, par_ref,
    u_out, dz_out, dht_out, at_out, score_out, small_out,
    U, W, E, G1, G2, GC, DX, uu, XH, XS, DZ, H, HS, act, DA,
    zsA, zsB, rsA, rsB, sf, ss2, r2, Z, yS, yF, X0, Dv, CS, SM, T, TR, T2, TX, T3, TZ, TY,
    loc, wss, wrs, es, er,
    a1s, a1r, a2s, a2r, b1s, b1r, b2s, b2r, c1s, c1r, c2s, c2r,
    rs1s, rs1r, rs2s, rs2r, ys, yr, xs, xr, dxs, dxr, dzs, dzr, scs, scr, sms, smr,
):
    y = lax.axis_index("group")
    fi = lax.axis_index("fsdp")
    ti = lax.axis_index("tp")
    xl, z = lax.div(fi, 4), lax.rem(fi, 4)
    xh, c = lax.div(ti, 2), lax.rem(ti, 2)
    x = xh * 2 + xl
    role = jnp.maximum(y - 1, 0)
    is_gen = y < 2
    pending = []

    def xdev(d):
        return device(turn(x, d), y, z, c)

    def zdev(d):
        return device(x, y, turn(z, d), c)

    sib = device(x, y, z, 1 - c)

    def send(src, dst, s, r, dev):
        cp = pltpu.make_async_remote_copy(
            src_ref=src, dst_ref=dst, send_sem=s, recv_sem=r, device_id=dev, device_id_type=MESH
        )
        cp.start()
        return cp

    def sent(src, s):
        pltpu.make_async_copy(src, src, s).wait()

    def arrived(dst, r):
        pltpu.make_async_copy(dst, dst, r).wait()

    loads = [
        pltpu.make_async_copy(up_ref.at[0], U.at[0], loc.at[0]),
        pltpu.make_async_copy(down_ref.at[0], W.at[0], loc.at[1]),
    ]
    for cp in loads:
        cp.start()

    barrier = pltpu.get_barrier_semaphore()
    peers = [xdev(d) for d in FAR] + [zdev(d) for d in FAR]
    peers += [device(x, turn(y, d), z, c) for d in FAR] + [sib]
    for dev in peers:
        pl.semaphore_signal(barrier, inc=1, device_id=dev, device_id_type=MESH)
    pl.semaphore_wait(barrier, len(peers))

    def own_cols(p):
        return pl.ds(pl.multiple_of(xh * (2 * PW) + p * PW, 128), PW)

    own_rows = pl.ds(pl.multiple_of(c * RB, RB), RB)

    class Gather:
        def __init__(self, buf, order, s1s, s1r, s2s, s2r):
            self.buf, self.order = buf, order
            self.sems = (s1s, s1r, s2s, s2r)

        def block(self, d1, d2):
            if self.order == "xz":
                return self.buf.at[turn(x, -d1), turn(z, -d2)]
            return self.buf.at[turn(x, -d2), turn(z, -d1)]

        def peer(self, ring, d):
            return xdev(d) if (self.order == "xz") == (ring == 1) else zdev(d)

        def first(self):
            own = self.block(0, 0)
            for d in FAR:
                send(own, own, self.sems[0].at[d - 1], self.sems[1].at[d - 1], self.peer(1, d))

        def second(self, d1):
            b = self.block(d1, 0)
            for d in FAR:
                send(b, b, self.sems[2].at[d1, d - 1], self.sems[3].at[d1, d - 1], self.peer(2, d))

        def wait1(self, d1):
            arrived(self.block(d1, 0), self.sems[1].at[d1 - 1])

        def wait2(self, d1, d2):
            arrived(self.block(d1, d2), self.sems[3].at[d1, d2 - 1])

        def drain(self):
            own = self.block(0, 0)
            for d in FAR:
                sent(own, self.sems[0].at[d - 1])
                for d1 in range(4):
                    sent(own, self.sems[2].at[d1, d - 1])

    def gather_start(A, B):
        A.first()
        B.first()
        A.second(0)
        B.second(0)

    def gather_forward(A, B):
        for d in FAR:
            A.wait1(d)
            A.second(d)
            B.wait1(d)
            B.second(d)

    def gather_group(A, B, dz):
        if dz == 0:
            for d in FAR:
                B.wait2(0, d)
        else:
            for d1 in range(4):
                A.wait2(d1, dz)
            for d in FAR:
                B.wait2(dz, d)

    g1a = Gather(G1.at[0], "xz", a1s.at[0], a1r.at[0], a2s.at[0], a2r.at[0])
    g1b = Gather(G1.at[1], "zx", b1s.at[0], b1r.at[0], b2s.at[0], b2r.at[0])
    g2a = Gather(G2.at[0], "xz", a1s.at[1], a1r.at[1], a2s.at[1], a2r.at[1])
    g2b = Gather(G2.at[1], "zx", b1s.at[1], b1r.at[1], b2s.at[1], b2r.at[1])
    g2c = Gather(GC, "xz", c1s, c1r, c2s, c2r)

    @pl.when(is_gen)
    def _():
        for p in range(2):
            G1[p, x, z] = nin_ref[own_rows, own_cols(p)]
        gather_start(g1a, g1b)

    send(up_ref.at[0], U.at[1], wss.at[0], wrs.at[0], sib)
    send(down_ref.at[0], W.at[1], wss.at[1], wrs.at[1], sib)

    @pl.when(is_gen)
    def _():
        for l in range(8):
            E[l // 4, l % 4] = vec_ref[0:1, :]

    @pl.when(jnp.logical_not(is_gen))
    def _():
        E[xl, z] = vec_ref[1:2, :]
        own = E.at[xl, z]
        for d in FAR:
            send(own, own, es.at[d - 1], er.at[d - 1], zdev(d))
        for d in FAR:
            arrived(E.at[xl, turn(z, -d)], er.at[d - 1])
        send(E.at[xl], E.at[xl], es.at[3], er.at[3], xdev(1))
        arrived(E.at[1 - xl], er.at[3])

    H[...] = jnp.zeros_like(H)
    act[...] = jnp.zeros_like(act)
    DA[...] = jnp.zeros_like(DA)

    def make_x0():
        for p in range(2):
            total = yS[0, p].astype(f32) + yS[1, p].astype(f32)
            gate = par_ref[0, 4:5, own_cols(p)] + vec_ref[0:1, own_cols(p)]
            X0[p] = (nin_ref[own_rows, own_cols(p)].astype(f32) + gate * total).astype(bf16)

    def y_send(buf, slot, k):
        for d in FAR:
            send(buf.at[slot], buf.at[slot], ys.at[k, d - 1], yr.at[k, slot], device(x, turn(y, d), z, c))

    def y_drain(buf, k):
        for d in FAR:
            sent(buf.at[0], ys.at[k, d - 1])

    @pl.when(jnp.logical_not(is_gen))
    def _():
        arrived(yS.at[0], yr.at[0, 0])
        arrived(yS.at[1], yr.at[0, 1])
        make_x0()
        for p in range(2):
            cols = own_cols(p)
            noisy = vec_ref[2:3, cols] * X0[p].astype(f32) + vec_ref[3:4, cols] * noi_ref[own_rows, cols].astype(f32)
            G1[p, x, z] = noisy.astype(bf16)
        gather_start(g1a, g1b)

    gather_forward(g1a, g1b)

    def norm_rows(zz, xl_):
        rows = pl.ds(pl.multiple_of(zz * 32 + xl_ * RB, RB), RB)

        def piece(k):
            return G1[k % 2, 2 * (k // 2) + xl_, zz].astype(f32)

        mean = sum(jnp.sum(piece(k), axis=1, keepdims=True) for k in range(4)) / D
        var = sum(jnp.sum(jnp.square(piece(k) - mean), axis=1, keepdims=True) for k in range(4)) / D
        rstd = lax.rsqrt(var + epsilon_norm)
        for k in range(4):
            cols = slice(k * PW, (k + 1) * PW)
            e = E[xl_, zz, :, cols]
            scale = 1.0 + par_ref[role, 3:4, cols] + e
            gain = (1.0 + par_ref[role, 0:1, cols]) * scale
            bias = par_ref[role, 1:2, cols] * scale + (par_ref[role, 2:3, cols] + e)
            xhat = (piece(k) - mean) * rstd
            uu[rows, cols] = (xhat * gain + bias).astype(bf16)
            XH[rows, cols] = xhat.astype(bf16)
            XS[rows, cols] = (xhat * scale).astype(bf16)

    for dz in (0, 1, 3, 2):
        gather_group(g1a, g1b, dz)
        zz = turn(z, -dz)

        def both(i, carry, zz=zz):
            norm_rows(zz, i)
            return carry

        lax.fori_loop(0, 2, both, 0)
        if dz == 0:
            for cp in loads:
                cp.wait()
            arrived(U.at[1], wrs.at[0])
        rows = pl.ds(pl.multiple_of(zz * 32, 32), 32)
        for s in range(2):
            h = lax.dot_general(uu[rows, :], U[s], NT, preferred_element_type=f32)
            H[s, rows, 0:HU] = h

    for s in range(2):
        act[s] = gelu_parts(H[s])[0].astype(bf16)
    arrived(W.at[1], wrs.at[1])

    def z_piece(xh_, p):
        cols = slice((xh_ * 2 + p) * PW, (xh_ * 2 + p + 1) * PW)
        acc = jnp.dot(act[0, :, 0:HU], W[0, :, cols], preferred_element_type=f32)
        acc += jnp.dot(act[1, :, 0:HU], W[1, :, cols], preferred_element_type=f32)
        acc = acc.astype(bf16)
        for z_ in range(4):
            for xl_ in range(2):
                rows = acc[z_ * 32 + xl_ * RB : z_ * 32 + (xl_ + 1) * RB]
                if p == 0:
                    zsA[2 * xh_ + xl_, z_] = rows
                else:
                    zsB[z_, 2 * xh_ + xl_] = rows

    z_piece(0, 0)
    z_piece(1, 0)
    for d in FAR:
        send(zsA.at[turn(x, d)], rsA.at[d - 1], rs1s.at[0, d - 1], rs1r.at[0, d - 1], xdev(d))
    z_piece(0, 1)
    z_piece(1, 1)
    for d in FAR:
        send(zsB.at[turn(z, d)], rsB.at[d - 1], rs1s.at[1, d - 1], rs1r.at[1, d - 1], zdev(d))

    half = pl.ds(0, 128)
    other = pl.ds(128, 128)
    shared = [
        (H.at[1], HS, 0),
        (uu.at[half], uu.at[other], 1),
        (XH.at[half], XH.at[other], 2),
        (XS.at[half], XS.at[other], 3),
    ]
    for src, dst, k in shared:
        send(src, dst, xs.at[k], xr.at[k], sib)

    parts = ((0, zsA, rsA, x, z, zdev), (1, zsB, rsB, z, x, xdev))
    for p, zs, rs, first, second, peer in parts:
        for d in FAR:
            arrived(rs.at[d - 1], rs1r.at[p, d - 1])

        def add(i, carry, p=p, zs=zs, rs=rs, first=first):
            total = zs[first, i].astype(f32)
            for d in range(3):
                total += rs[d, i].astype(f32)
            sf[p, i] = total
            ss2[p, i] = total.astype(bf16)
            return carry

        lax.fori_loop(0, 4, add, 0)
        for d in FAR:
            send(ss2.at[p, turn(second, d)], r2.at[p, d - 1], rs2s.at[p, d - 1], rs2r.at[p, d - 1], peer(d))
    for p, zs, rs, first, second, peer in parts:
        for d in FAR:
            arrived(r2.at[p, d - 1], rs2r.at[p, d - 1])
        total = sf[p, second]
        for d in range(3):
            total += r2[p, d].astype(f32)
        Z[p] = total

    @pl.when(is_gen)
    def _():
        for p in range(2):
            yS[y, p] = Z[p].astype(bf16)
        y_send(yS, y, 0)
        arrived(yS.at[1 - y], yr.at[0, 1 - y])
        make_x0()
        for p in range(2):
            Z[p] = yS[0, p].astype(f32) + yS[1, p].astype(f32)
        arrived(yF.at[0], yr.at[1, 0])
        arrived(yF.at[1], yr.at[1, 1])

    @pl.when(jnp.logical_not(is_gen))
    def _():
        for p in range(2):
            gate = par_ref[role, 4:5, own_cols(p)] + vec_ref[1:2, own_cols(p)]
            yF[y - 2, p] = (G1[p, x, z].astype(f32) + gate * Z[p]).astype(bf16)
        y_send(yF, y - 2, 1)
        arrived(yF.at[3 - y], yr.at[1, 3 - y])

    dist = jnp.zeros((1, 1), f32)
    for p in range(2):
        fake, real, x0 = yF[0, p].astype(f32), yF[1, p].astype(f32), X0[p].astype(f32)
        gap = (fake - real).astype(bf16)
        Dv[p] = gap
        dist += jnp.sum(jnp.sum(jnp.abs(x0 - real), axis=1, keepdims=True), axis=0, keepdims=True)
        gate = par_ref[1, 4:5, own_cols(p)] + vec_ref[1:2, own_cols(p)]
        critic = ((fake - x0) * 0.125 * gate).astype(bf16)
        G2[p, x, z] = jnp.where(y == 2, critic, gap)
    gather_start(g2a, g2b)
    CS[0] = jnp.broadcast_to(dist, (8, 128))
    cs = send(CS.at[0], CS.at[1], scs.at[0], scr.at[0], sib)

    @pl.when(y == 2)
    def _():
        for p in range(2):
            DX[xh, p] = Dv[p]
        send(DX.at[xh], DX.at[xh], dxs, dxr, xdev(2))

    cs.wait_recv()
    GC[x, z] = CS[0] + CS[1]
    g2c.first()
    g2c.second(0)
    gather_forward(g2a, g2b)
    for d in FAR:
        g2c.wait1(d)
        g2c.second(d)

    def inverse(xl_, zz):
        mean = (GC[xl_, zz] + GC[2 + xl_, zz]) / (32.0 * D)
        return 1.0 / (mean + epsilon_gap)

    def scaled_rows(zz, xl_):
        rows = pl.ds(pl.multiple_of(zz * 32 + xl_ * RB, RB), RB)
        inv = inverse(xl_, zz)[0:1, 0:1] * 0.125
        for k in range(4):
            cols = slice(k * PW, (k + 1) * PW)
            gate = par_ref[0, 4:5, cols] + vec_ref[0:1, cols]
            factor = jnp.where(y == 2, jnp.ones_like(gate), inv * gate)
            DZ[rows, cols] = (G2[k % 2, 2 * (k // 2) + xl_, zz].astype(f32) * factor).astype(bf16)

    for i, dz in enumerate((0, 1, 3, 2)):
        gather_group(g2a, g2b, dz)
        if dz > 0:
            for d1 in range(4):
                g2c.wait2(d1, dz)
        zz = turn(z, -dz)

        def both(j, carry, zz=zz):
            scaled_rows(zz, j)
            return carry

        lax.fori_loop(0, 2, both, 0)
        rows = pl.ds(pl.multiple_of(zz * 32, 32), 32)
        orows = pl.ds(pl.multiple_of(128 + zz * 32, 32), 32)
        send(DZ.at[rows], DZ.at[orows], dzs.at[i], dzr.at[i], sib)

        if dz == 0:
            inv_own = inverse(xl, z)[0:1, 0:1]

            @pl.when(y == 2)
            def _():
                arrived(DX.at[1 - xh], dxr)
                for k in range(4):
                    score_out[own_rows, k * PW : (k + 1) * PW] = DX[k // 2, k % 2].astype(f32) * inv_own

            @pl.when(y != 2)
            def _():
                for k in range(4):
                    score_out[own_rows, k * PW : (k + 1) * PW] = G2[k % 2, 2 * (k // 2) + xl, z].astype(f32) * inv_own

            send(score_out.at[own_rows], score_out.at[own_rows], scs.at[1], scr.at[1], sib)

    live = y < 3
    for s in range(2):
        rows = slice(s * 128, (s + 1) * 128)
        if s == 1:
            arrived(HS, xr.at[0])
            for i, dz in enumerate((0, 1, 3, 2)):
                orows = pl.ds(pl.multiple_of(128 + turn(z, -dz) * 32, 32), 32)
                arrived(DZ.at[orows], dzr.at[i])
        da = lax.dot_general(DZ[rows, :], W[0], NT, preferred_element_type=f32)
        DA[rows, 0:HU] = da
        value, slope = gelu_parts(H[0] if s == 0 else HS[...])
        dh = jnp.where(live, DA[rows, :] * slope, 0.0)
        DA[rows, :] = dh
        dht_out[:, rows] = dh.T.astype(bf16)
        at_out[:, rows] = jnp.where(live, value, 0.0).T.astype(bf16)

    for k in range(1, 4):
        arrived((uu, XH, XS)[k - 1].at[other], xr.at[k])
    outs = [
        pltpu.make_async_copy(uu, u_out, loc.at[2]),
        pltpu.make_async_copy(DZ, dz_out, loc.at[3]),
    ]
    for cp in outs:
        cp.start()

    latent = lax.broadcasted_iota(jnp.int32, (8, 256), 0)
    token = lax.broadcasted_iota(jnp.int32, (8, 256), 1)
    pick = (lax.div(lax.rem(token, 128), RB) == latent).astype(bf16)
    sums = jnp.dot(pick, DA[...].astype(bf16), preferred_element_type=f32)
    high = sums.astype(bf16)
    low = (sums - high.astype(f32)).astype(bf16)
    hilo = jnp.concatenate([high, low], axis=0)[:, 0:HU]
    SM[...] = jnp.zeros_like(SM)

    def small(i, carry):
        cols = pl.ds(pl.multiple_of(i * CW, CW), CW)
        uw = U[0, :, cols]
        uf = uw.astype(f32)
        both = jnp.dot(hilo, uw, preferred_element_type=f32)
        by_latent = both[0:8] + both[8:16]
        x1 = jnp.dot(dht_out[...], XH[:, cols], preferred_element_type=f32)[0:HU]
        x2 = jnp.dot(dht_out[...], XS[:, cols], preferred_element_type=f32)[0:HU]
        s1 = jnp.sum(x1 * uf, axis=0, keepdims=True)
        s2 = jnp.sum(x2 * uf, axis=0, keepdims=True)
        s3 = jnp.sum(by_latent, axis=0, keepdims=True)
        sdl = (1.0 + par_ref[role, 3:4, cols]) * s3
        for l in range(8):
            sdl += E[l % 2, l // 2, :, cols] * by_latent[l : l + 1]
        SM[0:1, cols] = s2
        SM[1:2, cols] = sdl
        SM[2:3, cols] = s3
        SM[3:4, cols] = (1.0 + par_ref[role, 0:1, cols]) * s1 + par_ref[role, 1:2, cols] * s3
        return carry

    lax.fori_loop(0, D // CW, small, 0)

    inv_own = inverse(xl, z)[0:1, 0:1]
    for p in range(2):
        fake, x0 = yF[0, p].astype(f32), X0[p].astype(f32)
        cot = jnp.where(y == 2, fake - x0, Dv[p].astype(f32) * inv_own) * 0.125
        row = jnp.sum(cot * Z[p], axis=0, keepdims=True)
        SM[4:5, own_cols(p)] = jnp.where(jnp.logical_or(y == 0, y == 2), row, 0.0)

    for k in range(32):
        start = k * SW // 128 * 128
        window = SM[:, start : start + 256]
        off = k * SW - start
        if off:
            window = pltpu.roll(window, 256 - off, 1)
        f_, t_ = k // 4, k % 4
        T[t_ % 2, (t_ // 2) * 2 + f_ // 4, f_ % 4] = window

    tc = send(T.at[1 - c], TR, sms.at[0], smr.at[0], sib)
    arrived(TR, smr.at[0])
    T2[...] = T[c] + TR[...]
    for d in FAR:
        send(T2.at[turn(x, d)], TX.at[d - 1], sms.at[d], smr.at[d], xdev(d))
    for d in FAR:
        arrived(TX.at[d - 1], smr.at[d])
    T3[...] = T2[x] + TX[0] + TX[1] + TX[2]
    for d in FAR:
        send(T3.at[turn(z, d)], TZ.at[d - 1], sms.at[3 + d], smr.at[3 + d], zdev(d))
    for d in FAR:
        arrived(TZ.at[d - 1], smr.at[3 + d])
    small_out[...] = T3[z] + TZ[0] + TZ[1] + TZ[2]

    @pl.when(is_gen)
    def _():
        TY[0] = small_out[...]
        cp = send(TY.at[0], TY.at[1], sms.at[7], smr.at[7], device(x, 1 - y, z, c))
        cp.wait()
        small_out[...] = TY[0] + TY[1]

    arrived(score_out.at[pl.ds(pl.multiple_of((1 - c) * RB, RB), RB)], scr.at[1])
    sent(score_out.at[own_rows], scs.at[1])
    sent(CS.at[0], scs.at[0])
    sent(T.at[0], sms.at[0])
    for d in FAR:
        sent(T2.at[0], sms.at[d])
        sent(T3.at[0], sms.at[3 + d])
    for g in (g1a, g1b, g2a, g2b, g2c):
        g.drain()
    sent(up_ref.at[0], wss.at[0])
    sent(down_ref.at[0], wss.at[1])
    for src, dst, k in shared:
        sent(src, xs.at[k])
    for p, zs, rs, first, second, peer in parts:
        for d in FAR:
            sent(rs.at[0], rs1s.at[p, d - 1])
            sent(r2.at[p, 0], rs2s.at[p, d - 1])
    for i in range(4):
        sent(DZ.at[pl.ds(0, 32)], dzs.at[i])

    @pl.when(is_gen)
    def _():
        y_drain(yS, 0)

    @pl.when(jnp.logical_not(is_gen))
    def _():
        y_drain(yF, 1)
        for d in FAR:
            sent(E.at[0, 0], es.at[d - 1])
        sent(E.at[0], es.at[3])

    @pl.when(y == 2)
    def _():
        sent(DX.at[0], dxs)

    for cp in outs:
        cp.wait()


def weight_kernel(dht_ref, at_ref, u_ref, dz_ref, up_ref, down_ref):
    up_ref[0] = jnp.dot(dht_ref[...], u_ref[...], preferred_element_type=f32)[0:HU]
    down_ref[0] = jnp.dot(at_ref[...], dz_ref[...], preferred_element_type=f32)[0:HU]


def per_device(noise_in, noise, timesteps, up_weight, down_weight, small_params):
    step_value = timesteps[0].astype(f32)
    angle = 0.5 * math.pi * step_value / 1000.0
    vec = jnp.stack(
        [
            embedding(jnp.float32(gen_time), D),
            embedding(step_value, D),
            jnp.full((D,), jnp.cos(angle)),
            jnp.full((D,), jnp.sin(angle)),
        ]
    )
    dma = pltpu.SemaphoreType.DMA
    vm = pltpu.VMEM
    vmem = pl.BlockSpec(memory_space=pltpu.VMEM)
    hbm = pl.BlockSpec(memory_space=pl.ANY)
    scratch = [
        vm((2, HU, D), bf16),
        vm((2, HU, D), bf16),
        vm((2, 4, 1, D), f32),
        vm((2, 4, 4, RB, PW), bf16),
        vm((2, 4, 4, RB, PW), bf16),
        vm((4, 4, 8, 128), f32),
        vm((2, 2, RB, PW), bf16),
        vm((256, D), bf16),
        vm((256, D), bf16),
        vm((256, D), bf16),
        vm((256, D), bf16),
        vm((2, 128, HP), f32),
        vm((128, HP), f32),
        vm((2, 128, HP), bf16),
        vm((256, HP), f32),
        vm((4, 4, RB, PW), bf16),
        vm((4, 4, RB, PW), bf16),
        vm((3, 4, RB, PW), bf16),
        vm((3, 4, RB, PW), bf16),
        vm((2, 4, RB, PW), f32),
        vm((2, 4, RB, PW), bf16),
        vm((2, 3, RB, PW), bf16),
        vm((2, RB, PW), f32),
        vm((2, 2, RB, PW), bf16),
        vm((2, 2, RB, PW), bf16),
        vm((2, RB, PW), bf16),
        vm((2, RB, PW), bf16),
        vm((2, 8, 128), f32),
        vm((8, D), f32),
        vm((2, 4, 4, 8, 256), f32),
        vm((4, 4, 8, 256), f32),
        vm((4, 4, 8, 256), f32),
        vm((3, 4, 8, 256), f32),
        vm((4, 8, 256), f32),
        vm((3, 8, 256), f32),
        vm((2, 8, 256), f32),
        dma((4,)), dma((2,)), dma((2,)), dma((4,)), dma((4,)),
        dma((2, 3)), dma((2, 3)), dma((2, 4, 3)), dma((2, 4, 3)),
        dma((2, 3)), dma((2, 3)), dma((2, 4, 3)), dma((2, 4, 3)),
        dma((3,)), dma((3,)), dma((4, 3)), dma((4, 3)),
        dma((2, 3)), dma((2, 3)), dma((2, 3)), dma((2, 3)),
        dma((2, 3)), dma((2, 2)), dma((4,)), dma((4,)), dma(()), dma(()),
        dma((4,)), dma((4,)), dma((2,)), dma((2,)), dma((8,)), dma((8,)),
    ]
    u_all, dz_all, dht, at, score, small = pl.pallas_call(
        chain_kernel,
        out_shape=[
            jax.ShapeDtypeStruct((256, D), bf16),
            jax.ShapeDtypeStruct((256, D), bf16),
            jax.ShapeDtypeStruct((HP, 256), bf16),
            jax.ShapeDtypeStruct((HP, 256), bf16),
            jax.ShapeDtypeStruct((32, D), f32),
            jax.ShapeDtypeStruct((8, 256), f32),
        ],
        in_specs=[hbm, hbm, vmem, vmem, vmem, vmem],
        out_specs=[hbm, hbm, vmem, vmem, vmem, vmem],
        scratch_shapes=scratch,
        compiler_params=pltpu.CompilerParams(
            collective_id=0, has_side_effects=True, vmem_limit_bytes=56 * 2**20
        ),
        name="chain",
    )(up_weight, down_weight, noise_in, noise, vec, small_params)
    full = pl.BlockSpec((HP, 256), lambda i: (0, 0))
    cols = pl.BlockSpec((256, CW), lambda i: (0, i))
    out = pl.BlockSpec((1, HU, CW), lambda i: (0, 0, i))
    up_grad, down_grad = pl.pallas_call(
        weight_kernel,
        grid=(D // CW,),
        out_shape=[jax.ShapeDtypeStruct((1, HU, D), f32)] * 2,
        in_specs=[full, full, cols, cols],
        out_specs=[out, out],
        name="weight_grads",
    )(dht, at, u_all, dz_all)
    return (score, up_grad, down_grad, small[None, 0:5, 0:SW])


def solution(mesh):
    in_specs = (
        P("fsdp", None),
        P("fsdp", None),
        P("fsdp"),
        P("group", ("fsdp", "tp"), None),
        P("group", ("fsdp", "tp"), None),
        P(),
    )
    out_specs = (
        P("fsdp", None),
        P("group", ("fsdp", "tp"), None),
        P("group", ("fsdp", "tp"), None),
        P("group", None, ("fsdp", "tp")),
    )
    return jax.shard_map(
        per_device, mesh=mesh, in_specs=in_specs, out_specs=out_specs, check_vma=False
    )
```

```python
import functools
import math

import jax
import jax.numpy as jnp
from jax import lax
from jax.experimental import pallas as pl
from jax.experimental.pallas import tpu as pltpu
from jax.sharding import PartitionSpec as P

MESH = pl.DeviceIdType.MESH
bf16, f32 = jnp.bfloat16, jnp.float32
gen_time = 999.0
epsilon_norm = 1e-06
epsilon_gap = 1e-05

D = 5120
HU = 216
HP = 256
RB = 16
PW = 1280
SW = 160
CW = 512
NT = (((1,), (1,)), ((), ()))
FAR = (1, 3, 2)

def embedding(step_value, feature_width):
    half_width = feature_width // 2
    freqs = jnp.exp(-math.log(10000.0) * jnp.arange(half_width, dtype=f32) / half_width)
    angles = step_value * freqs
    return jnp.concatenate([jnp.cos(angles), jnp.sin(angles)], axis=-1)

def device(x, y, z, c):
    return (y, lax.rem(x, 2) * 4 + z, lax.div(x, 2) * 2 + c)

def turn(value, steps):
    return lax.rem(value + (steps % 4), 4)

def gelu_parts(h):
    k = math.sqrt(2.0 / math.pi)
    t = jnp.tanh(k * (h + 0.044715 * (h * h * h)))
    value = 0.5 * h * (1.0 + t)
    slope = 0.5 * (1.0 + t) + 0.5 * h * (1.0 - t * t) * (k * (1.0 + 3.0 * 0.044715 * (h * h)))
    return value, slope

def chain_kernel(
    up_ref, down_ref, nin_ref, noi_ref, vec_ref, par_hbm,
    uu, DZ, dht_out, at_out, score_out, small_out,
    par_ref, U, UT, W, E, G1, G2, GC, DX, XH, H, HS, act, DA, dhb,
    zsA, zsB, rsA, rsB, sf, ss2, r2, Z, yS, yF, X0, Dv, CS, SM, T, TX, T3, TZ,
    loc, wss, wrs, es, er,
    a1s, a1r, a2s, a2r, b1s, b1r, b2s, b2r, c1s, c1r, c2s, c2r,
    rsAs, rsAr, rsBs, rsBr, rs2s, rs2r, ys, yr, xs, xr, dxs, dxr, dzs, dzr, scs, scr, t1s, t1r, t2s, t2r,
):
    y = lax.axis_index("group")
    fi = lax.axis_index("fsdp")
    ti = lax.axis_index("tp")
    xl, z = lax.div(fi, 4), lax.rem(fi, 4)
    xh, c = lax.div(ti, 2), lax.rem(ti, 2)
    x = xh * 2 + xl
    role = jnp.maximum(y - 1, 0)
    is_gen = y < 2
    pending = []

    def xdev(d):
        return device(turn(x, d), y, z, c)

    def zdev(d):
        return device(x, y, turn(z, d), c)

    sib = device(x, y, z, 1 - c)

    def send(src, dst, s, r, dev):
        cp = pltpu.make_async_remote_copy(
            src_ref=src, dst_ref=dst, send_sem=s, recv_sem=r, device_id=dev, device_id_type=MESH
        )
        cp.start()
        return cp

    def sent(src, s):
        pltpu.make_async_copy(src, src, s).wait()

    def arrived(dst, r):
        pltpu.make_async_copy(dst, dst, r).wait()

    loads = [
        pltpu.make_async_copy(up_ref.at[0], U, loc.at[0]),
        pltpu.make_async_copy(down_ref.at[0], W.at[0], loc.at[1]),
        pltpu.make_async_copy(par_hbm, par_ref, loc.at[2]),
    ]
    for cp in loads:
        cp.start()

    barrier = pltpu.get_barrier_semaphore()
    peers = [xdev(d) for d in FAR] + [zdev(d) for d in FAR]
    peers += [device(x, turn(y, d), z, c) for d in FAR] + [sib]
    twin = y + 1 - 2 * lax.rem(y, 2)
    peers += [device(turn(x, d), y, z, 1 - c) for d in FAR]
    peers += [device(x, twin, turn(z, d), c) for d in FAR]
    for dev in peers:
        pl.semaphore_signal(barrier, inc=1, device_id=dev, device_id_type=MESH)
    pl.semaphore_wait(barrier, len(peers))

    def own_cols(p):
        return pl.ds(pl.multiple_of(xh * (2 * PW) + p * PW, 128), PW)

    own_rows = pl.ds(pl.multiple_of(c * RB, RB), RB)

    class Gather:
        def __init__(self, buf, order, s1s, s1r, s2s, s2r):
            self.buf, self.order = buf, order
            self.sems = (s1s, s1r, s2s, s2r)

        def block(self, d1, d2):
            if self.order == "xz":
                return self.buf.at[turn(x, -d1), turn(z, -d2)]
            return self.buf.at[turn(x, -d2), turn(z, -d1)]

        def peer(self, ring, d):
            return xdev(d) if (self.order == "xz") == (ring == 1) else zdev(d)

        def first(self):
            own = self.block(0, 0)
            for d in FAR:
                send(own, own, self.sems[0].at[d - 1], self.sems[1].at[d - 1], self.peer(1, d))

        def second(self, d1):
            b = self.block(d1, 0)
            for d in FAR:
                send(b, b, self.sems[2].at[d1, d - 1], self.sems[3].at[d1, d - 1], self.peer(2, d))

        def wait1(self, d1):
            arrived(self.block(d1, 0), self.sems[1].at[d1 - 1])

        def wait2(self, d1, d2):
            arrived(self.block(d1, d2), self.sems[3].at[d1, d2 - 1])

        def drain(self):
            own = self.block(0, 0)
            for d in FAR:
                sent(own, self.sems[0].at[d - 1])
                for d1 in range(4):
                    sent(own, self.sems[2].at[d1, d - 1])

    def gather_start(A, B):
        A.first()
        B.first()
        A.second(0)
        B.second(0)

    def gather_forward(A, B):
        for d in FAR:
            A.wait1(d)
            A.second(d)
            B.wait1(d)
            B.second(d)

    def gather_group(A, B, dz):
        if dz == 0:
            for d in FAR:
                B.wait2(0, d)
        else:
            for d1 in range(4):
                A.wait2(d1, dz)
            for d in FAR:
                B.wait2(dz, d)

    g1a = Gather(G1.at[0], "xz", a1s.at[0], a1r.at[0], a2s.at[0], a2r.at[0])
    g1b = Gather(G1.at[1], "zx", b1s.at[0], b1r.at[0], b2s.at[0], b2r.at[0])
    g2a = Gather(G2.at[0], "xz", a1s.at[1], a1r.at[1], a2s.at[1], a2r.at[1])
    g2b = Gather(G2.at[1], "zx", b1s.at[1], b1r.at[1], b2s.at[1], b2r.at[1])
    g2c = Gather(GC, "xz", c1s, c1r, c2s, c2r)

    @pl.when(is_gen)
    def _():
        for p in range(2):
            G1[p, x, z] = nin_ref[own_rows, own_cols(p)]
        gather_start(g1a, g1b)

    loads[0].wait()

    def transpose(i, carry):
        cols = pl.ds(pl.multiple_of(i * CW, CW), CW)
        UT[0, cols, :] = U[:, cols].T
        return carry

    lax.fori_loop(0, D // CW, transpose, 0)
    send(UT.at[0], UT.at[1], wss.at[0], wrs.at[0], sib)
    send(down_ref.at[0], W.at[1], wss.at[1], wrs.at[1], sib)
    loads[2].wait()

    @pl.when(is_gen)
    def _():
        for l in range(8):
            E[l // 4, l % 4] = vec_ref[0:1, :]

    @pl.when(jnp.logical_not(is_gen))
    def _():
        E[xl, z] = vec_ref[1:2, :]
        own = E.at[xl, z]
        for d in FAR:
            send(own, own, es.at[d - 1], er.at[d - 1], zdev(d))
        for d in FAR:
            arrived(E.at[xl, turn(z, -d)], er.at[d - 1])
        send(E.at[xl], E.at[xl], es.at[3], er.at[3], xdev(1))
        arrived(E.at[1 - xl], er.at[3])

    H[...] = jnp.zeros_like(H)
    act[...] = jnp.zeros_like(act)
    DA[...] = jnp.zeros_like(DA)

    def make_x0(p):
        total = yS[0, p].astype(f32) + yS[1, p].astype(f32)
        gate = par_ref[0, 4:5, own_cols(p)] + vec_ref[0:1, own_cols(p)]
        X0[p] = (nin_ref[own_rows, own_cols(p)].astype(f32) + gate * total).astype(bf16)

    def y_send(buf, slot, p, k):
        own = buf.at[slot, p]
        for d in FAR:
            send(own, own, ys.at[k, p, d - 1], yr.at[k, p, slot], device(x, turn(y, d), z, c))

    def y_wait(buf, slot, p, k):
        arrived(buf.at[slot, p], yr.at[k, p, slot])

    def y_drain(buf, k):
        for p in range(2):
            for d in FAR:
                sent(buf.at[0, 0], ys.at[k, p, d - 1])

    @pl.when(jnp.logical_not(is_gen))
    def _():
        for p, g in ((0, g1a), (1, g1b)):
            y_wait(yS, 0, p, 0)
            y_wait(yS, 1, p, 0)
            make_x0(p)
            cols = own_cols(p)
            noisy = vec_ref[2:3, cols] * X0[p].astype(f32) + vec_ref[3:4, cols] * noi_ref[own_rows, cols].astype(f32)
            G1[p, x, z] = noisy.astype(bf16)
            g.first()
        g1a.second(0)
        g1b.second(0)

    gather_forward(g1a, g1b)

    def norm_rows(zz, xl_):
        rows = pl.ds(pl.multiple_of(zz * 32 + xl_ * RB, RB), RB)

        def piece(k):
            return G1[k % 2, 2 * (k // 2) + xl_, zz].astype(f32)

        mean = sum(jnp.sum(piece(k), axis=1, keepdims=True) for k in range(4)) / D
        var = sum(jnp.sum(jnp.square(piece(k) - mean), axis=1, keepdims=True) for k in range(4)) / D
        rstd = lax.rsqrt(var + epsilon_norm)
        for k in range(4):
            cols = slice(k * PW, (k + 1) * PW)
            e = E[xl_, zz, :, cols]
            scale = 1.0 + par_ref[role, 3:4, cols] + e
            gain = (1.0 + par_ref[role, 0:1, cols]) * scale
            bias = par_ref[role, 1:2, cols] * scale + (par_ref[role, 2:3, cols] + e)
            xhat = (piece(k) - mean) * rstd
            uu[rows, cols] = (xhat * gain + bias).astype(bf16)
            XH[rows, cols] = xhat.astype(bf16)

    for dz in (0, 1, 3, 2):
        gather_group(g1a, g1b, dz)
        zz = turn(z, -dz)

        def both(i, carry, zz=zz):
            norm_rows(zz, i)
            return carry

        lax.fori_loop(0, 2, both, 0)

    arrived(UT.at[1], wrs.at[0])
    for s in range(2):
        H[s, :, 0:HU] = jnp.dot(uu[0:128, :], UT[s], preferred_element_type=f32)

    for s in range(2):
        act[s] = gelu_parts(H[s])[0].astype(bf16)
    loads[1].wait()
    arrived(W.at[1], wrs.at[1])

    def z_piece(xh_, p):
        cols = slice((xh_ * 2 + p) * PW, (xh_ * 2 + p + 1) * PW)
        acc = jnp.dot(act[0, :, 0:HU], W[0, :, cols], preferred_element_type=f32)
        acc += jnp.dot(act[1, :, 0:HU], W[1, :, cols], preferred_element_type=f32)
        acc = acc.astype(bf16)
        for z_ in range(4):
            for xl_ in range(2):
                rows = acc[z_ * 32 + xl_ * RB : z_ * 32 + (xl_ + 1) * RB]
                if p == 0:
                    zsA[2 * xh_ + xl_, z_] = rows
                else:
                    zsB[z_, 2 * xh_ + xl_] = rows

    for xh_ in range(2):
        z_piece(xh_, 0)
        for xl_ in range(2):
            to = 2 * xh_ + xl_

            @pl.when(to != x)
            def _():
                d = lax.rem(to + 4 - x, 4)
                send(zsA.at[to], rsA.at[d - 1], rsAs.at[d - 1], rsAr.at[d - 1], device(to, y, z, c))

        z_piece(xh_, 1)
        two = pl.ds(2 * xh_, 2)
        for d in FAR:
            send(
                zsB.at[turn(z, d), two], rsB.at[d - 1, two],
                rsBs.at[d - 1, xh_], rsBr.at[d - 1, xh_], zdev(d),
            )

    half = pl.ds(0, 128)
    other = pl.ds(128, 128)
    shared = [
        (H.at[1], HS, 0),
        (uu.at[half], uu.at[other], 1),
        (XH.at[half], XH.at[other], 2),
    ]
    for src, dst, k in shared:
        send(src, dst, xs.at[k], xr.at[k], sib)

    parts = ((0, zsA, rsA, x, z, zdev), (1, zsB, rsB, z, x, xdev))
    for p, zs, rs, first, second, peer in parts:
        for d in FAR:
            if p == 0:
                arrived(rsA.at[d - 1], rsAr.at[d - 1])
            else:
                for xh_ in range(2):
                    arrived(rsB.at[d - 1, pl.ds(2 * xh_, 2)], rsBr.at[d - 1, xh_])

        def add(i, carry, p=p, zs=zs, rs=rs, first=first):
            total = zs[first, i].astype(f32)
            for d in range(3):
                total += rs[d, i].astype(f32)
            sf[p, i] = total
            ss2[p, i] = total.astype(bf16)
            return carry

        lax.fori_loop(0, 4, add, 0)
        for d in FAR:
            send(ss2.at[p, turn(second, d)], r2.at[p, d - 1], rs2s.at[p, d - 1], rs2r.at[p, d - 1], peer(d))
    for p, zs, rs, first, second, peer in parts:
        for d in FAR:
            arrived(r2.at[p, d - 1], rs2r.at[p, d - 1])
        total = sf[p, second]
        for d in range(3):
            total += r2[p, d].astype(f32)
        Z[p] = total

        @pl.when(is_gen)
        def _(p=p, total=total):
            yS[y, p] = total.astype(bf16)
            y_send(yS, y, p, 0)

        @pl.when(jnp.logical_not(is_gen))
        def _(p=p, total=total):
            gate = par_ref[role, 4:5, own_cols(p)] + vec_ref[1:2, own_cols(p)]
            yF[y - 2, p] = (G1[p, x, z].astype(f32) + gate * total).astype(bf16)
            y_send(yF, y - 2, p, 1)

    @pl.when(is_gen)
    def _():
        for p in range(2):
            y_wait(yS, 1 - y, p, 0)
            make_x0(p)
            Z[p] = yS[0, p].astype(f32) + yS[1, p].astype(f32)

    dist = jnp.zeros((1, 1), f32)
    for p, g in ((0, g2a), (1, g2b)):
        @pl.when(is_gen)
        def _(p=p):
            y_wait(yF, 0, p, 1)
            y_wait(yF, 1, p, 1)

        @pl.when(jnp.logical_not(is_gen))
        def _(p=p):
            y_wait(yF, 3 - y, p, 1)

        fake, real, x0 = yF[0, p].astype(f32), yF[1, p].astype(f32), X0[p].astype(f32)
        gap = (fake - real).astype(bf16)
        Dv[p] = gap
        dist += jnp.sum(jnp.sum(jnp.abs(x0 - real), axis=1, keepdims=True), axis=0, keepdims=True)
        gate = par_ref[1, 4:5, own_cols(p)] + vec_ref[1:2, own_cols(p)]
        critic = ((fake - x0) * 0.125 * gate).astype(bf16)
        G2[p, x, z] = jnp.where(y == 2, critic, gap)
        g.first()
    g2a.second(0)
    g2b.second(0)
    CS[0] = jnp.broadcast_to(dist, (8, 128))
    cs = send(CS.at[0], CS.at[1], scs.at[0], scr.at[0], sib)

    @pl.when(y == 2)
    def _():
        for p in range(2):
            DX[xh, p] = Dv[p]
        send(DX.at[xh], DX.at[xh], dxs, dxr, xdev(2))

    cs.wait_recv()
    GC[x, z] = CS[0] + CS[1]
    g2c.first()
    g2c.second(0)
    gather_forward(g2a, g2b)
    for d in FAR:
        g2c.wait1(d)
        g2c.second(d)

    def inverse(xl_, zz):
        mean = (GC[xl_, zz] + GC[2 + xl_, zz]) / (32.0 * D)
        return 1.0 / (mean + epsilon_gap)

    def scaled_rows(zz, xl_):
        rows = pl.ds(pl.multiple_of(zz * 32 + xl_ * RB, RB), RB)
        inv = inverse(xl_, zz)[0:1, 0:1] * 0.125
        for k in range(4):
            cols = slice(k * PW, (k + 1) * PW)
            gate = par_ref[0, 4:5, cols] + vec_ref[0:1, cols]
            factor = jnp.where(y == 2, jnp.ones_like(gate), inv * gate)
            DZ[rows, cols] = (G2[k % 2, 2 * (k // 2) + xl_, zz].astype(f32) * factor).astype(bf16)

    for i, dz in enumerate((0, 1, 3, 2)):
        gather_group(g2a, g2b, dz)
        if dz > 0:
            for d1 in range(4):
                g2c.wait2(d1, dz)
        zz = turn(z, -dz)

        def both(j, carry, zz=zz):
            scaled_rows(zz, j)
            return carry

        lax.fori_loop(0, 2, both, 0)
        rows = pl.ds(pl.multiple_of(zz * 32, 32), 32)
        orows = pl.ds(pl.multiple_of(128 + zz * 32, 32), 32)
        send(DZ.at[rows], DZ.at[orows], dzs.at[i], dzr.at[i], sib)

        if dz == 0:
            inv_own = inverse(xl, z)[0:1, 0:1]

            @pl.when(y == 2)
            def _():
                arrived(DX.at[1 - xh], dxr)
                for k in range(4):
                    score_out[own_rows, k * PW : (k + 1) * PW] = DX[k // 2, k % 2].astype(f32) * inv_own

            @pl.when(y != 2)
            def _():
                for k in range(4):
                    score_out[own_rows, k * PW : (k + 1) * PW] = G2[k % 2, 2 * (k // 2) + xl, z].astype(f32) * inv_own

            send(score_out.at[own_rows], score_out.at[own_rows], scs.at[1], scr.at[1], sib)

    live = y < 3
    arrived(HS, xr.at[0])
    for i, dz in enumerate((0, 1, 3, 2)):
        orows = pl.ds(pl.multiple_of(128 + turn(z, -dz) * 32, 32), 32)
        arrived(DZ.at[orows], dzr.at[i])
    DA[:, 0:HU] = lax.dot_general(DZ[...], W[0], NT, preferred_element_type=f32)
    for s in range(2):
        rows = slice(s * 128, (s + 1) * 128)
        value, slope = gelu_parts(H[0] if s == 0 else HS[...])
        dh = jnp.where(live, DA[rows, :] * slope, 0.0)
        dhb[rows, :] = dh.astype(bf16)
        dht_out[:, rows] = dh.T.astype(bf16)
        at_out[:, rows] = jnp.where(live, value, 0.0).T.astype(bf16)

    for k in range(1, 3):
        arrived((uu, XH)[k - 1].at[other], xr.at[k])

    SM[...] = jnp.zeros_like(SM)

    def small(i, carry):
        cols = pl.ds(pl.multiple_of(i * CW, CW), CW)
        du = jnp.dot(dhb[:, 0:HU], U[:, cols], preferred_element_type=f32)
        dx = du * XH[:, cols].astype(f32)
        p3 = 1.0 + par_ref[role, 3:4, cols]
        rows = [jnp.zeros((1, CW), f32) for _ in range(4)]
        for l in range(8):
            first, second = slice(l * RB, (l + 1) * RB), slice(128 + l * RB, 128 + (l + 1) * RB)
            plain = jnp.sum(du[first] + du[second], axis=0, keepdims=True)
            norm = jnp.sum(dx[first] + dx[second], axis=0, keepdims=True)
            scale = p3 + E[l % 2, l // 2, :, cols]
            for k, term in enumerate((scale * norm, scale * plain, plain, norm)):
                rows[k] += term
        SM[0:1, cols] = rows[0]
        SM[1:2, cols] = rows[1]
        SM[2:3, cols] = rows[2]
        SM[3:4, cols] = (1.0 + par_ref[role, 0:1, cols]) * rows[3] + par_ref[role, 1:2, cols] * rows[2]
        return carry

    lax.fori_loop(0, D // CW, small, 0)

    inv_own = inverse(xl, z)[0:1, 0:1]
    for p in range(2):
        fake, x0 = yF[0, p].astype(f32), X0[p].astype(f32)
        cot = jnp.where(y == 2, fake - x0, Dv[p].astype(f32) * inv_own) * 0.125
        row = jnp.sum(cot * Z[p], axis=0, keepdims=True)
        SM[4:5, own_cols(p)] = jnp.where(jnp.logical_or(y == 0, y == 2), row, 0.0)

    for k in range(32):
        start = k * SW // 128 * 128
        window = SM[:, start : start + 256]
        off = k * SW - start
        if off:
            window = pltpu.roll(window, 256 - off, 1)
        f_, t_ = k // 4, k % 4
        T[t_ % 2, (t_ // 2) * 2 + f_ // 4, f_ % 4] = window

    near = [(dx, dc) for dc in range(2) for dx in (0, 1, 3, 2) if dx + dc]
    for k, (dx, dc) in enumerate(near):
        c_ = c if dc == 0 else 1 - c
        send(T.at[c_, turn(x, dx)], TX.at[k], t1s.at[k], t1r.at[k], device(turn(x, dx), y, z, c_))
    for k in range(7):
        arrived(TX.at[k], t1r.at[k])
    T3[...] = T[c, x] + ((TX[0] + TX[1] + TX[2]) + (TX[3] + TX[4] + TX[5] + TX[6]))
    for k, d in enumerate(FAR):
        send(T3.at[turn(z, d)], TZ.at[k], t2s.at[k], t2r.at[k], zdev(d))

    @pl.when(is_gen)
    def _():
        for k in range(4):
            d = (0,) + FAR
            send(T3.at[turn(z, d[k])], TZ.at[3 + k], t2s.at[3 + k], t2r.at[3 + k], device(x, twin, turn(z, d[k]), c))

    for k in range(3):
        arrived(TZ.at[k], t2r.at[k])
    small_out[...] = T3[z] + TZ[0] + TZ[1] + TZ[2]

    @pl.when(is_gen)
    def _():
        for k in range(4):
            arrived(TZ.at[3 + k], t2r.at[3 + k])
            sent(TZ.at[3 + k], t2s.at[3 + k])
        small_out[...] = small_out[...] + (TZ[3] + TZ[4] + TZ[5] + TZ[6])

    arrived(score_out.at[pl.ds(pl.multiple_of((1 - c) * RB, RB), RB)], scr.at[1])
    sent(score_out.at[own_rows], scs.at[1])
    sent(CS.at[0], scs.at[0])
    for k in range(7):
        sent(TX.at[k], t1s.at[k])
    for k in range(3):
        sent(TZ.at[k], t2s.at[k])
    for g in (g1a, g1b, g2a, g2b, g2c):
        g.drain()
    sent(UT.at[0], wss.at[0])
    sent(down_ref.at[0], wss.at[1])
    for src, dst, k in shared:
        sent(src, xs.at[k])
    for p, zs, rs, first, second, peer in parts:
        for d in FAR:
            if p == 0:
                sent(rs.at[0], rsAs.at[d - 1])
            else:
                for xh_ in range(2):
                    sent(rs.at[0, pl.ds(0, 2)], rsBs.at[d - 1, xh_])
            sent(r2.at[p, 0], rs2s.at[p, d - 1])
    for i in range(4):
        sent(DZ.at[pl.ds(0, 32)], dzs.at[i])

    @pl.when(is_gen)
    def _():
        y_drain(yS, 0)

    @pl.when(jnp.logical_not(is_gen))
    def _():
        y_drain(yF, 1)
        for d in FAR:
            sent(E.at[0, 0], es.at[d - 1])
        sent(E.at[0], es.at[3])

    @pl.when(y == 2)
    def _():
        sent(DX.at[0], dxs)

def weight_kernel(dht_ref, at_ref, u_ref, dz_ref, up_ref, down_ref, ubuf, dbuf, usem, dsem):
    count = D // CW

    def copies(i, slot):
        cols = pl.ds(pl.multiple_of(i * CW, CW), CW)
        return (
            pltpu.make_async_copy(ubuf.at[slot], up_ref.at[0, :, cols], usem.at[slot]),
            pltpu.make_async_copy(dbuf.at[slot], down_ref.at[0, :, cols], dsem.at[slot]),
        )

    def step(i, carry):
        slot = lax.rem(i, 2)
        cols = pl.ds(pl.multiple_of(i * CW, CW), CW)
        up_copy, down_copy = copies(i, slot)

        @pl.when(i >= 2)
        def _():
            up_copy.wait()

        ubuf[slot] = jnp.dot(dht_ref[...], u_ref[:, cols], preferred_element_type=f32)[0:HU]
        up_copy.start()

        @pl.when(i >= 2)
        def _():
            down_copy.wait()

        dbuf[slot] = jnp.dot(at_ref[...], dz_ref[:, cols], preferred_element_type=f32)[0:HU]
        down_copy.start()
        return carry

    lax.fori_loop(0, count, step, 0)
    for i in (count - 2, count - 1):
        for cp in copies(i, i % 2):
            cp.wait()

def per_device(noise_in, noise, timesteps, up_weight, down_weight, small_params):
    step_value = timesteps[0].astype(f32)
    angle = 0.5 * math.pi * step_value / 1000.0
    vec = jnp.stack(
        [
            embedding(jnp.float32(gen_time), D),
            embedding(step_value, D),
            jnp.full((D,), jnp.cos(angle)),
            jnp.full((D,), jnp.sin(angle)),
        ]
    )
    dma = pltpu.SemaphoreType.DMA
    vm = pltpu.VMEM
    vmem = pl.BlockSpec(memory_space=pltpu.VMEM)
    hbm = pl.BlockSpec(memory_space=pl.ANY)
    scratch = [
        vm((3, 5, D), f32),
        vm((HU, D), bf16),
        vm((2, D, HU), bf16),
        vm((2, HU, D), bf16),
        vm((2, 4, 1, D), f32),
        vm((2, 4, 4, RB, PW), bf16),
        vm((2, 4, 4, RB, PW), bf16),
        vm((4, 4, 8, 128), f32),
        vm((2, 2, RB, PW), bf16),
        vm((256, D), bf16),
        vm((2, 128, HP), f32),
        vm((128, HP), f32),
        vm((2, 128, HP), bf16),
        vm((256, HP), f32),
        vm((256, HP), bf16),
        vm((4, 4, RB, PW), bf16),
        vm((4, 4, RB, PW), bf16),
        vm((3, 4, RB, PW), bf16),
        vm((3, 4, RB, PW), bf16),
        vm((2, 4, RB, PW), f32),
        vm((2, 4, RB, PW), bf16),
        vm((2, 3, RB, PW), bf16),
        vm((2, RB, PW), f32),
        vm((2, 2, RB, PW), bf16),
        vm((2, 2, RB, PW), bf16),
        vm((2, RB, PW), bf16),
        vm((2, RB, PW), bf16),
        vm((2, 8, 128), f32),
        vm((8, D), f32),
        vm((2, 4, 4, 8, 256), f32),
        vm((7, 4, 8, 256), f32),
        vm((4, 8, 256), f32),
        vm((7, 8, 256), f32),
        dma((3,)), dma((2,)), dma((2,)), dma((4,)), dma((4,)),
        dma((2, 3)), dma((2, 3)), dma((2, 4, 3)), dma((2, 4, 3)),
        dma((2, 3)), dma((2, 3)), dma((2, 4, 3)), dma((2, 4, 3)),
        dma((3,)), dma((3,)), dma((4, 3)), dma((4, 3)),
        dma((3,)), dma((3,)), dma((3, 2)), dma((3, 2)), dma((2, 3)), dma((2, 3)),
        dma((2, 2, 3)), dma((2, 2, 2)), dma((3,)), dma((3,)), dma(()), dma(()),
        dma((4,)), dma((4,)), dma((2,)), dma((2,)), dma((7,)), dma((7,)), dma((7,)), dma((7,)),
    ]
    u_all, dz_all, dht, at, score, small = pl.pallas_call(
        chain_kernel,
        out_shape=[
            vm((256, D), bf16),
            vm((256, D), bf16),
            vm((HP, 256), bf16),
            vm((HP, 256), bf16),
            jax.ShapeDtypeStruct((32, D), f32),
            jax.ShapeDtypeStruct((8, 256), f32),
        ],
        in_specs=[hbm, hbm, vmem, vmem, vmem, hbm],
        out_specs=[vmem] * 6,
        scratch_shapes=scratch,
        compiler_params=pltpu.CompilerParams(
            collective_id=0, has_side_effects=True, vmem_limit_bytes=52 * 2**20
        ),
        name="chain",
    )(up_weight, down_weight, noise_in, noise, vec, small_params)
    up_grad, down_grad = pl.pallas_call(
        weight_kernel,
        out_shape=[jax.ShapeDtypeStruct((1, HU, D), f32)] * 2,
        in_specs=[vmem] * 4,
        out_specs=[hbm, hbm],
        scratch_shapes=[vm((2, HU, CW), f32), vm((2, HU, CW), f32), dma((2,)), dma((2,))],
        compiler_params=pltpu.CompilerParams(vmem_limit_bytes=24 * 2**20),
        name="weight_grads",
    )(dht, at, u_all, dz_all)
    return (score, up_grad, down_grad, small[None, 0:5, 0:SW])

def solution(mesh):
    in_specs = (
        P("fsdp", None),
        P("fsdp", None),
        P("fsdp"),
        P("group", ("fsdp", "tp"), None),
        P("group", ("fsdp", "tp"), None),
        P(),
    )
    out_specs = (
        P("fsdp", None),
        P("group", ("fsdp", "tp"), None),
        P("group", ("fsdp", "tp"), None),
        P("group", None, ("fsdp", "tp")),
    )
    return jax.shard_map(
        per_device, mesh=mesh, in_specs=in_specs, out_specs=out_specs, check_vma=False
    )
```

```python
import functools
import math

import jax
import jax.numpy as jnp
from jax import lax
from jax.experimental import pallas as pl
from jax.experimental.pallas import tpu as pltpu
from jax.sharding import PartitionSpec as P

MESH = pl.DeviceIdType.MESH
bf16, f32 = jnp.bfloat16, jnp.float32
gen_time = 999.0
epsilon_norm = 1e-06
epsilon_gap = 1e-05

D = 5120
HU = 216
HP = 256
RB = 16
PW = 1280
SW = 160
CW = 512
NT = (((1,), (1,)), ((), ()))
FAR = (1, 3, 2)

def embedding(step_value, feature_width):
    half_width = feature_width // 2
    freqs = jnp.exp(-math.log(10000.0) * jnp.arange(half_width, dtype=f32) / half_width)
    angles = step_value * freqs
    return jnp.concatenate([jnp.cos(angles), jnp.sin(angles)], axis=-1)

def device(x, y, z, c):
    return (y, lax.rem(x, 2) * 4 + z, lax.div(x, 2) * 2 + c)

def turn(value, steps):
    return lax.rem(value + (steps % 4), 4)

def gelu_parts(h):
    k = math.sqrt(2.0 / math.pi)
    t = jnp.tanh(k * (h + 0.044715 * (h * h * h)))
    value = 0.5 * h * (1.0 + t)
    slope = 0.5 * (1.0 + t) + 0.5 * h * (1.0 - t * t) * (k * (1.0 + 3.0 * 0.044715 * (h * h)))
    return value, slope

def chain_kernel(
    up_ref, down_ref, nin_ref, noi_ref, vec_ref, par_hbm,
    GU, GD, score_out, small_out,
    uu, DZ, par_ref, PR, dht, at, IV, U, UT, W, E, G1, G2A, G2B, DX, XH, H, HS, act, DA, dhb,
    zsA, zsB, rsA, rsB, sf, ss2, r2, Z, yS, yF, X0, Dv, CS, SM, T, T16, TX, T3, TZ,
    loc, wss, wrs, es, er,
    a1s, a1r, a2s, a2r, b1s, b1r, b2s, b2r,
    rsAs, rsAr, rsBs, rsBr, rs2s, rs2r, ys, yr, xs, xr, dxs, dxr, dzs, dzr, scs, scr, t1s, t1r, t2s, t2r,
):
    y = lax.axis_index("group")
    fi = lax.axis_index("fsdp")
    ti = lax.axis_index("tp")
    xl, z = lax.div(fi, 4), lax.rem(fi, 4)
    xh, c = lax.div(ti, 2), lax.rem(ti, 2)
    x = xh * 2 + xl
    role = jnp.maximum(y - 1, 0)
    is_gen = y < 2
    pending = []

    def xdev(d):
        return device(turn(x, d), y, z, c)

    def zdev(d):
        return device(x, y, turn(z, d), c)

    sib = device(x, y, z, 1 - c)

    def send(src, dst, s, r, dev):
        cp = pltpu.make_async_remote_copy(
            src_ref=src, dst_ref=dst, send_sem=s, recv_sem=r, device_id=dev, device_id_type=MESH
        )
        cp.start()
        return cp

    def sent(src, s):
        pltpu.make_async_copy(src, src, s).wait()

    def arrived(dst, r):
        pltpu.make_async_copy(dst, dst, r).wait()

    loads = [
        pltpu.make_async_copy(up_ref.at[0], U, loc.at[0]),
        pltpu.make_async_copy(down_ref.at[0], W.at[0], loc.at[1]),
        pltpu.make_async_copy(par_hbm, par_ref, loc.at[2]),
    ]
    for cp in loads:
        cp.start()

    barrier = pltpu.get_barrier_semaphore()
    peers = [xdev(d) for d in FAR] + [zdev(d) for d in FAR]
    peers += [device(x, turn(y, d), z, c) for d in FAR] + [sib]
    twin = y + 1 - 2 * lax.rem(y, 2)
    peers += [device(turn(x, d), y, z, 1 - c) for d in FAR]
    peers += [device(x, twin, turn(z, d), c) for d in FAR]
    for dev in peers:
        pl.semaphore_signal(barrier, inc=1, device_id=dev, device_id_type=MESH)
    pl.semaphore_wait(barrier, len(peers))

    def own_cols(p):
        return pl.ds(pl.multiple_of(xh * (2 * PW) + p * PW, 128), PW)

    own_rows = pl.ds(pl.multiple_of(c * RB, RB), RB)

    class Gather:
        def __init__(self, buf, order, s1s, s1r, s2s, s2r):
            self.buf, self.order = buf, order
            self.sems = (s1s, s1r, s2s, s2r)

        def block(self, d1, d2):
            if self.order == "xz":
                return self.buf.at[turn(x, -d1), turn(z, -d2)]
            return self.buf.at[turn(x, -d2), turn(z, -d1)]

        def peer(self, ring, d):
            return xdev(d) if (self.order == "xz") == (ring == 1) else zdev(d)

        def first(self):
            own = self.block(0, 0)
            for d in FAR:
                send(own, own, self.sems[0].at[d - 1], self.sems[1].at[d - 1], self.peer(1, d))

        def second(self, d1):
            b = self.block(d1, 0)
            for d in FAR:
                send(b, b, self.sems[2].at[d1, d - 1], self.sems[3].at[d1, d - 1], self.peer(2, d))

        def wait1(self, d1):
            arrived(self.block(d1, 0), self.sems[1].at[d1 - 1])

        def wait2(self, d1, d2):
            arrived(self.block(d1, d2), self.sems[3].at[d1, d2 - 1])

        def drain(self):
            own = self.block(0, 0)
            for d in FAR:
                sent(own, self.sems[0].at[d - 1])
                for d1 in range(4):
                    sent(own, self.sems[2].at[d1, d - 1])

    def gather_start(A, B):
        A.first()
        B.first()
        A.second(0)
        B.second(0)

    def gather_forward(A, B):
        for d in FAR:
            A.wait1(d)
            A.second(d)
            B.wait1(d)
            B.second(d)

    def gather_group(A, B, dz):
        if dz == 0:
            for d in FAR:
                B.wait2(0, d)
        else:
            for d1 in range(4):
                A.wait2(d1, dz)
            for d in FAR:
                B.wait2(dz, d)

    g1a = Gather(G1.at[0], "xz", a1s.at[0], a1r.at[0], a2s.at[0], a2r.at[0])
    g1b = Gather(G1.at[1], "zx", b1s.at[0], b1r.at[0], b2s.at[0], b2r.at[0])
    g2a = Gather(G2A, "xz", a1s.at[1], a1r.at[1], a2s.at[1], a2r.at[1])
    g2b = Gather(G2B, "zx", b1s.at[1], b1r.at[1], b2s.at[1], b2r.at[1])

    @pl.when(is_gen)
    def _():
        for p in range(2):
            G1[p, x, z] = nin_ref[own_rows, own_cols(p)]
        gather_start(g1a, g1b)

    loads[0].wait()

    def transpose(i, carry):
        cols = pl.ds(pl.multiple_of(i * CW, CW), CW)
        UT[0, cols, :] = U[:, cols].T
        return carry

    lax.fori_loop(0, D // CW, transpose, 0)
    send(UT.at[0], UT.at[1], wss.at[0], wrs.at[0], sib)
    send(down_ref.at[0], W.at[1], wss.at[1], wrs.at[1], sib)
    loads[2].wait()
    for j in range(5):
        PR[j : j + 1, :] = par_ref[j, pl.ds(role, 1), :]
    PR[5:6, :] = par_ref[4, 0:1, :]
    PR[6:7, :] = par_ref[4, 1:2, :]

    @pl.when(is_gen)
    def _():
        for l in range(8):
            E[l // 4, l % 4] = vec_ref[0:1, :]

    @pl.when(jnp.logical_not(is_gen))
    def _():
        E[xl, z] = vec_ref[1:2, :]
        own = E.at[xl, z]
        for d in FAR:
            send(own, own, es.at[d - 1], er.at[d - 1], zdev(d))
        for d in FAR:
            arrived(E.at[xl, turn(z, -d)], er.at[d - 1])
        send(E.at[xl], E.at[xl], es.at[3], er.at[3], xdev(1))
        arrived(E.at[1 - xl], er.at[3])

    H[...] = jnp.zeros_like(H)
    act[...] = jnp.zeros_like(act)
    DA[...] = jnp.zeros_like(DA)

    def make_x0(p):
        total = yS[0, p].astype(f32) + yS[1, p].astype(f32)
        gate = PR[5:6, own_cols(p)] + vec_ref[0:1, own_cols(p)]
        X0[p] = (nin_ref[own_rows, own_cols(p)].astype(f32) + gate * total).astype(bf16)

    def y_send(buf, slot, p, k):
        own = buf.at[slot, p]
        for d in FAR:
            send(own, own, ys.at[k, p, d - 1], yr.at[k, p, slot], device(x, turn(y, d), z, c))

    def y_wait(buf, slot, p, k):
        arrived(buf.at[slot, p], yr.at[k, p, slot])

    def y_drain(buf, k):
        for p in range(2):
            for d in FAR:
                sent(buf.at[0, 0], ys.at[k, p, d - 1])

    @pl.when(jnp.logical_not(is_gen))
    def _():
        for p, g in ((0, g1a), (1, g1b)):
            y_wait(yS, 0, p, 0)
            y_wait(yS, 1, p, 0)
            make_x0(p)
            cols = own_cols(p)
            noisy = vec_ref[2:3, cols] * X0[p].astype(f32) + vec_ref[3:4, cols] * noi_ref[own_rows, cols].astype(f32)
            G1[p, x, z] = noisy.astype(bf16)
            g.first()
        g1a.second(0)
        g1b.second(0)

    gather_forward(g1a, g1b)

    def norm_rows(zz, xl_):
        rows = pl.ds(pl.multiple_of(zz * 32 + xl_ * RB, RB), RB)

        def piece(k):
            return G1[k % 2, 2 * (k // 2) + xl_, zz].astype(f32)

        mean = sum(jnp.sum(piece(k), axis=1, keepdims=True) for k in range(4)) / D
        var = sum(jnp.sum(jnp.square(piece(k) - mean), axis=1, keepdims=True) for k in range(4)) / D
        rstd = lax.rsqrt(var + epsilon_norm)
        for k in range(4):
            cols = slice(k * PW, (k + 1) * PW)
            e = E[xl_, zz, :, cols]
            scale = 1.0 + PR[3:4, cols] + e
            gain = (1.0 + PR[0:1, cols]) * scale
            bias = PR[1:2, cols] * scale + (PR[2:3, cols] + e)
            xhat = (piece(k) - mean) * rstd
            uu[rows, cols] = (xhat * gain + bias).astype(bf16)
            XH[rows, cols] = xhat.astype(bf16)

    for dz in (0, 1, 3, 2):
        gather_group(g1a, g1b, dz)
        zz = turn(z, -dz)

        def both(i, carry, zz=zz):
            norm_rows(zz, i)
            return carry

        lax.fori_loop(0, 2, both, 0)

    arrived(UT.at[1], wrs.at[0])
    for s in range(2):
        H[s, :, 0:HU] = jnp.dot(uu[0:128, :], UT[s], preferred_element_type=f32)

    for s in range(2):
        act[s] = gelu_parts(H[s])[0].astype(bf16)
    loads[1].wait()
    arrived(W.at[1], wrs.at[1])

    def z_piece(xh_, p):
        cols = slice((xh_ * 2 + p) * PW, (xh_ * 2 + p + 1) * PW)
        acc = jnp.dot(act[0, :, 0:HU], W[0, :, cols], preferred_element_type=f32)
        acc += jnp.dot(act[1, :, 0:HU], W[1, :, cols], preferred_element_type=f32)
        acc = acc.astype(bf16)
        for z_ in range(4):
            for xl_ in range(2):
                rows = acc[z_ * 32 + xl_ * RB : z_ * 32 + (xl_ + 1) * RB]
                if p == 0:
                    zsA[2 * xh_ + xl_, z_] = rows
                else:
                    zsB[z_, 2 * xh_ + xl_] = rows

    for xh_ in range(2):
        z_piece(xh_, 0)
        for xl_ in range(2):
            to = 2 * xh_ + xl_

            @pl.when(to != x)
            def _():
                d = lax.rem(to + 4 - x, 4)
                send(zsA.at[to], rsA.at[d - 1], rsAs.at[d - 1], rsAr.at[d - 1], device(to, y, z, c))

        z_piece(xh_, 1)
        two = pl.ds(2 * xh_, 2)
        for d in FAR:
            send(
                zsB.at[turn(z, d), two], rsB.at[d - 1, two],
                rsBs.at[d - 1, xh_], rsBr.at[d - 1, xh_], zdev(d),
            )

    half = pl.ds(0, 128)
    other = pl.ds(128, 128)
    shared = [
        (H.at[1], HS, 0),
        (uu.at[half], uu.at[other], 1),
        (XH.at[half], XH.at[other], 2),
    ]
    for src, dst, k in shared:
        send(src, dst, xs.at[k], xr.at[k], sib)

    parts = ((0, zsA, rsA, x, z, zdev), (1, zsB, rsB, z, x, xdev))
    for p, zs, rs, first, second, peer in parts:
        for d in FAR:
            if p == 0:
                arrived(rsA.at[d - 1], rsAr.at[d - 1])
            else:
                for xh_ in range(2):
                    arrived(rsB.at[d - 1, pl.ds(2 * xh_, 2)], rsBr.at[d - 1, xh_])

        def add(i, carry, p=p, zs=zs, rs=rs, first=first):
            total = zs[first, i].astype(f32)
            for d in range(3):
                total += rs[d, i].astype(f32)
            sf[p, i] = total
            ss2[p, i] = total.astype(bf16)
            return carry

        lax.fori_loop(0, 4, add, 0)
        for d in FAR:
            send(ss2.at[p, turn(second, d)], r2.at[p, d - 1], rs2s.at[p, d - 1], rs2r.at[p, d - 1], peer(d))
    for p, zs, rs, first, second, peer in parts:
        for d in FAR:
            arrived(r2.at[p, d - 1], rs2r.at[p, d - 1])
        total = sf[p, second]
        for d in range(3):
            total += r2[p, d].astype(f32)
        Z[p] = total

        @pl.when(is_gen)
        def _(p=p, total=total):
            yS[y, p] = total.astype(bf16)
            y_send(yS, y, p, 0)

        @pl.when(jnp.logical_not(is_gen))
        def _(p=p, total=total):
            gate = PR[4:5, own_cols(p)] + vec_ref[1:2, own_cols(p)]
            yF[y - 2, p] = (G1[p, x, z].astype(f32) + gate * total).astype(bf16)
            y_send(yF, y - 2, p, 1)

    @pl.when(is_gen)
    def _():
        for p in range(2):
            y_wait(yS, 1 - y, p, 0)
            make_x0(p)
            Z[p] = yS[0, p].astype(f32) + yS[1, p].astype(f32)

    dist = jnp.zeros((1, 1), f32)
    for p, g in ((0, g2a), (1, g2b)):
        @pl.when(is_gen)
        def _(p=p):
            y_wait(yF, 0, p, 1)
            y_wait(yF, 1, p, 1)

        @pl.when(jnp.logical_not(is_gen))
        def _(p=p):
            y_wait(yF, 3 - y, p, 1)

        fake, real, x0 = yF[0, p].astype(f32), yF[1, p].astype(f32), X0[p].astype(f32)
        gap = (fake - real).astype(bf16)
        Dv[p] = gap
        dist += jnp.sum(jnp.sum(jnp.abs(x0 - real), axis=0, keepdims=True), axis=1, keepdims=True)
        gate = PR[6:7, own_cols(p)] + vec_ref[1:2, own_cols(p)]
        critic = ((fake - x0) * 0.125 * gate).astype(bf16)
        block = jnp.where(y == 2, critic, gap)
        if p == 0:
            G2A[x, z, :, 0:PW] = block
        else:
            G2B[x, z] = block
    hi = dist.astype(bf16)
    mid = (dist - hi.astype(f32)).astype(bf16)
    low = (dist - hi.astype(f32) - mid.astype(f32)).astype(bf16)
    lane = lax.broadcasted_iota(jnp.int32, (RB, 128), 1)
    tile = jnp.where(lane == 0, hi.astype(f32), jnp.where(lane == 1, mid.astype(f32), low.astype(f32)))
    G2A[x, z, :, PW:] = tile.astype(bf16)
    g2a.first()
    g2b.first()
    g2a.second(0)
    g2b.second(0)

    @pl.when(y == 2)
    def _():
        for p in range(2):
            DX[xh, p] = Dv[p]
        send(DX.at[xh], DX.at[xh], dxs, dxr, xdev(2))

    gather_forward(g2a, g2b)

    def gap_piece(k, xl_, zz):
        col = 2 * (k // 2) + xl_
        return G2A[col, zz, :, 0:PW] if k % 2 == 0 else G2B[col, zz]

    def share(xl_, zz):
        def one(col):
            tile = G2A[col, zz, :, PW:].astype(f32)
            return (tile[0:1, 0:1] + tile[0:1, 1:2]) + tile[0:1, 2:3]

        return one(xl_) + one(2 + xl_)

    def inverse(l):
        return 1.0 / ((CS[0, l : l + 1, :] + CS[1, l : l + 1, :]) / (32.0 * D) + epsilon_gap)

    def scaled_rows(zz, xl_):
        rows = pl.ds(pl.multiple_of(zz * 32 + xl_ * RB, RB), RB)
        for k in range(4):
            cols = slice(k * PW, (k + 1) * PW)
            gate = PR[5:6, cols] + vec_ref[0:1, cols]
            factor = jnp.where(y == 2, jnp.ones_like(gate), gate * 0.125)
            DZ[rows, cols] = (gap_piece(k, xl_, zz).astype(f32) * factor).astype(bf16)

    for i, dz in enumerate((0, 1, 3, 2)):
        gather_group(g2a, g2b, dz)
        zz = turn(z, -dz)

        def both(j, carry, zz=zz):
            scaled_rows(zz, j)
            return carry

        lax.fori_loop(0, 2, both, 0)
        rows = pl.ds(pl.multiple_of(zz * 32, 32), 32)
        orows = pl.ds(pl.multiple_of(128 + zz * 32, 32), 32)
        send(DZ.at[rows], DZ.at[orows], dzs.at[i], dzr.at[i], sib)

    for l in range(8):
        CS[0, l : l + 1, :] = jnp.broadcast_to(share(l % 2, l // 2), (1, 128))
    send(CS.at[0], CS.at[1], scs.at[0], scr.at[0], sib)
    live = y < 3
    arrived(HS, xr.at[0])
    for i, dz in enumerate((0, 1, 3, 2)):
        orows = pl.ds(pl.multiple_of(128 + turn(z, -dz) * 32, 32), 32)
        arrived(DZ.at[orows], dzr.at[i])
    DA[:, 0:HU] = lax.dot_general(DZ[...], W[0], NT, preferred_element_type=f32)
    arrived(CS.at[1], scr.at[0])
    for l in range(8):
        inv = jnp.where(y == 2, 1.0, inverse(l)[:, 0:1])
        IV[l * RB : (l + 1) * RB, :] = jnp.broadcast_to(inv, (RB, 256))
    for s in range(2):
        rows = slice(s * 128, (s + 1) * 128)
        value, slope = gelu_parts(H[0] if s == 0 else HS[...])
        dh = jnp.where(live, DA[rows, :] * slope * IV[...], 0.0)
        DA[rows, :] = dh
        dhb[rows, :] = dh.astype(bf16)

    arrived(XH.at[other], xr.at[2])

    SM[...] = jnp.zeros_like(SM)

    def small(i, carry):
        cols = pl.ds(pl.multiple_of(i * CW, CW), CW)
        du = jnp.dot(dhb[:, 0:HU], U[:, cols], preferred_element_type=f32)
        dx = du * XH[:, cols].astype(f32)
        p3 = 1.0 + PR[3:4, cols]
        rows = [jnp.zeros((8, CW), f32) for _ in range(4)]
        for l in range(8):
            starts = [l * RB + k for k in (0, 8, 128, 136)]
            plain = sum(du[k : k + 8] for k in starts)
            norm = sum(dx[k : k + 8] for k in starts)
            scale = p3 + E[l % 2, l // 2, :, cols]
            for k, term in enumerate((scale * norm, scale * plain, plain, norm)):
                rows[k] += term
        rows = [jnp.sum(row, axis=0, keepdims=True) for row in rows]
        SM[0:1, cols] = rows[0]
        SM[1:2, cols] = rows[1]
        SM[2:3, cols] = rows[2]
        SM[3:4, cols] = (1.0 + PR[0:1, cols]) * rows[3] + PR[1:2, cols] * rows[2]
        return carry

    lax.fori_loop(0, D // CW, small, 0)

    own_row = pl.ds(z * 2 + xl, 1)
    inv_own = (1.0 / ((CS[0, own_row, :] + CS[1, own_row, :]) / (32.0 * D) + epsilon_gap))[:, 0:1]

    @pl.when(y == 2)
    def _():
        arrived(DX.at[1 - xh], dxr)
        for k in range(4):
            score_out[own_rows, k * PW : (k + 1) * PW] = DX[k // 2, k % 2].astype(f32) * inv_own

    @pl.when(y != 2)
    def _():
        for k in range(4):
            score_out[own_rows, k * PW : (k + 1) * PW] = gap_piece(k, xl, z).astype(f32) * inv_own

    send(score_out.at[own_rows], score_out.at[own_rows], scs.at[1], scr.at[1], sib)

    own_row = pl.ds(z * 2 + xl, 1)
    inv_own = (1.0 / ((CS[0, own_row, :] + CS[1, own_row, :]) / (32.0 * D) + epsilon_gap))[:, 0:1]
    for p in range(2):
        fake, x0 = yF[0, p].astype(f32), X0[p].astype(f32)
        cot = jnp.where(y == 2, fake - x0, Dv[p].astype(f32) * inv_own) * 0.125
        row = jnp.sum(cot * Z[p], axis=0, keepdims=True)
        SM[4:5, own_cols(p)] = jnp.where(jnp.logical_or(y == 0, y == 2), row, 0.0)

    for k in range(32):
        start = k * SW // 128 * 128
        window = SM[:, start : start + 256]
        off = k * SW - start
        if off:
            window = pltpu.roll(window, 256 - off, 1)
        f_, t_ = k // 4, k % 4
        row = f_ % 4 * 8
        T[t_ % 2, (t_ // 2) * 2 + f_ // 4, row : row + 8] = window

    T16[...] = T[...].astype(bf16)
    near = [(dx, dc) for dc in range(2) for dx in (0, 1, 3, 2) if dx + dc]
    for k, (dx, dc) in enumerate(near):
        c_ = c if dc == 0 else 1 - c
        send(T16.at[c_, turn(x, dx)], TX.at[k], t1s.at[k], t1r.at[k], device(turn(x, dx), y, z, c_))

    live_rows = jnp.where(live, IV[...], 0.0)
    for s in range(2):
        rows = slice(s * 128, (s + 1) * 128)
        value = gelu_parts(H[0] if s == 0 else HS[...])[0]
        dht[:, rows] = DA[rows, :].T.astype(bf16)
        at[:, rows] = (value * live_rows).T.astype(bf16)
    arrived(uu.at[other], xr.at[1])

    def product(left, right, out):
        def step(i, carry):
            cols = pl.ds(pl.multiple_of(i * CW, CW), CW)
            out[:, cols] = jnp.dot(left[...], right[:, cols], preferred_element_type=f32)[0:HU]
            return carry

        lax.fori_loop(0, D // CW, step, 0)

    product(dht, uu, GU)
    for k in range(7):
        arrived(TX.at[k], t1r.at[k])
    total = T[c, x]
    for k in range(7):
        total += TX[k].astype(f32)
    for z_ in range(4):
        T3[z_] = total[z_ * 8 : z_ * 8 + 8]
    for k, d in enumerate(FAR):
        send(T3.at[turn(z, d)], TZ.at[k], t2s.at[k], t2r.at[k], zdev(d))

    @pl.when(is_gen)
    def _():
        for k in range(4):
            d = (0,) + FAR
            send(T3.at[turn(z, d[k])], TZ.at[3 + k], t2s.at[3 + k], t2r.at[3 + k], device(x, twin, turn(z, d[k]), c))

    product(at, DZ, GD)

    for k in range(3):
        arrived(TZ.at[k], t2r.at[k])
    small_out[...] = T3[z] + TZ[0] + TZ[1] + TZ[2]

    @pl.when(is_gen)
    def _():
        for k in range(4):
            arrived(TZ.at[3 + k], t2r.at[3 + k])
            sent(TZ.at[3 + k], t2s.at[3 + k])
        small_out[...] = small_out[...] + (TZ[3] + TZ[4] + TZ[5] + TZ[6])

    arrived(score_out.at[pl.ds(pl.multiple_of((1 - c) * RB, RB), RB)], scr.at[1])
    sent(score_out.at[own_rows], scs.at[1])
    sent(CS.at[0], scs.at[0])
    for k in range(7):
        sent(TX.at[k], t1s.at[k])
    for k in range(3):
        sent(TZ.at[k], t2s.at[k])
    for g in (g1a, g1b, g2a, g2b):
        g.drain()
    sent(UT.at[0], wss.at[0])
    sent(down_ref.at[0], wss.at[1])
    for src, dst, k in shared:
        sent(src, xs.at[k])
    for p, zs, rs, first, second, peer in parts:
        for d in FAR:
            if p == 0:
                sent(rs.at[0], rsAs.at[d - 1])
            else:
                for xh_ in range(2):
                    sent(rs.at[0, pl.ds(0, 2)], rsBs.at[d - 1, xh_])
            sent(r2.at[p, 0], rs2s.at[p, d - 1])
    for i in range(4):
        sent(DZ.at[pl.ds(0, 32)], dzs.at[i])

    @pl.when(is_gen)
    def _():
        y_drain(yS, 0)

    @pl.when(jnp.logical_not(is_gen))
    def _():
        y_drain(yF, 1)
        for d in FAR:
            sent(E.at[0, 0], es.at[d - 1])
        sent(E.at[0], es.at[3])

    @pl.when(y == 2)
    def _():
        sent(DX.at[0], dxs)

def place_kernel(gu, gd, score, small, up_out, down_out, score_out, small_out, sems):
    cuts = ((0, 56), (56, 56), (112, 56), (168, 48))
    copies = [pltpu.make_async_copy(score, score_out, sems.at[0])]
    for k, (start, size) in enumerate(cuts):
        rows = pl.ds(start, size)
        copies.append(pltpu.make_async_copy(gu.at[rows], up_out.at[0, rows], sems.at[1 + k]))
        copies.append(pltpu.make_async_copy(gd.at[rows], down_out.at[0, rows], sems.at[5 + k]))
    for cp in copies:
        cp.start()
    for k in range(5):
        small_out[k] = small[k : k + 1, 0:SW]
    for cp in copies:
        cp.wait()

def per_device(noise_in, noise, timesteps, up_weight, down_weight, small_params):
    step_value = timesteps[0].astype(f32)
    angle = 0.5 * math.pi * step_value / 1000.0
    vec = jnp.stack(
        [
            embedding(jnp.float32(gen_time), D),
            embedding(step_value, D),
            jnp.full((D,), jnp.cos(angle)),
            jnp.full((D,), jnp.sin(angle)),
        ]
    )
    dma = pltpu.SemaphoreType.DMA
    vm = pltpu.VMEM
    vmem = pl.BlockSpec(memory_space=pltpu.VMEM)
    hbm = pl.BlockSpec(memory_space=pl.ANY)
    scratch = [
        vm((256, D), bf16),
        vm((256, D), bf16),
        vm((5, 3, D), f32),
        vm((8, D), f32),
        vm((HP, 256), bf16),
        vm((HP, 256), bf16),
        vm((128, 256), f32),
        vm((HU, D), bf16),
        vm((2, D, HU), bf16),
        vm((2, HU, D), bf16),
        vm((2, 4, 1, D), f32),
        vm((2, 4, 4, RB, PW), bf16),
        vm((4, 4, RB, PW + 128), bf16),
        vm((4, 4, RB, PW), bf16),
        vm((2, 2, RB, PW), bf16),
        vm((256, D), bf16),
        vm((2, 128, HP), f32),
        vm((128, HP), f32),
        vm((2, 128, HP), bf16),
        vm((256, HP), f32),
        vm((256, HP), bf16),
        vm((4, 4, RB, PW), bf16),
        vm((4, 4, RB, PW), bf16),
        vm((3, 4, RB, PW), bf16),
        vm((3, 4, RB, PW), bf16),
        vm((2, 4, RB, PW), f32),
        vm((2, 4, RB, PW), bf16),
        vm((2, 3, RB, PW), bf16),
        vm((2, RB, PW), f32),
        vm((2, 2, RB, PW), bf16),
        vm((2, 2, RB, PW), bf16),
        vm((2, RB, PW), bf16),
        vm((2, RB, PW), bf16),
        vm((2, 8, 128), f32),
        vm((8, D), f32),
        vm((2, 4, 32, 256), f32),
        vm((2, 4, 32, 256), bf16),
        vm((7, 32, 256), bf16),
        vm((4, 8, 256), f32),
        vm((7, 8, 256), f32),
        dma((3,)), dma((2,)), dma((2,)), dma((4,)), dma((4,)),
        dma((2, 3)), dma((2, 3)), dma((2, 4, 3)), dma((2, 4, 3)),
        dma((2, 3)), dma((2, 3)), dma((2, 4, 3)), dma((2, 4, 3)),
        dma((3,)), dma((3,)), dma((3, 2)), dma((3, 2)), dma((2, 3)), dma((2, 3)),
        dma((2, 2, 3)), dma((2, 2, 2)), dma((3,)), dma((3,)), dma(()), dma(()),
        dma((4,)), dma((4,)), dma((2,)), dma((2,)), dma((7,)), dma((7,)), dma((7,)), dma((7,)),
    ]
    parts = pl.pallas_call(
        chain_kernel,
        out_shape=[
            vm((HU, D), f32),
            vm((HU, D), f32),
            vm((32, D), f32),
            vm((8, 256), f32),
        ],
        in_specs=[hbm, hbm, vmem, vmem, vmem, hbm],
        out_specs=[vmem] * 4,
        scratch_shapes=scratch,
        compiler_params=pltpu.CompilerParams(
            collective_id=0, has_side_effects=True, vmem_limit_bytes=52 * 2**20
        ),
        name="chain",
    )(up_weight, down_weight, noise_in, noise, vec, jnp.transpose(small_params, (1, 0, 2)))
    up_grad, down_grad, score, small = pl.pallas_call(
        place_kernel,
        out_shape=[
            jax.ShapeDtypeStruct((1, HU, D), f32),
            jax.ShapeDtypeStruct((1, HU, D), f32),
            jax.ShapeDtypeStruct((32, D), f32),
            jax.ShapeDtypeStruct((5, 1, SW), f32),
        ],
        in_specs=[vmem] * 4,
        out_specs=[hbm, hbm, hbm, vmem],
        scratch_shapes=[dma((9,))],
        compiler_params=pltpu.CompilerParams(vmem_limit_bytes=24 * 2**20),
        name="place",
    )(*parts)
    return (score, up_grad, down_grad, jnp.transpose(small, (1, 0, 2)))

def solution(mesh):
    in_specs = (
        P("fsdp", None),
        P("fsdp", None),
        P("fsdp"),
        P("group", ("fsdp", "tp"), None),
        P("group", ("fsdp", "tp"), None),
        P(),
    )
    out_specs = (
        P("fsdp", None),
        P("group", ("fsdp", "tp"), None),
        P("group", ("fsdp", "tp"), None),
        P("group", None, ("fsdp", "tp")),
    )
    return jax.shard_map(
        per_device, mesh=mesh, in_specs=in_specs, out_specs=out_specs, check_vma=False
    )
```

```python
import functools
import math

import jax
import jax.numpy as jnp
from jax import lax
from jax.experimental import pallas as pl
from jax.experimental.pallas import tpu as pltpu
from jax.sharding import PartitionSpec as P

MESH = pl.DeviceIdType.MESH
bf16, f32 = jnp.bfloat16, jnp.float32
gen_time = 999.0
epsilon_norm = 1e-06
epsilon_gap = 1e-05

D = 5120
HU = 216
HP = 256
RB = 16
PW = 1280
SW = 160
CW = 1024
NT = (((1,), (1,)), ((), ()))
FAR = (2, 1, 3)

def embedding(step_value, feature_width):
    half_width = feature_width // 2
    freqs = jnp.exp(-math.log(10000.0) * jnp.arange(half_width, dtype=f32) / half_width)
    angles = step_value * freqs
    return jnp.concatenate([jnp.cos(angles), jnp.sin(angles)], axis=-1)

def device(x, y, z, c):
    return (y, lax.rem(x, 2) * 4 + z, lax.div(x, 2) * 2 + c)

def turn(value, steps):
    return lax.rem(value + (steps % 4), 4)

def gelu_parts(h):
    k = math.sqrt(2.0 / math.pi)
    t = jnp.tanh(k * (h + 0.044715 * (h * h * h)))
    value = 0.5 * h * (1.0 + t)
    slope = 0.5 * (1.0 + t) + 0.5 * h * (1.0 - t * t) * (k * (1.0 + 3.0 * 0.044715 * (h * h)))
    return value, slope

def chain_kernel(
    up_ref, down_ref, nin_hbm, noi_hbm, vec_ref, par_hbm,
    GU, at, DZ, score_out, small_out,
    nin_ref, noi_ref, uu, par_ref, PR, dht, IV, U, UT, W, E, G1, G2A, G2B, DX, XH, H, HS, act, DA, dhb,
    zsA, zsB, rsA, rsB, sf, ss2, r2, Z, yS, yF, X0, Dv, CS, SM, T, T16, TX, T3, TZ,
    loc, wss, wrs, es, er,
    a1s, a1r, a2s, a2r, b1s, b1r, b2s, b2r,
    rsAs, rsAr, rsBs, rsBr, rs2s, rs2r, ys, yr, xs, xr, dxs, dxr, dzs, dzr, scs, scr, t1s, t1r, t2s, t2r,
):
    y = lax.axis_index("group")
    fi = lax.axis_index("fsdp")
    ti = lax.axis_index("tp")
    xl, z = lax.div(fi, 4), lax.rem(fi, 4)
    xh, c = lax.div(ti, 2), lax.rem(ti, 2)
    x = xh * 2 + xl
    role = jnp.maximum(y - 1, 0)
    is_gen = y < 2
    pending = []

    def xdev(d):
        return device(turn(x, d), y, z, c)

    def zdev(d):
        return device(x, y, turn(z, d), c)

    sib = device(x, y, z, 1 - c)

    def send(src, dst, s, r, dev):
        cp = pltpu.make_async_remote_copy(
            src_ref=src, dst_ref=dst, send_sem=s, recv_sem=r, device_id=dev, device_id_type=MESH
        )
        cp.start()
        return cp

    def sent(src, s):
        pltpu.make_async_copy(src, src, s).wait()

    def arrived(dst, r):
        pltpu.make_async_copy(dst, dst, r).wait()

    early = [
        pltpu.make_async_copy(nin_hbm, nin_ref, loc.at[3]),
        pltpu.make_async_copy(noi_hbm, noi_ref, loc.at[4]),
    ]
    loads = [
        pltpu.make_async_copy(up_ref.at[0], U, loc.at[0]),
        pltpu.make_async_copy(down_ref.at[0], W.at[0], loc.at[1]),
        pltpu.make_async_copy(par_hbm, par_ref, loc.at[2]),
    ]
    for cp in early + loads:
        cp.start()

    barrier = pltpu.get_barrier_semaphore()
    peers = [xdev(d) for d in FAR] + [zdev(d) for d in FAR]
    peers += [device(x, turn(y, d), z, c) for d in FAR] + [sib]
    twin = y + 1 - 2 * lax.rem(y, 2)
    peers += [device(turn(x, d), y, z, 1 - c) for d in FAR]
    peers += [device(x, twin, turn(z, d), c) for d in FAR]
    for dev in peers:
        pl.semaphore_signal(barrier, inc=1, device_id=dev, device_id_type=MESH)
    pl.semaphore_wait(barrier, len(peers))
    for cp in early:
        cp.wait()

    def own_cols(p):
        return pl.ds(pl.multiple_of(xh * (2 * PW) + p * PW, 128), PW)

    own_rows = pl.ds(pl.multiple_of(c * RB, RB), RB)

    class Gather:
        def __init__(self, buf, order, s1s, s1r, s2s, s2r):
            self.buf, self.order = buf, order
            self.sems = (s1s, s1r, s2s, s2r)

        def block(self, d1, d2):
            if self.order == "xz":
                return self.buf.at[turn(x, -d1), turn(z, -d2)]
            return self.buf.at[turn(x, -d2), turn(z, -d1)]

        def peer(self, ring, d):
            return xdev(d) if (self.order == "xz") == (ring == 1) else zdev(d)

        def first(self):
            own = self.block(0, 0)
            for d in FAR:
                send(own, own, self.sems[0].at[d - 1], self.sems[1].at[d - 1], self.peer(1, d))

        def second(self, d1):
            b = self.block(d1, 0)
            for d in FAR:
                send(b, b, self.sems[2].at[d1, d - 1], self.sems[3].at[d1, d - 1], self.peer(2, d))

        def wait1(self, d1):
            arrived(self.block(d1, 0), self.sems[1].at[d1 - 1])

        def wait2(self, d1, d2):
            arrived(self.block(d1, d2), self.sems[3].at[d1, d2 - 1])

        def drain(self):
            own = self.block(0, 0)
            for d in FAR:
                sent(own, self.sems[0].at[d - 1])
                for d1 in range(4):
                    sent(own, self.sems[2].at[d1, d - 1])

    def gather_start(A, B):
        A.first()
        B.first()
        A.second(0)
        B.second(0)

    def gather_forward(A, B):
        for d in FAR:
            A.wait1(d)
            A.second(d)
            B.wait1(d)
            B.second(d)

    def gather_group(A, B, dz):
        if dz == 0:
            for d in FAR:
                B.wait2(0, d)
        else:
            for d1 in range(4):
                A.wait2(d1, dz)
            for d in FAR:
                B.wait2(dz, d)

    g1a = Gather(G1.at[0], "xz", a1s.at[0], a1r.at[0], a2s.at[0], a2r.at[0])
    g1b = Gather(G1.at[1], "zx", b1s.at[0], b1r.at[0], b2s.at[0], b2r.at[0])
    g2a = Gather(G2A, "xz", a1s.at[1], a1r.at[1], a2s.at[1], a2r.at[1])
    g2b = Gather(G2B, "zx", b1s.at[1], b1r.at[1], b2s.at[1], b2r.at[1])

    @pl.when(is_gen)
    def _():
        for p in range(2):
            G1[p, x, z] = nin_ref[own_rows, own_cols(p)]
        gather_start(g1a, g1b)

    loads[0].wait()

    def transpose(i, carry):
        cols = pl.ds(pl.multiple_of(i * CW, CW), CW)
        UT[0, cols, :] = U[:, cols].T
        return carry

    lax.fori_loop(0, D // CW, transpose, 0)
    send(UT.at[0], UT.at[1], wss.at[0], wrs.at[0], sib)
    send(down_ref.at[0], W.at[1], wss.at[1], wrs.at[1], sib)
    loads[2].wait()
    for j in range(5):
        PR[j : j + 1, :] = par_ref[j, pl.ds(role, 1), :]
    PR[5:6, :] = par_ref[4, 0:1, :]
    PR[6:7, :] = par_ref[4, 1:2, :]

    @pl.when(is_gen)
    def _():
        for l in range(8):
            E[l // 4, l % 4] = vec_ref[0:1, :]

    @pl.when(jnp.logical_not(is_gen))
    def _():
        E[xl, z] = vec_ref[1:2, :]
        own = E.at[xl, z]
        for d in FAR:
            send(own, own, es.at[d - 1], er.at[d - 1], zdev(d))
        for d in FAR:
            arrived(E.at[xl, turn(z, -d)], er.at[d - 1])
        send(E.at[xl], E.at[xl], es.at[3], er.at[3], xdev(1))
        arrived(E.at[1 - xl], er.at[3])

    H[...] = jnp.zeros_like(H)
    act[...] = jnp.zeros_like(act)
    DA[...] = jnp.zeros_like(DA)

    def make_x0(p):
        total = yS[0, p].astype(f32) + yS[1, p].astype(f32)
        gate = PR[5:6, own_cols(p)] + vec_ref[0:1, own_cols(p)]
        X0[p] = (nin_ref[own_rows, own_cols(p)].astype(f32) + gate * total).astype(bf16)

    def y_send(buf, slot, p, k):
        own = buf.at[slot, p]
        for i, to in enumerate((3 - y, turn(y, 2), twin)):
            send(own, own, ys.at[k, p, i], yr.at[k, p, slot], device(x, to, z, c))

    def y_wait(buf, slot, p, k):
        arrived(buf.at[slot, p], yr.at[k, p, slot])

    def y_drain(buf, k):
        for p in range(2):
            for d in FAR:
                sent(buf.at[0, 0], ys.at[k, p, d - 1])

    @pl.when(jnp.logical_not(is_gen))
    def _():
        for p, g in ((0, g1a), (1, g1b)):
            y_wait(yS, 0, p, 0)
            y_wait(yS, 1, p, 0)
            make_x0(p)
            cols = own_cols(p)
            noisy = vec_ref[2:3, cols] * X0[p].astype(f32) + vec_ref[3:4, cols] * noi_ref[own_rows, cols].astype(f32)
            G1[p, x, z] = noisy.astype(bf16)
            g.first()
        g1a.second(0)
        g1b.second(0)

    gather_forward(g1a, g1b)

    def norm_rows(zz, xl_):
        rows = pl.ds(pl.multiple_of(zz * 32 + xl_ * RB, RB), RB)

        def piece(k):
            return G1[k % 2, 2 * (k // 2) + xl_, zz].astype(f32)

        mean = sum(jnp.sum(piece(k), axis=1, keepdims=True) for k in range(4)) / D
        var = sum(jnp.sum(jnp.square(piece(k) - mean), axis=1, keepdims=True) for k in range(4)) / D
        rstd = lax.rsqrt(var + epsilon_norm)
        for k in range(4):
            cols = slice(k * PW, (k + 1) * PW)
            e = E[xl_, zz, :, cols]
            scale = 1.0 + PR[3:4, cols] + e
            gain = (1.0 + PR[0:1, cols]) * scale
            bias = PR[1:2, cols] * scale + (PR[2:3, cols] + e)
            xhat = (piece(k) - mean) * rstd
            uu[rows, cols] = (xhat * gain + bias).astype(bf16)
            XH[rows, cols] = xhat.astype(bf16)

    for dz in (0, 1, 3, 2):
        gather_group(g1a, g1b, dz)
        zz = turn(z, -dz)

        def both(i, carry, zz=zz):
            norm_rows(zz, i)
            return carry

        lax.fori_loop(0, 2, both, 0)

    arrived(UT.at[1], wrs.at[0])
    for s in range(2):
        H[s, :, 0:HU] = jnp.dot(uu[0:128, :], UT[s], preferred_element_type=f32)

    for s in range(2):
        act[s] = gelu_parts(H[s])[0].astype(bf16)
    loads[1].wait()
    arrived(W.at[1], wrs.at[1])

    def z_piece(xh_, p):
        cols = slice((xh_ * 2 + p) * PW, (xh_ * 2 + p + 1) * PW)
        acc = jnp.dot(act[0, :, 0:HU], W[0, :, cols], preferred_element_type=f32)
        acc += jnp.dot(act[1, :, 0:HU], W[1, :, cols], preferred_element_type=f32)
        acc = acc.astype(bf16)
        for z_ in range(4):
            for xl_ in range(2):
                rows = acc[z_ * 32 + xl_ * RB : z_ * 32 + (xl_ + 1) * RB]
                if p == 0:
                    zsA[2 * xh_ + xl_, z_] = rows
                else:
                    zsB[z_, 2 * xh_ + xl_] = rows

    for xh_ in range(2):
        z_piece(xh_, 0)
        for xl_ in range(2):
            to = 2 * xh_ + xl_

            @pl.when(to != x)
            def _():
                d = lax.rem(to + 4 - x, 4)
                send(zsA.at[to], rsA.at[d - 1], rsAs.at[d - 1], rsAr.at[d - 1], device(to, y, z, c))

        z_piece(xh_, 1)
        two = pl.ds(2 * xh_, 2)
        for d in FAR:
            send(
                zsB.at[turn(z, d), two], rsB.at[d - 1, two],
                rsBs.at[d - 1, xh_], rsBr.at[d - 1, xh_], zdev(d),
            )

    half = pl.ds(0, 128)
    other = pl.ds(128, 128)
    shared = [
        (H.at[1], HS, 0),
        (uu.at[half], uu.at[other], 1),
        (XH.at[half], XH.at[other], 2),
    ]
    for src, dst, k in shared:
        send(src, dst, xs.at[k], xr.at[k], sib)

    parts = ((0, zsA, rsA, x, z, zdev), (1, zsB, rsB, z, x, xdev))
    for p, zs, rs, first, second, peer in parts:
        for d in FAR:
            if p == 0:
                arrived(rsA.at[d - 1], rsAr.at[d - 1])
            else:
                for xh_ in range(2):
                    arrived(rsB.at[d - 1, pl.ds(2 * xh_, 2)], rsBr.at[d - 1, xh_])

        def add(i, carry, p=p, zs=zs, rs=rs, first=first):
            total = zs[first, i].astype(f32)
            for d in range(3):
                total += rs[d, i].astype(f32)
            sf[p, i] = total
            ss2[p, i] = total.astype(bf16)
            return carry

        lax.fori_loop(0, 4, add, 0)
        for d in FAR:
            send(ss2.at[p, turn(second, d)], r2.at[p, d - 1], rs2s.at[p, d - 1], rs2r.at[p, d - 1], peer(d))
    for p, zs, rs, first, second, peer in parts:
        for d in FAR:
            arrived(r2.at[p, d - 1], rs2r.at[p, d - 1])
        total = sf[p, second]
        for d in range(3):
            total += r2[p, d].astype(f32)
        Z[p] = total

        @pl.when(is_gen)
        def _(p=p, total=total):
            yS[y, p] = total.astype(bf16)
            y_send(yS, y, p, 0)

        @pl.when(jnp.logical_not(is_gen))
        def _(p=p, total=total):
            gate = PR[4:5, own_cols(p)] + vec_ref[1:2, own_cols(p)]
            yF[y - 2, p] = (G1[p, x, z].astype(f32) + gate * total).astype(bf16)
            y_send(yF, y - 2, p, 1)

    @pl.when(is_gen)
    def _():
        for p in range(2):
            y_wait(yS, 1 - y, p, 0)
            make_x0(p)
            Z[p] = yS[0, p].astype(f32) + yS[1, p].astype(f32)

    dist = jnp.zeros((1, 1), f32)
    for p, g in ((0, g2a), (1, g2b)):
        @pl.when(is_gen)
        def _(p=p):
            y_wait(yF, 0, p, 1)
            y_wait(yF, 1, p, 1)

        @pl.when(jnp.logical_not(is_gen))
        def _(p=p):
            y_wait(yF, 3 - y, p, 1)

        fake, real, x0 = yF[0, p].astype(f32), yF[1, p].astype(f32), X0[p].astype(f32)
        gap = (fake - real).astype(bf16)
        Dv[p] = gap
        dist += jnp.sum(jnp.sum(jnp.abs(x0 - real), axis=0, keepdims=True), axis=1, keepdims=True)
        gate = PR[6:7, own_cols(p)] + vec_ref[1:2, own_cols(p)]
        critic = ((fake - x0) * 0.125 * gate).astype(bf16)
        block = jnp.where(y == 2, critic, gap)
        if p == 0:
            G2A[x, z, :, 0:PW] = block
        else:
            G2B[x, z] = block
    hi = dist.astype(bf16)
    mid = (dist - hi.astype(f32)).astype(bf16)
    low = (dist - hi.astype(f32) - mid.astype(f32)).astype(bf16)
    lane = lax.broadcasted_iota(jnp.int32, (RB, 128), 1)
    tile = jnp.where(lane == 0, hi.astype(f32), jnp.where(lane == 1, mid.astype(f32), low.astype(f32)))
    G2A[x, z, :, PW:] = tile.astype(bf16)
    g2a.first()
    g2b.first()
    g2a.second(0)
    g2b.second(0)

    @pl.when(y == 2)
    def _():
        for p in range(2):
            DX[xh, p] = Dv[p]
        send(DX.at[xh], DX.at[xh], dxs, dxr, xdev(2))

    gather_forward(g2a, g2b)

    def gap_piece(k, xl_, zz):
        col = 2 * (k // 2) + xl_
        return G2A[col, zz, :, 0:PW] if k % 2 == 0 else G2B[col, zz]

    def share(xl_, zz):
        def one(col):
            tile = G2A[col, zz, :, PW:].astype(f32)
            return (tile[0:1, 0:1] + tile[0:1, 1:2]) + tile[0:1, 2:3]

        return one(xl_) + one(2 + xl_)

    def inverse(l):
        return 1.0 / ((CS[0, l : l + 1, :] + CS[1, l : l + 1, :]) / (32.0 * D) + epsilon_gap)

    def scaled_rows(zz, xl_):
        rows = pl.ds(pl.multiple_of(zz * 32 + xl_ * RB, RB), RB)
        for k in range(4):
            cols = slice(k * PW, (k + 1) * PW)
            gate = PR[5:6, cols] + vec_ref[0:1, cols]
            factor = jnp.where(y == 2, jnp.ones_like(gate), gate * 0.125)
            DZ[rows, cols] = (gap_piece(k, xl_, zz).astype(f32) * factor).astype(bf16)

    for i, dz in enumerate((0, 1, 3, 2)):
        gather_group(g2a, g2b, dz)
        zz = turn(z, -dz)

        def both(j, carry, zz=zz):
            scaled_rows(zz, j)
            return carry

        lax.fori_loop(0, 2, both, 0)
        rows = pl.ds(pl.multiple_of(zz * 32, 32), 32)
        orows = pl.ds(pl.multiple_of(128 + zz * 32, 32), 32)
        send(DZ.at[rows], DZ.at[orows], dzs.at[i], dzr.at[i], sib)

    for l in range(8):
        CS[0, l : l + 1, :] = jnp.broadcast_to(share(l % 2, l // 2), (1, 128))
    send(CS.at[0], CS.at[1], scs.at[0], scr.at[0], sib)
    live = y < 3
    arrived(HS, xr.at[0])
    for i, dz in enumerate((0, 1, 3, 2)):
        orows = pl.ds(pl.multiple_of(128 + turn(z, -dz) * 32, 32), 32)
        arrived(DZ.at[orows], dzr.at[i])
    DA[:, 0:HU] = lax.dot_general(DZ[...], W[0], NT, preferred_element_type=f32)
    arrived(CS.at[1], scr.at[0])
    for l in range(8):
        inv = jnp.where(y == 2, 1.0, inverse(l)[:, 0:1])
        IV[l * RB : (l + 1) * RB, :] = jnp.broadcast_to(inv, (RB, 256))
    for s in range(2):
        rows = slice(s * 128, (s + 1) * 128)
        value, slope = gelu_parts(H[0] if s == 0 else HS[...])
        dh = jnp.where(live, DA[rows, :] * slope * IV[...], 0.0)
        DA[rows, :] = dh
        dhb[rows, :] = dh.astype(bf16)

    arrived(XH.at[other], xr.at[2])

    SM[...] = jnp.zeros_like(SM)

    def small(i, carry):
        cols = pl.ds(pl.multiple_of(i * CW, CW), CW)
        du = jnp.dot(dhb[:, 0:HU], U[:, cols], preferred_element_type=f32)
        dx = du * XH[:, cols].astype(f32)
        p3 = 1.0 + PR[3:4, cols]
        rows = [jnp.zeros((8, CW), f32) for _ in range(4)]
        for l in range(8):
            starts = [l * RB + k for k in (0, 8, 128, 136)]
            plain = sum(du[k : k + 8] for k in starts)
            norm = sum(dx[k : k + 8] for k in starts)
            scale = p3 + E[l % 2, l // 2, :, cols]
            for k, term in enumerate((scale * norm, scale * plain, plain, norm)):
                rows[k] += term
        rows = [jnp.sum(row, axis=0, keepdims=True) for row in rows]
        SM[0:1, cols] = rows[0]
        SM[1:2, cols] = rows[1]
        SM[2:3, cols] = rows[2]
        SM[3:4, cols] = (1.0 + PR[0:1, cols]) * rows[3] + PR[1:2, cols] * rows[2]
        return carry

    lax.fori_loop(0, D // CW, small, 0)

    own_row = pl.ds(z * 2 + xl, 1)
    inv_own = (1.0 / ((CS[0, own_row, :] + CS[1, own_row, :]) / (32.0 * D) + epsilon_gap))[:, 0:1]

    @pl.when(y == 2)
    def _():
        arrived(DX.at[1 - xh], dxr)
        for k in range(4):
            score_out[own_rows, k * PW : (k + 1) * PW] = DX[k // 2, k % 2].astype(f32) * inv_own

    @pl.when(y != 2)
    def _():
        for k in range(4):
            score_out[own_rows, k * PW : (k + 1) * PW] = gap_piece(k, xl, z).astype(f32) * inv_own

    send(score_out.at[own_rows], score_out.at[own_rows], scs.at[1], scr.at[1], sib)

    own_row = pl.ds(z * 2 + xl, 1)
    inv_own = (1.0 / ((CS[0, own_row, :] + CS[1, own_row, :]) / (32.0 * D) + epsilon_gap))[:, 0:1]
    for p in range(2):
        fake, x0 = yF[0, p].astype(f32), X0[p].astype(f32)
        cot = jnp.where(y == 2, fake - x0, Dv[p].astype(f32) * inv_own) * 0.125
        row = jnp.sum(cot * Z[p], axis=0, keepdims=True)
        SM[4:5, own_cols(p)] = jnp.where(jnp.logical_or(y == 0, y == 2), row, 0.0)

    for k in range(32):
        start = k * SW // 128 * 128
        window = SM[:, start : start + 256]
        off = k * SW - start
        if off:
            window = pltpu.roll(window, 256 - off, 1)
        f_, t_ = k // 4, k % 4
        row = f_ % 4 * 8
        T[t_ % 2, (t_ // 2) * 2 + f_ // 4, row : row + 8] = window

    T16[...] = T[...].astype(bf16)
    near = [(dx, dc) for dc in range(2) for dx in (0, 1, 3, 2) if dx + dc]
    for k, (dx, dc) in enumerate(near):
        c_ = c if dc == 0 else 1 - c
        send(T16.at[c_, turn(x, dx)], TX.at[k], t1s.at[k], t1r.at[k], device(turn(x, dx), y, z, c_))

    live_rows = jnp.where(live, IV[...], 0.0)
    for s in range(2):
        rows = slice(s * 128, (s + 1) * 128)
        value = gelu_parts(H[0] if s == 0 else HS[...])[0]
        dht[:, rows] = DA[rows, :].T.astype(bf16)
        at[:, rows] = (value * live_rows).T.astype(bf16)
    arrived(uu.at[other], xr.at[1])

    def product(left, right, out):
        def step(i, carry):
            cols = pl.ds(pl.multiple_of(i * CW, CW), CW)
            out[:, cols] = jnp.dot(left[...], right[:, cols], preferred_element_type=f32)[0:HU]
            return carry

        lax.fori_loop(0, D // CW, step, 0)

    product(dht, uu, GU)
    for k in range(7):
        arrived(TX.at[k], t1r.at[k])
    total = T[c, x]
    for k in range(7):
        total += TX[k].astype(f32)
    for z_ in range(4):
        T3[z_] = total[z_ * 8 : z_ * 8 + 8]
    for k, d in enumerate(FAR):
        send(T3.at[turn(z, d)], TZ.at[k], t2s.at[k], t2r.at[k], zdev(d))

    @pl.when(is_gen)
    def _():
        for k in range(4):
            d = (0,) + FAR
            send(T3.at[turn(z, d[k])], TZ.at[3 + k], t2s.at[3 + k], t2r.at[3 + k], device(x, twin, turn(z, d[k]), c))

    for k in range(3):
        arrived(TZ.at[k], t2r.at[k])
    small_out[...] = T3[z] + TZ[0] + TZ[1] + TZ[2]

    @pl.when(is_gen)
    def _():
        for k in range(4):
            arrived(TZ.at[3 + k], t2r.at[3 + k])
            sent(TZ.at[3 + k], t2s.at[3 + k])
        small_out[...] = small_out[...] + (TZ[3] + TZ[4] + TZ[5] + TZ[6])

    arrived(score_out.at[pl.ds(pl.multiple_of((1 - c) * RB, RB), RB)], scr.at[1])
    sent(score_out.at[own_rows], scs.at[1])
    sent(CS.at[0], scs.at[0])
    for k in range(7):
        sent(TX.at[k], t1s.at[k])
    for k in range(3):
        sent(TZ.at[k], t2s.at[k])
    for g in (g1a, g1b, g2a, g2b):
        g.drain()
    sent(UT.at[0], wss.at[0])
    sent(down_ref.at[0], wss.at[1])
    for src, dst, k in shared:
        sent(src, xs.at[k])
    for p, zs, rs, first, second, peer in parts:
        for d in FAR:
            if p == 0:
                sent(rs.at[0], rsAs.at[d - 1])
            else:
                for xh_ in range(2):
                    sent(rs.at[0, pl.ds(0, 2)], rsBs.at[d - 1, xh_])
            sent(r2.at[p, 0], rs2s.at[p, d - 1])
    for i in range(4):
        sent(DZ.at[pl.ds(0, 32)], dzs.at[i])

    @pl.when(is_gen)
    def _():
        y_drain(yS, 0)

    @pl.when(jnp.logical_not(is_gen))
    def _():
        y_drain(yF, 1)
        for d in FAR:
            sent(E.at[0, 0], es.at[d - 1])
        sent(E.at[0], es.at[3])

    @pl.when(y == 2)
    def _():
        sent(DX.at[0], dxs)

def place_kernel(gu, at, dz, score, small, up_out, down_out, score_out, small_out, gd, sems, down_sems):
    cuts = ((0, 56), (56, 56), (112, 56), (168, 48))
    copies = [pltpu.make_async_copy(score, score_out, sems.at[0])]
    for k, (start, size) in enumerate(cuts):
        rows = pl.ds(start, size)
        copies.append(pltpu.make_async_copy(gu.at[rows], up_out.at[0, rows], sems.at[1 + k]))
    for cp in copies:
        cp.start()
    for k in range(5):
        small_out[k] = small[k : k + 1, 0:SW]
    for i in range(D // CW):
        cols = pl.ds(i * CW, CW)
        gd[:, cols] = jnp.dot(at[...], dz[:, cols], preferred_element_type=f32)[0:HU]
        cp = pltpu.make_async_copy(gd.at[:, cols], down_out.at[0, :, cols], down_sems.at[i])
        cp.start()
        copies.append(cp)
    for cp in copies:
        cp.wait()

def per_device(noise_in, noise, timesteps, up_weight, down_weight, small_params):
    step_value = timesteps[0].astype(f32)
    angle = 0.5 * math.pi * step_value / 1000.0
    vec = jnp.stack(
        [
            embedding(jnp.float32(gen_time), D),
            embedding(step_value, D),
            jnp.full((D,), jnp.cos(angle)),
            jnp.full((D,), jnp.sin(angle)),
        ]
    )
    dma = pltpu.SemaphoreType.DMA
    vm = pltpu.VMEM
    vmem = pl.BlockSpec(memory_space=pltpu.VMEM)
    hbm = pl.BlockSpec(memory_space=pl.ANY)
    scratch = [
        vm((32, D), bf16),
        vm((32, D), bf16),
        vm((256, D), bf16),
        vm((5, 3, D), f32),
        vm((8, D), f32),
        vm((HP, 256), bf16),
        vm((128, 256), f32),
        vm((HU, D), bf16),
        vm((2, D, HU), bf16),
        vm((2, HU, D), bf16),
        vm((2, 4, 1, D), f32),
        vm((2, 4, 4, RB, PW), bf16),
        vm((4, 4, RB, PW + 128), bf16),
        vm((4, 4, RB, PW), bf16),
        vm((2, 2, RB, PW), bf16),
        vm((256, D), bf16),
        vm((2, 128, HP), f32),
        vm((128, HP), f32),
        vm((2, 128, HP), bf16),
        vm((256, HP), f32),
        vm((256, HP), bf16),
        vm((4, 4, RB, PW), bf16),
        vm((4, 4, RB, PW), bf16),
        vm((3, 4, RB, PW), bf16),
        vm((3, 4, RB, PW), bf16),
        vm((2, 4, RB, PW), f32),
        vm((2, 4, RB, PW), bf16),
        vm((2, 3, RB, PW), bf16),
        vm((2, RB, PW), f32),
        vm((2, 2, RB, PW), bf16),
        vm((2, 2, RB, PW), bf16),
        vm((2, RB, PW), bf16),
        vm((2, RB, PW), bf16),
        vm((2, 8, 128), f32),
        vm((8, D), f32),
        vm((2, 4, 32, 256), f32),
        vm((2, 4, 32, 256), bf16),
        vm((7, 32, 256), bf16),
        vm((4, 8, 256), f32),
        vm((7, 8, 256), f32),
        dma((5,)), dma((2,)), dma((2,)), dma((4,)), dma((4,)),
        dma((2, 3)), dma((2, 3)), dma((2, 4, 3)), dma((2, 4, 3)),
        dma((2, 3)), dma((2, 3)), dma((2, 4, 3)), dma((2, 4, 3)),
        dma((3,)), dma((3,)), dma((3, 2)), dma((3, 2)), dma((2, 3)), dma((2, 3)),
        dma((2, 2, 3)), dma((2, 2, 2)), dma((3,)), dma((3,)), dma(()), dma(()),
        dma((4,)), dma((4,)), dma((2,)), dma((2,)), dma((7,)), dma((7,)), dma((7,)), dma((7,)),
    ]
    parts = pl.pallas_call(
        chain_kernel,
        out_shape=[
            vm((HU, D), f32),
            vm((HP, 256), bf16),
            vm((256, D), bf16),
            vm((32, D), f32),
            vm((8, 256), f32),
        ],
        in_specs=[hbm, hbm, hbm, hbm, vmem, hbm],
        out_specs=[vmem] * 5,
        scratch_shapes=scratch,
        compiler_params=pltpu.CompilerParams(
            collective_id=0, has_side_effects=True, vmem_limit_bytes=52 * 2**20
        ),
        name="chain",
    )(up_weight, down_weight, noise_in, noise, vec, jnp.transpose(small_params, (1, 0, 2)))
    up_grad, down_grad, score, small = pl.pallas_call(
        place_kernel,
        out_shape=[
            jax.ShapeDtypeStruct((1, HU, D), f32),
            jax.ShapeDtypeStruct((1, HU, D), f32),
            jax.ShapeDtypeStruct((32, D), f32),
            jax.ShapeDtypeStruct((5, 1, SW), f32),
        ],
        in_specs=[vmem] * 5,
        out_specs=[hbm, hbm, hbm, vmem],
        scratch_shapes=[vm((HU, D), f32), dma((5,)), dma((D // CW,))],
        compiler_params=pltpu.CompilerParams(vmem_limit_bytes=24 * 2**20),
        name="place",
    )(*parts)
    return (score, up_grad, down_grad, jnp.transpose(small, (1, 0, 2)))

def solution(mesh):
    in_specs = (
        P("fsdp", None),
        P("fsdp", None),
        P("fsdp"),
        P("group", ("fsdp", "tp"), None),
        P("group", ("fsdp", "tp"), None),
        P(),
    )
    out_specs = (
        P("fsdp", None),
        P("group", ("fsdp", "tp"), None),
        P("group", ("fsdp", "tp"), None),
        P("group", None, ("fsdp", "tp")),
    )
    return jax.shard_map(
        per_device, mesh=mesh, in_specs=in_specs, out_specs=out_specs, check_vma=False
    )
```

```python
import functools
import math

import jax
import jax.numpy as jnp
from jax import lax
from jax.experimental import pallas as pl
from jax.experimental.pallas import tpu as pltpu
from jax.sharding import PartitionSpec as P

MESH = pl.DeviceIdType.MESH
bf16, f32 = jnp.bfloat16, jnp.float32
gen_time = 999.0
epsilon_norm = 1e-06
epsilon_gap = 1e-05

D = 5120
HU = 216
HP = 256
RB = 16
PW = 1280
SW = 160
CW = 1024
NT = (((1,), (1,)), ((), ()))
FAR = (2, 1, 3)


def device(x, y, z, c):
    return (y, lax.rem(x, 2) * 4 + z, lax.div(x, 2) * 2 + c)


def turn(value, steps):
    return lax.rem(value + (steps % 4), 4)


def gelu_parts(h):
    k = math.sqrt(2.0 / math.pi)
    t = jnp.tanh(k * (h + 0.044715 * (h * h * h)))
    value = 0.5 * h * (1.0 + t)
    slope = 0.5 * (1.0 + t) + 0.5 * h * (1.0 - t * t) * (k * (1.0 + 3.0 * 0.044715 * (h * h)))
    return value, slope


def chain_kernel(
    up_ref, down_ref, nin_hbm, noi_hbm, time_ref, par_hbm,
    GU, at, DZ, score_out, small_out,
    vec_ref, nin_ref, noi_ref, uu, par_ref, PR, dht, IV, U, UT, W, E, G1, G2A, G2B, DX, XH, H, HS, act, DA, dhb,
    zsA, zsB, rsA, rsB, sf, ss2, r2, Z, yS, yF, X0, Dv, CS, SM, T, T16, TX, T3, TZ,
    loc, wss, wrs, es, er,
    a1s, a1r, a2s, a2r, b1s, b1r, b2s, b2r,
    rsAs, rsAr, rsBs, rsBr, rs2s, rs2r, ys, yr, xs, xr, dxs, dxr, dzs, dzr, scs, scr, t1s, t1r, t2s, t2r,
):
    y = lax.axis_index("group")
    fi = lax.axis_index("fsdp")
    ti = lax.axis_index("tp")
    xl, z = lax.div(fi, 4), lax.rem(fi, 4)
    xh, c = lax.div(ti, 2), lax.rem(ti, 2)
    x = xh * 2 + xl
    role = jnp.maximum(y - 1, 0)
    is_gen = y < 2
    pending = []

    def xdev(d):
        return device(turn(x, d), y, z, c)

    def zdev(d):
        return device(x, y, turn(z, d), c)

    sib = device(x, y, z, 1 - c)

    def send(src, dst, s, r, dev):
        cp = pltpu.make_async_remote_copy(
            src_ref=src, dst_ref=dst, send_sem=s, recv_sem=r, device_id=dev, device_id_type=MESH
        )
        cp.start()
        return cp

    def sent(src, s):
        pltpu.make_async_copy(src, src, s).wait()

    def arrived(dst, r):
        pltpu.make_async_copy(dst, dst, r).wait()

    early = [
        pltpu.make_async_copy(nin_hbm, nin_ref, loc.at[3]),
        pltpu.make_async_copy(noi_hbm, noi_ref, loc.at[4]),
    ]
    loads = [
        pltpu.make_async_copy(up_ref.at[0], U, loc.at[0]),
        pltpu.make_async_copy(down_ref.at[0], W.at[0], loc.at[1]),
        pltpu.make_async_copy(par_hbm, par_ref, loc.at[2]),
    ]
    for cp in early + loads:
        cp.start()

    barrier = pltpu.get_barrier_semaphore()
    peers = [xdev(d) for d in FAR] + [zdev(d) for d in FAR]
    peers += [device(x, turn(y, d), z, c) for d in FAR] + [sib]
    twin = y + 1 - 2 * lax.rem(y, 2)
    peers += [device(turn(x, d), y, z, 1 - c) for d in FAR]
    peers += [device(x, twin, turn(z, d), c) for d in FAR]
    for dev in peers:
        pl.semaphore_signal(barrier, inc=1, device_id=dev, device_id_type=MESH)
    pl.semaphore_wait(barrier, len(peers))
    for cp in early:
        cp.wait()

    def own_cols(p):
        return pl.ds(pl.multiple_of(xh * (2 * PW) + p * PW, 128), PW)

    own_rows = pl.ds(pl.multiple_of(c * RB, RB), RB)

    class Gather:
        def __init__(self, buf, order, s1s, s1r, s2s, s2r):
            self.buf, self.order = buf, order
            self.sems = (s1s, s1r, s2s, s2r)

        def block(self, d1, d2):
            if self.order == "xz":
                return self.buf.at[turn(x, -d1), turn(z, -d2)]
            return self.buf.at[turn(x, -d2), turn(z, -d1)]

        def peer(self, ring, d):
            return xdev(d) if (self.order == "xz") == (ring == 1) else zdev(d)

        def first(self):
            own = self.block(0, 0)
            for d in FAR:
                send(own, own, self.sems[0].at[d - 1], self.sems[1].at[d - 1], self.peer(1, d))

        def second(self, d1):
            b = self.block(d1, 0)
            for d in FAR:
                send(b, b, self.sems[2].at[d1, d - 1], self.sems[3].at[d1, d - 1], self.peer(2, d))

        def wait1(self, d1):
            arrived(self.block(d1, 0), self.sems[1].at[d1 - 1])

        def wait2(self, d1, d2):
            arrived(self.block(d1, d2), self.sems[3].at[d1, d2 - 1])

        def drain(self):
            own = self.block(0, 0)
            for d in FAR:
                sent(own, self.sems[0].at[d - 1])
                for d1 in range(4):
                    sent(own, self.sems[2].at[d1, d - 1])

    def gather_start(A, B):
        A.first()
        B.first()
        A.second(0)
        B.second(0)

    def gather_forward(A, B):
        for d in (1, 3, 2):
            A.wait1(d)
            A.second(d)
            B.wait1(d)
            B.second(d)

    def gather_group(A, B, dz):
        if dz == 0:
            for d in FAR:
                B.wait2(0, d)
        else:
            for d1 in range(4):
                A.wait2(d1, dz)
            for d in FAR:
                B.wait2(dz, d)

    g1a = Gather(G1.at[0], "xz", a1s.at[0], a1r.at[0], a2s.at[0], a2r.at[0])
    g1b = Gather(G1.at[1], "zx", b1s.at[0], b1r.at[0], b2s.at[0], b2r.at[0])
    g2a = Gather(G2A, "xz", a1s.at[1], a1r.at[1], a2s.at[1], a2r.at[1])
    g2b = Gather(G2B, "zx", b1s.at[1], b1r.at[1], b2s.at[1], b2r.at[1])

    @pl.when(is_gen)
    def _():
        for p in range(2):
            G1[p, x, z] = nin_ref[own_rows, own_cols(p)]
        gather_start(g1a, g1b)

    loads[0].wait()

    def transpose(i, carry):
        cols = pl.ds(pl.multiple_of(i * CW, CW), CW)
        UT[0, cols, :] = U[:, cols].T
        return carry

    lax.fori_loop(0, D // CW, transpose, 0)
    send(UT.at[0], UT.at[1], wss.at[0], wrs.at[0], sib)
    send(down_ref.at[0], W.at[1], wss.at[1], wrs.at[1], sib)
    loads[2].wait()
    for j in range(5):
        PR[j : j + 1, :] = par_ref[j, pl.ds(role, 1), :]
    PR[5:6, :] = par_ref[4, 0:1, :]
    PR[6:7, :] = par_ref[4, 1:2, :]

    step_value = time_ref[0].astype(f32)
    lane = lax.broadcasted_iota(jnp.int32, (2, D // 2), 1).astype(f32)
    row = lax.broadcasted_iota(jnp.int32, (2, D // 2), 0)
    angles = jnp.where(row == 0, gen_time, step_value) * jnp.exp(-math.log(10000.0) * lane / (D // 2))
    vec_ref[0:2, 0 : D // 2] = jnp.cos(angles)
    vec_ref[0:2, D // 2 : D] = jnp.sin(angles)
    turn_angle = jnp.full((1, 128), 0.5 * math.pi, f32) * step_value / 1000.0
    vec_ref[2:3, :] = jnp.broadcast_to(jnp.cos(turn_angle)[:, 0:1], (1, D))
    vec_ref[3:4, :] = jnp.broadcast_to(jnp.sin(turn_angle)[:, 0:1], (1, D))

    @pl.when(is_gen)
    def _():
        for l in range(8):
            E[l // 4, l % 4] = vec_ref[0:1, :]

    @pl.when(jnp.logical_not(is_gen))
    def _():
        E[xl, z] = vec_ref[1:2, :]
        own = E.at[xl, z]
        for d in FAR:
            send(own, own, es.at[d - 1], er.at[d - 1], zdev(d))
        for d in FAR:
            arrived(E.at[xl, turn(z, -d)], er.at[d - 1])
        send(E.at[xl], E.at[xl], es.at[3], er.at[3], xdev(1))
        arrived(E.at[1 - xl], er.at[3])

    H[...] = jnp.zeros_like(H)
    act[...] = jnp.zeros_like(act)
    DA[...] = jnp.zeros_like(DA)

    def make_x0(p):
        total = yS[0, p].astype(f32) + yS[1, p].astype(f32)
        gate = PR[5:6, own_cols(p)] + vec_ref[0:1, own_cols(p)]
        X0[p] = (nin_ref[own_rows, own_cols(p)].astype(f32) + gate * total).astype(bf16)

    def y_send(buf, slot, p, k):
        own = buf.at[slot, p]
        for i, to in enumerate((3 - y, turn(y, 2), twin)):
            send(own, own, ys.at[k, p, i], yr.at[k, p, slot], device(x, to, z, c))

    def y_wait(buf, slot, p, k):
        arrived(buf.at[slot, p], yr.at[k, p, slot])

    def y_drain(buf, k):
        for p in range(2):
            for d in FAR:
                sent(buf.at[0, 0], ys.at[k, p, d - 1])

    @pl.when(jnp.logical_not(is_gen))
    def _():
        for p, g in ((0, g1a), (1, g1b)):
            y_wait(yS, 0, p, 0)
            y_wait(yS, 1, p, 0)
            make_x0(p)
            cols = own_cols(p)
            noisy = vec_ref[2:3, cols] * X0[p].astype(f32) + vec_ref[3:4, cols] * noi_ref[own_rows, cols].astype(f32)
            G1[p, x, z] = noisy.astype(bf16)
            g.first()
        g1a.second(0)
        g1b.second(0)

    gather_forward(g1a, g1b)

    def norm_rows(zz, xl_):
        rows = pl.ds(pl.multiple_of(zz * 32 + xl_ * RB, RB), RB)

        def piece(k):
            return G1[k % 2, 2 * (k // 2) + xl_, zz].astype(f32)

        mean = sum(jnp.sum(piece(k), axis=1, keepdims=True) for k in range(4)) / D
        var = sum(jnp.sum(jnp.square(piece(k) - mean), axis=1, keepdims=True) for k in range(4)) / D
        rstd = lax.rsqrt(var + epsilon_norm)
        for k in range(4):
            cols = slice(k * PW, (k + 1) * PW)
            e = E[xl_, zz, :, cols]
            scale = 1.0 + PR[3:4, cols] + e
            gain = (1.0 + PR[0:1, cols]) * scale
            bias = PR[1:2, cols] * scale + (PR[2:3, cols] + e)
            xhat = (piece(k) - mean) * rstd
            uu[rows, cols] = (xhat * gain + bias).astype(bf16)
            XH[rows, cols] = xhat.astype(bf16)

    for dz in (0, 1, 3, 2):
        gather_group(g1a, g1b, dz)
        zz = turn(z, -dz)

        def both(i, carry, zz=zz):
            norm_rows(zz, i)
            return carry

        lax.fori_loop(0, 2, both, 0, unroll=True)

    arrived(UT.at[1], wrs.at[0])
    for s in range(2):
        H[s, :, 0:HU] = jnp.dot(uu[0:128, :], UT[s], preferred_element_type=f32)
    for s in range(2):
        act[s] = gelu_parts(H[s])[0].astype(bf16)
    loads[1].wait()
    arrived(W.at[1], wrs.at[1])

    def z_piece(xh_, p):
        cols = slice((xh_ * 2 + p) * PW, (xh_ * 2 + p + 1) * PW)
        acc = jnp.dot(act[0, :, 0:HU], W[0, :, cols], preferred_element_type=f32)
        acc += jnp.dot(act[1, :, 0:HU], W[1, :, cols], preferred_element_type=f32)
        acc = acc.astype(bf16)
        for z_ in range(4):
            for xl_ in range(2):
                rows = acc[z_ * 32 + xl_ * RB : z_ * 32 + (xl_ + 1) * RB]
                if p == 0:
                    zsA[2 * xh_ + xl_, z_] = rows
                else:
                    zsB[z_, 2 * xh_ + xl_] = rows

    for xh_ in range(2):
        z_piece(xh_, 0)
        for xl_ in range(2):
            to = 2 * xh_ + xl_

            @pl.when(to != x)
            def _():
                d = lax.rem(to + 4 - x, 4)
                send(zsA.at[to], rsA.at[d - 1], rsAs.at[d - 1], rsAr.at[d - 1], device(to, y, z, c))

        z_piece(xh_, 1)
        two = pl.ds(2 * xh_, 2)
        for d in FAR:
            send(
                zsB.at[turn(z, d), two], rsB.at[d - 1, two],
                rsBs.at[d - 1, xh_], rsBr.at[d - 1, xh_], zdev(d),
            )

    half = pl.ds(0, 128)
    other = pl.ds(128, 128)
    shared = [
        (H.at[1], HS, 0),
        (uu.at[half], uu.at[other], 1),
        (XH.at[half], XH.at[other], 2),
    ]
    for src, dst, k in shared:
        send(src, dst, xs.at[k], xr.at[k], sib)

    parts = ((0, zsA, rsA, x, z, zdev), (1, zsB, rsB, z, x, xdev))
    for p, zs, rs, first, second, peer in parts:
        for d in FAR:
            if p == 0:
                arrived(rsA.at[d - 1], rsAr.at[d - 1])
            else:
                for xh_ in range(2):
                    arrived(rsB.at[d - 1, pl.ds(2 * xh_, 2)], rsBr.at[d - 1, xh_])

        for d in FAR + (0,):
            to = turn(second, d)
            total = zs[first, to].astype(f32)
            for k in range(3):
                total += rs[k, to].astype(f32)
            if d == 0:
                sf[p] = total
            else:
                ss2[p, to] = total.astype(bf16)
                send(ss2.at[p, to], r2.at[p, d - 1], rs2s.at[p, d - 1], rs2r.at[p, d - 1], peer(d))
    for p, zs, rs, first, second, peer in parts:
        for d in FAR:
            arrived(r2.at[p, d - 1], rs2r.at[p, d - 1])
        total = sf[p]
        for d in range(3):
            total += r2[p, d].astype(f32)
        Z[p] = total

        @pl.when(is_gen)
        def _(p=p, total=total):
            yS[y, p] = total.astype(bf16)
            y_send(yS, y, p, 0)

        @pl.when(jnp.logical_not(is_gen))
        def _(p=p, total=total):
            gate = PR[4:5, own_cols(p)] + vec_ref[1:2, own_cols(p)]
            yF[y - 2, p] = (G1[p, x, z].astype(f32) + gate * total).astype(bf16)
            y_send(yF, y - 2, p, 1)

    @pl.when(is_gen)
    def _():
        for p in range(2):
            y_wait(yS, 1 - y, p, 0)
            make_x0(p)
            Z[p] = yS[0, p].astype(f32) + yS[1, p].astype(f32)

    dist = jnp.zeros((1, 1), f32)
    for p, g in ((0, g2a), (1, g2b)):
        @pl.when(is_gen)
        def _(p=p):
            y_wait(yF, 0, p, 1)
            y_wait(yF, 1, p, 1)

        @pl.when(jnp.logical_not(is_gen))
        def _(p=p):
            y_wait(yF, 3 - y, p, 1)

        fake, real, x0 = yF[0, p].astype(f32), yF[1, p].astype(f32), X0[p].astype(f32)
        gap = (fake - real).astype(bf16)
        Dv[p] = gap
        dist += jnp.sum(jnp.sum(jnp.abs(x0 - real), axis=0, keepdims=True), axis=1, keepdims=True)
        gate = PR[6:7, own_cols(p)] + vec_ref[1:2, own_cols(p)]
        critic = ((fake - x0) * 0.125 * gate).astype(bf16)
        block = jnp.where(y == 2, critic, gap)
        if p == 0:
            G2A[x, z] = block
            g2a.first()
        else:
            G2B[x, z, :, 0:PW] = block
    hi = dist.astype(bf16)
    mid = (dist - hi.astype(f32)).astype(bf16)
    low = (dist - hi.astype(f32) - mid.astype(f32)).astype(bf16)
    lane = lax.broadcasted_iota(jnp.int32, (RB, 128), 1)
    tile = jnp.where(lane == 0, hi.astype(f32), jnp.where(lane == 1, mid.astype(f32), low.astype(f32)))
    G2B[x, z, :, PW:] = tile.astype(bf16)
    g2b.first()
    g2a.second(0)
    g2b.second(0)

    @pl.when(y == 2)
    def _():
        for p in range(2):
            DX[xh, p] = Dv[p]
        send(DX.at[xh], DX.at[xh], dxs, dxr, xdev(2))

    gather_forward(g2a, g2b)

    def gap_piece(k, xl_, zz):
        col = 2 * (k // 2) + xl_
        return G2A[col, zz] if k % 2 == 0 else G2B[col, zz, :, 0:PW]

    def share(xl_, zz):
        def one(col):
            tile = G2B[col, zz, :, PW:].astype(f32)
            return (tile[0:1, 0:1] + tile[0:1, 1:2]) + tile[0:1, 2:3]

        return one(xl_) + one(2 + xl_)

    def inverse(l):
        return 1.0 / ((CS[0, l : l + 1, :] + CS[1, l : l + 1, :]) / (32.0 * D) + epsilon_gap)

    def scaled_rows(zz, xl_):
        rows = pl.ds(pl.multiple_of(zz * 32 + xl_ * RB, RB), RB)
        for k in range(4):
            cols = slice(k * PW, (k + 1) * PW)
            gate = PR[5:6, cols] + vec_ref[0:1, cols]
            factor = jnp.where(y == 2, jnp.ones_like(gate), gate * 0.125)
            DZ[rows, cols] = (gap_piece(k, xl_, zz).astype(f32) * factor).astype(bf16)

    for i, dz in enumerate((0, 1, 3, 2)):
        gather_group(g2a, g2b, dz)
        zz = turn(z, -dz)

        def both(j, carry, zz=zz):
            scaled_rows(zz, j)
            return carry

        lax.fori_loop(0, 2, both, 0, unroll=True)
        rows = pl.ds(pl.multiple_of(zz * 32, 32), 32)
        orows = pl.ds(pl.multiple_of(128 + zz * 32, 32), 32)
        send(DZ.at[rows], DZ.at[orows], dzs.at[i], dzr.at[i], sib)


    for l in range(8):
        CS[0, l : l + 1, :] = jnp.broadcast_to(share(l % 2, l // 2), (1, 128))
    send(CS.at[0], CS.at[1], scs.at[0], scr.at[0], sib)
    live = y < 3
    arrived(HS, xr.at[0])
    for i, dz in enumerate((0, 1, 3, 2)):
        orows = pl.ds(pl.multiple_of(128 + turn(z, -dz) * 32, 32), 32)
        arrived(DZ.at[orows], dzr.at[i])
    DA[:, 0:HU] = lax.dot_general(DZ[...], W[0], NT, preferred_element_type=f32)
    arrived(CS.at[1], scr.at[0])
    for l in range(8):
        inv = jnp.where(y == 2, 1.0, inverse(l)[:, 0:1])
        IV[l * RB : (l + 1) * RB, :] = jnp.broadcast_to(inv, (RB, 256))
    for s in range(2):
        rows = slice(s * 128, (s + 1) * 128)
        value, slope = gelu_parts(H[0] if s == 0 else HS[...])
        dh = jnp.where(live, DA[rows, :] * slope * IV[...], 0.0)
        DA[rows, :] = dh
        dhb[rows, :] = dh.astype(bf16)

    arrived(XH.at[other], xr.at[2])

    SM[...] = jnp.zeros_like(SM)

    def small(i, carry):
        cols = pl.ds(pl.multiple_of(i * CW, CW), CW)
        du = jnp.dot(dhb[:, 0:HU], U[:, cols], preferred_element_type=f32)
        dx = du * XH[:, cols].astype(f32)
        p3 = 1.0 + PR[3:4, cols]
        rows = [jnp.zeros((8, CW), f32) for _ in range(4)]
        for l in range(8):
            starts = [l * RB + k for k in (0, 8, 128, 136)]
            plain = sum(du[k : k + 8] for k in starts)
            norm = sum(dx[k : k + 8] for k in starts)
            scale = p3 + E[l % 2, l // 2, :, cols]
            for k, term in enumerate((scale * norm, scale * plain, plain, norm)):
                rows[k] += term
        rows = [jnp.sum(row, axis=0, keepdims=True) for row in rows]
        SM[0:1, cols] = rows[0]
        SM[1:2, cols] = rows[1]
        SM[2:3, cols] = rows[2]
        SM[3:4, cols] = (1.0 + PR[0:1, cols]) * rows[3] + PR[1:2, cols] * rows[2]
        return carry

    lax.fori_loop(0, D // CW, small, 0)

    own_row = pl.ds(z * 2 + xl, 1)
    inv_own = (1.0 / ((CS[0, own_row, :] + CS[1, own_row, :]) / (32.0 * D) + epsilon_gap))[:, 0:1]

    @pl.when(y == 2)
    def _():
        arrived(DX.at[1 - xh], dxr)
        for k in range(4):
            score_out[own_rows, k * PW : (k + 1) * PW] = DX[k // 2, k % 2].astype(f32) * inv_own

    @pl.when(y != 2)
    def _():
        for k in range(4):
            score_out[own_rows, k * PW : (k + 1) * PW] = gap_piece(k, xl, z).astype(f32) * inv_own

    send(score_out.at[own_rows], score_out.at[own_rows], scs.at[1], scr.at[1], sib)

    own_row = pl.ds(z * 2 + xl, 1)
    inv_own = (1.0 / ((CS[0, own_row, :] + CS[1, own_row, :]) / (32.0 * D) + epsilon_gap))[:, 0:1]
    for p in range(2):
        fake, x0 = yF[0, p].astype(f32), X0[p].astype(f32)
        cot = jnp.where(y == 2, fake - x0, Dv[p].astype(f32) * inv_own) * 0.125
        row = jnp.sum(cot * Z[p], axis=0, keepdims=True)
        SM[4:5, own_cols(p)] = jnp.where(jnp.logical_or(y == 0, y == 2), row, 0.0)

    for k in range(32):
        start = k * SW // 128 * 128
        window = SM[:, start : start + 256]
        off = k * SW - start
        if off:
            window = pltpu.roll(window, 256 - off, 1)
        f_, t_ = k // 4, k % 4
        row = f_ % 4 * 8
        T[t_ % 2, (t_ // 2) * 2 + f_ // 4, row : row + 8] = window

    T16[...] = T[...].astype(bf16)
    near = [(dx, dc) for dc in range(2) for dx in (0, 1, 3, 2) if dx + dc]
    for k, (dx, dc) in enumerate(near):
        c_ = c if dc == 0 else 1 - c
        send(T16.at[c_, turn(x, dx)], TX.at[k], t1s.at[k], t1r.at[k], device(turn(x, dx), y, z, c_))

    live_rows = jnp.where(live, IV[...], 0.0)
    for s in range(2):
        rows = slice(s * 128, (s + 1) * 128)
        value = gelu_parts(H[0] if s == 0 else HS[...])[0]
        dht[:, rows] = DA[rows, :].T.astype(bf16)
        at[:, rows] = (value * live_rows).T.astype(bf16)
    arrived(uu.at[other], xr.at[1])

    def product(left, right, out):
        def step(i, carry):
            cols = pl.ds(pl.multiple_of(i * CW, CW), CW)
            out[:, cols] = jnp.dot(left[...], right[:, cols], preferred_element_type=f32)[0:HU]
            return carry

        lax.fori_loop(0, D // CW, step, 0)

    product(dht, uu, GU)
    for k in range(7):
        arrived(TX.at[k], t1r.at[k])
    total = T[c, x]
    for k in range(7):
        total += TX[k].astype(f32)
    for z_ in range(4):
        T3[z_] = total[z_ * 8 : z_ * 8 + 8]
    for k, d in enumerate(FAR):
        send(T3.at[turn(z, d)], TZ.at[k], t2s.at[k], t2r.at[k], zdev(d))

    @pl.when(is_gen)
    def _():
        for k in range(4):
            d = (0,) + FAR
            send(T3.at[turn(z, d[k])], TZ.at[3 + k], t2s.at[3 + k], t2r.at[3 + k], device(x, twin, turn(z, d[k]), c))

    for k in range(3):
        arrived(TZ.at[k], t2r.at[k])
    small_out[...] = T3[z] + TZ[0] + TZ[1] + TZ[2]

    @pl.when(is_gen)
    def _():
        for k in range(4):
            arrived(TZ.at[3 + k], t2r.at[3 + k])
            sent(TZ.at[3 + k], t2s.at[3 + k])
        small_out[...] = small_out[...] + (TZ[3] + TZ[4] + TZ[5] + TZ[6])

    arrived(score_out.at[pl.ds(pl.multiple_of((1 - c) * RB, RB), RB)], scr.at[1])
    sent(score_out.at[own_rows], scs.at[1])
    sent(CS.at[0], scs.at[0])
    for k in range(7):
        sent(TX.at[k], t1s.at[k])
    for k in range(3):
        sent(TZ.at[k], t2s.at[k])
    for g in (g1a, g1b, g2a, g2b):
        g.drain()
    sent(UT.at[0], wss.at[0])
    sent(down_ref.at[0], wss.at[1])
    for src, dst, k in shared:
        sent(src, xs.at[k])
    for p, zs, rs, first, second, peer in parts:
        for d in FAR:
            if p == 0:
                sent(rs.at[0], rsAs.at[d - 1])
            else:
                for xh_ in range(2):
                    sent(rs.at[0, pl.ds(0, 2)], rsBs.at[d - 1, xh_])
            sent(r2.at[p, 0], rs2s.at[p, d - 1])
    for i in range(4):
        sent(DZ.at[pl.ds(0, 32)], dzs.at[i])

    @pl.when(is_gen)
    def _():
        y_drain(yS, 0)

    @pl.when(jnp.logical_not(is_gen))
    def _():
        y_drain(yF, 1)
        for d in FAR:
            sent(E.at[0, 0], es.at[d - 1])
        sent(E.at[0], es.at[3])

    @pl.when(y == 2)
    def _():
        sent(DX.at[0], dxs)


def place_kernel(gu, at, dz, score, small, up_out, down_out, score_out, small_out, gd, sems, down_sems):
    cuts = ((0, 56), (56, 56), (112, 56), (168, 48))
    copies = [pltpu.make_async_copy(score, score_out, sems.at[0])]
    for k, (start, size) in enumerate(cuts):
        rows = pl.ds(start, size)
        copies.append(pltpu.make_async_copy(gu.at[rows], up_out.at[0, rows], sems.at[1 + k]))
    for cp in copies:
        cp.start()
    for k in range(5):
        small_out[k] = small[k : k + 1, 0:SW]
    for i in range(D // CW):
        cols = pl.ds(i * CW, CW)
        gd[:, cols] = jnp.dot(at[...], dz[:, cols], preferred_element_type=f32)[0:HU]
        cp = pltpu.make_async_copy(gd.at[:, cols], down_out.at[0, :, cols], down_sems.at[i])
        cp.start()
        copies.append(cp)
    for cp in copies:
        cp.wait()


def per_device(noise_in, noise, timesteps, up_weight, down_weight, small_params):
    dma = pltpu.SemaphoreType.DMA
    vm = pltpu.VMEM
    vmem = pl.BlockSpec(memory_space=pltpu.VMEM)
    hbm = pl.BlockSpec(memory_space=pl.ANY)
    scratch = [
        vm((4, D), f32),
        vm((32, D), bf16),
        vm((32, D), bf16),
        vm((256, D), bf16),
        vm((5, 3, D), f32),
        vm((8, D), f32),
        vm((HP, 256), bf16),
        vm((128, 256), f32),
        vm((HU, D), bf16),
        vm((2, D, HU), bf16),
        vm((2, HU, D), bf16),
        vm((2, 4, 1, D), f32),
        vm((2, 4, 4, RB, PW), bf16),
        vm((4, 4, RB, PW), bf16),
        vm((4, 4, RB, PW + 128), bf16),
        vm((2, 2, RB, PW), bf16),
        vm((256, D), bf16),
        vm((2, 128, HP), f32),
        vm((128, HP), f32),
        vm((2, 128, HP), bf16),
        vm((256, HP), f32),
        vm((256, HP), bf16),
        vm((4, 4, RB, PW), bf16),
        vm((4, 4, RB, PW), bf16),
        vm((3, 4, RB, PW), bf16),
        vm((3, 4, RB, PW), bf16),
        vm((2, RB, PW), f32),
        vm((2, 4, RB, PW), bf16),
        vm((2, 3, RB, PW), bf16),
        vm((2, RB, PW), f32),
        vm((2, 2, RB, PW), bf16),
        vm((2, 2, RB, PW), bf16),
        vm((2, RB, PW), bf16),
        vm((2, RB, PW), bf16),
        vm((2, 8, 128), f32),
        vm((8, D), f32),
        vm((2, 4, 32, 256), f32),
        vm((2, 4, 32, 256), bf16),
        vm((7, 32, 256), bf16),
        vm((4, 8, 256), f32),
        vm((7, 8, 256), f32),
        dma((5,)), dma((2,)), dma((2,)), dma((4,)), dma((4,)),
        dma((2, 3)), dma((2, 3)), dma((2, 4, 3)), dma((2, 4, 3)),
        dma((2, 3)), dma((2, 3)), dma((2, 4, 3)), dma((2, 4, 3)),
        dma((3,)), dma((3,)), dma((3, 2)), dma((3, 2)), dma((2, 3)), dma((2, 3)),
        dma((2, 2, 3)), dma((2, 2, 2)), dma((3,)), dma((3,)), dma(()), dma(()),
        dma((4,)), dma((4,)), dma((2,)), dma((2,)), dma((7,)), dma((7,)), dma((7,)), dma((7,)),
    ]
    parts = pl.pallas_call(
        chain_kernel,
        out_shape=[
            vm((HU, D), f32),
            vm((HP, 256), bf16),
            vm((256, D), bf16),
            vm((32, D), f32),
            vm((8, 256), f32),
        ],
        in_specs=[hbm, hbm, hbm, hbm, pl.BlockSpec(memory_space=pltpu.SMEM), hbm],
        out_specs=[vmem] * 5,
        scratch_shapes=scratch,
        compiler_params=pltpu.CompilerParams(
            collective_id=0, has_side_effects=True, vmem_limit_bytes=52 * 2**20
        ),
        name="chain",
    )(up_weight, down_weight, noise_in, noise, timesteps, jnp.transpose(small_params, (1, 0, 2)))
    up_grad, down_grad, score, small = pl.pallas_call(
        place_kernel,
        out_shape=[
            jax.ShapeDtypeStruct((1, HU, D), f32),
            jax.ShapeDtypeStruct((1, HU, D), f32),
            jax.ShapeDtypeStruct((32, D), f32),
            jax.ShapeDtypeStruct((5, 1, SW), f32),
        ],
        in_specs=[vmem] * 5,
        out_specs=[hbm, hbm, hbm, vmem],
        scratch_shapes=[vm((HU, D), f32), dma((5,)), dma((D // CW,))],
        compiler_params=pltpu.CompilerParams(vmem_limit_bytes=24 * 2**20),
        name="place",
    )(*parts)
    return (score, up_grad, down_grad, jnp.transpose(small, (1, 0, 2)))


def solution(mesh):
    in_specs = (
        P("fsdp", None),
        P("fsdp", None),
        P("fsdp"),
        P("group", ("fsdp", "tp"), None),
        P("group", ("fsdp", "tp"), None),
        P(),
    )
    out_specs = (
        P("fsdp", None),
        P("group", ("fsdp", "tp"), None),
        P("group", ("fsdp", "tp"), None),
        P("group", None, ("fsdp", "tp")),
    )
    return jax.shard_map(
        per_device, mesh=mesh, in_specs=in_specs, out_specs=out_specs, check_vma=False
    )
```

```python
import functools
import math

import jax
import jax.numpy as jnp
from jax import lax
from jax.experimental import pallas as pl
from jax.experimental.pallas import tpu as pltpu
from jax.sharding import PartitionSpec as P

MESH = pl.DeviceIdType.MESH
bf16, f32 = jnp.bfloat16, jnp.float32
gen_time = 999.0
epsilon_norm = 1e-06
epsilon_gap = 1e-05

D = 5120
HU = 216
HP = 256
RB = 16
PW = 1280
SW = 160
CW = 1024
NT = (((1,), (1,)), ((), ()))
FAR = (2, 1, 3)


def device(x, y, z, c):
    return (y, lax.rem(x, 2) * 4 + z, lax.div(x, 2) * 2 + c)


def turn(value, steps):
    return lax.rem(value + (steps % 4), 4)


def gelu_parts(h):
    k = math.sqrt(2.0 / math.pi)
    t = jnp.tanh(k * (h + 0.044715 * (h * h * h)))
    value = 0.5 * h * (1.0 + t)
    slope = 0.5 * (1.0 + t) + 0.5 * h * (1.0 - t * t) * (k * (1.0 + 3.0 * 0.044715 * (h * h)))
    return value, slope


def chain_kernel(
    up_ref, down_ref, nin_hbm, noi_hbm, time_ref, par_hbm,
    GU, at, DZ, score_out, small_out,
    vec_ref, nin_ref, noi_ref, uu, par_ref, PR, dht, IV, U, UT, W, E, G1, G2A, G2B, DX, XH, H, HS, SL, VA, act, DA, dhb,
    zsA, zsB, rsA, rsB, sf, ss2, r2, Z, yS, yF, X0, Dv, CS, SM, T, T16, TX, T3, TZ,
    loc, wss, wrs, es, er,
    a1s, a1r, a2s, a2r, b1s, b1r, b2s, b2r,
    rsAs, rsAr, rsBs, rsBr, rs2s, rs2r, ys, yr, xs, xr, dxs, dxr, dzs, dzr, scs, scr, t1s, t1r, t2s, t2r,
):
    y = lax.axis_index("group")
    fi = lax.axis_index("fsdp")
    ti = lax.axis_index("tp")
    xl, z = lax.div(fi, 4), lax.rem(fi, 4)
    xh, c = lax.div(ti, 2), lax.rem(ti, 2)
    x = xh * 2 + xl
    role = jnp.maximum(y - 1, 0)
    is_gen = y < 2
    pending = []

    def xdev(d):
        return device(turn(x, d), y, z, c)

    def zdev(d):
        return device(x, y, turn(z, d), c)

    sib = device(x, y, z, 1 - c)

    def send(src, dst, s, r, dev):
        cp = pltpu.make_async_remote_copy(
            src_ref=src, dst_ref=dst, send_sem=s, recv_sem=r, device_id=dev, device_id_type=MESH
        )
        cp.start()
        return cp

    def sent(src, s):
        pltpu.make_async_copy(src, src, s).wait()

    def arrived(dst, r):
        pltpu.make_async_copy(dst, dst, r).wait()

    early = [
        pltpu.make_async_copy(nin_hbm, nin_ref, loc.at[3]),
        pltpu.make_async_copy(noi_hbm, noi_ref, loc.at[4]),
    ]
    loads = [
        pltpu.make_async_copy(up_ref.at[0], U, loc.at[0]),
        pltpu.make_async_copy(down_ref.at[0], W.at[0], loc.at[1]),
        pltpu.make_async_copy(par_hbm, par_ref, loc.at[2]),
    ]
    for cp in early + loads:
        cp.start()

    barrier = pltpu.get_barrier_semaphore()
    peers = [xdev(d) for d in FAR] + [zdev(d) for d in FAR]
    peers += [device(x, turn(y, d), z, c) for d in FAR] + [sib]
    twin = y + 1 - 2 * lax.rem(y, 2)
    peers += [device(turn(x, d), y, z, 1 - c) for d in FAR]
    peers += [device(x, twin, turn(z, d), c) for d in FAR]
    for dev in peers:
        pl.semaphore_signal(barrier, inc=1, device_id=dev, device_id_type=MESH)
    pl.semaphore_wait(barrier, len(peers))
    for cp in early:
        cp.wait()

    def own_cols(p):
        return pl.ds(pl.multiple_of(xh * (2 * PW) + p * PW, 128), PW)

    own_rows = pl.ds(pl.multiple_of(c * RB, RB), RB)

    class Gather:
        def __init__(self, buf, order, s1s, s1r, s2s, s2r):
            self.buf, self.order = buf, order
            self.sems = (s1s, s1r, s2s, s2r)

        def block(self, d1, d2):
            if self.order == "xz":
                return self.buf.at[turn(x, -d1), turn(z, -d2)]
            return self.buf.at[turn(x, -d2), turn(z, -d1)]

        def peer(self, ring, d):
            return xdev(d) if (self.order == "xz") == (ring == 1) else zdev(d)

        def first(self):
            own = self.block(0, 0)
            for d in FAR:
                send(own, own, self.sems[0].at[d - 1], self.sems[1].at[d - 1], self.peer(1, d))

        def second(self, d1):
            b = self.block(d1, 0)
            for d in FAR:
                send(b, b, self.sems[2].at[d1, d - 1], self.sems[3].at[d1, d - 1], self.peer(2, d))

        def wait1(self, d1):
            arrived(self.block(d1, 0), self.sems[1].at[d1 - 1])

        def wait2(self, d1, d2):
            arrived(self.block(d1, d2), self.sems[3].at[d1, d2 - 1])

        def drain(self):
            own = self.block(0, 0)
            for d in FAR:
                sent(own, self.sems[0].at[d - 1])
                for d1 in range(4):
                    sent(own, self.sems[2].at[d1, d - 1])

    def gather_start(A, B):
        A.first()
        B.first()
        A.second(0)
        B.second(0)

    def gather_forward(A, B):
        for d in (1, 3, 2):
            A.wait1(d)
            A.second(d)
            B.wait1(d)
            B.second(d)

    def gather_group(A, B, dz):
        if dz == 0:
            for d in FAR:
                B.wait2(0, d)
        else:
            for d1 in range(4):
                A.wait2(d1, dz)
            for d in FAR:
                B.wait2(dz, d)

    g1a = Gather(G1.at[0], "xz", a1s.at[0], a1r.at[0], a2s.at[0], a2r.at[0])
    g1b = Gather(G1.at[1], "zx", b1s.at[0], b1r.at[0], b2s.at[0], b2r.at[0])
    g2a = Gather(G2A, "xz", a1s.at[1], a1r.at[1], a2s.at[1], a2r.at[1])
    g2b = Gather(G2B, "zx", b1s.at[1], b1r.at[1], b2s.at[1], b2r.at[1])

    @pl.when(is_gen)
    def _():
        for p in range(2):
            G1[p, x, z] = nin_ref[own_rows, own_cols(p)]
        gather_start(g1a, g1b)

    loads[0].wait()

    def transpose(i, carry):
        cols = pl.ds(pl.multiple_of(i * CW, CW), CW)
        UT[0, cols, :] = U[:, cols].T
        return carry

    lax.fori_loop(0, D // CW, transpose, 0)
    send(UT.at[0], UT.at[1], wss.at[0], wrs.at[0], sib)
    send(down_ref.at[0], W.at[1], wss.at[1], wrs.at[1], sib)
    loads[2].wait()
    for j in range(5):
        PR[j : j + 1, :] = par_ref[j, pl.ds(role, 1), :]
    PR[5:6, :] = par_ref[4, 0:1, :]
    PR[6:7, :] = par_ref[4, 1:2, :]

    step_value = time_ref[0].astype(f32)
    lane = lax.broadcasted_iota(jnp.int32, (2, D // 2), 1).astype(f32)
    row = lax.broadcasted_iota(jnp.int32, (2, D // 2), 0)
    angles = jnp.where(row == 0, gen_time, step_value) * jnp.exp(-math.log(10000.0) * lane / (D // 2))
    vec_ref[0:2, 0 : D // 2] = jnp.cos(angles)
    vec_ref[0:2, D // 2 : D] = jnp.sin(angles)
    turn_angle = jnp.full((1, 128), 0.5 * math.pi, f32) * step_value / 1000.0
    vec_ref[2:3, :] = jnp.broadcast_to(jnp.cos(turn_angle)[:, 0:1], (1, D))
    vec_ref[3:4, :] = jnp.broadcast_to(jnp.sin(turn_angle)[:, 0:1], (1, D))

    @pl.when(is_gen)
    def _():
        for l in range(8):
            E[l // 4, l % 4] = vec_ref[0:1, :]

    @pl.when(jnp.logical_not(is_gen))
    def _():
        E[xl, z] = vec_ref[1:2, :]
        own = E.at[xl, z]
        for d in FAR:
            send(own, own, es.at[d - 1], er.at[d - 1], zdev(d))
        for d in FAR:
            arrived(E.at[xl, turn(z, -d)], er.at[d - 1])
        send(E.at[xl], E.at[xl], es.at[3], er.at[3], xdev(1))
        arrived(E.at[1 - xl], er.at[3])

    H[...] = jnp.zeros_like(H)
    act[...] = jnp.zeros_like(act)
    DA[...] = jnp.zeros_like(DA)

    def make_x0(p):
        total = yS[0, p].astype(f32) + yS[1, p].astype(f32)
        gate = PR[5:6, own_cols(p)] + vec_ref[0:1, own_cols(p)]
        X0[p] = (nin_ref[own_rows, own_cols(p)].astype(f32) + gate * total).astype(bf16)

    def y_send(buf, slot, p, k):
        own = buf.at[slot, p]
        for i, to in enumerate((3 - y, turn(y, 2), twin)):
            send(own, own, ys.at[k, p, i], yr.at[k, p, slot], device(x, to, z, c))

    def y_wait(buf, slot, p, k):
        arrived(buf.at[slot, p], yr.at[k, p, slot])

    def y_drain(buf, k):
        for p in range(2):
            for d in FAR:
                sent(buf.at[0, 0], ys.at[k, p, d - 1])

    @pl.when(jnp.logical_not(is_gen))
    def _():
        for p, g in ((0, g1a), (1, g1b)):
            y_wait(yS, 0, p, 0)
            y_wait(yS, 1, p, 0)
            make_x0(p)
            cols = own_cols(p)
            noisy = vec_ref[2:3, cols] * X0[p].astype(f32) + vec_ref[3:4, cols] * noi_ref[own_rows, cols].astype(f32)
            G1[p, x, z] = noisy.astype(bf16)
            g.first()
        g1a.second(0)
        g1b.second(0)

    gather_forward(g1a, g1b)

    def norm_rows(zz, xl_):
        rows = pl.ds(pl.multiple_of(zz * 32 + xl_ * RB, RB), RB)

        def piece(k):
            return G1[k % 2, 2 * (k // 2) + xl_, zz].astype(f32)

        mean = sum(jnp.sum(piece(k), axis=1, keepdims=True) for k in range(4)) / D
        var = sum(jnp.sum(jnp.square(piece(k) - mean), axis=1, keepdims=True) for k in range(4)) / D
        rstd = lax.rsqrt(var + epsilon_norm)
        for k in range(4):
            cols = slice(k * PW, (k + 1) * PW)
            e = E[xl_, zz, :, cols]
            scale = 1.0 + PR[3:4, cols] + e
            gain = (1.0 + PR[0:1, cols]) * scale
            bias = PR[1:2, cols] * scale + (PR[2:3, cols] + e)
            xhat = (piece(k) - mean) * rstd
            uu[rows, cols] = (xhat * gain + bias).astype(bf16)
            XH[rows, cols] = xhat.astype(bf16)

    for dz in (0, 1, 3, 2):
        gather_group(g1a, g1b, dz)
        zz = turn(z, -dz)

        def both(i, carry, zz=zz):
            norm_rows(zz, i)
            return carry

        lax.fori_loop(0, 2, both, 0, unroll=True)

    arrived(UT.at[1], wrs.at[0])
    for s in range(2):
        H[s, :, 0:HU] = jnp.dot(uu[0:128, :], UT[s], preferred_element_type=f32)
    for s in range(2):
        act[s] = gelu_parts(H[s])[0].astype(bf16)
    loads[1].wait()
    arrived(W.at[1], wrs.at[1])

    def z_piece(xh_, p):
        cols = slice((xh_ * 2 + p) * PW, (xh_ * 2 + p + 1) * PW)
        acc = jnp.dot(act[0, :, 0:HU], W[0, :, cols], preferred_element_type=f32)
        acc += jnp.dot(act[1, :, 0:HU], W[1, :, cols], preferred_element_type=f32)
        acc = acc.astype(bf16)
        for z_ in range(4):
            for xl_ in range(2):
                rows = acc[z_ * 32 + xl_ * RB : z_ * 32 + (xl_ + 1) * RB]
                if p == 0:
                    zsA[2 * xh_ + xl_, z_] = rows
                else:
                    zsB[z_, 2 * xh_ + xl_] = rows

    for xh_ in range(2):
        z_piece(xh_, 0)
        for xl_ in range(2):
            to = 2 * xh_ + xl_

            @pl.when(to != x)
            def _():
                d = lax.rem(to + 4 - x, 4)
                send(zsA.at[to], rsA.at[d - 1], rsAs.at[d - 1], rsAr.at[d - 1], device(to, y, z, c))

        z_piece(xh_, 1)
        two = pl.ds(2 * xh_, 2)
        for d in FAR:
            send(
                zsB.at[turn(z, d), two], rsB.at[d - 1, two],
                rsBs.at[d - 1, xh_], rsBr.at[d - 1, xh_], zdev(d),
            )

    half = pl.ds(0, 128)
    other = pl.ds(128, 128)
    shared = [
        (H.at[1], HS, 0),
        (uu.at[half], uu.at[other], 1),
        (XH.at[half], XH.at[other], 2),
    ]
    for src, dst, k in shared:
        send(src, dst, xs.at[k], xr.at[k], sib)

    parts = ((0, zsA, rsA, x, z, zdev), (1, zsB, rsB, z, x, xdev))
    for p, zs, rs, first, second, peer in parts:
        for d in FAR:
            if p == 0:
                arrived(rsA.at[d - 1], rsAr.at[d - 1])
            else:
                for xh_ in range(2):
                    arrived(rsB.at[d - 1, pl.ds(2 * xh_, 2)], rsBr.at[d - 1, xh_])

        for d in FAR + (0,):
            to = turn(second, d)
            total = zs[first, to].astype(f32)
            for k in range(3):
                total += rs[k, to].astype(f32)
            if d == 0:
                sf[p] = total
            else:
                ss2[p, to] = total.astype(bf16)
                send(ss2.at[p, to], r2.at[p, d - 1], rs2s.at[p, d - 1], rs2r.at[p, d - 1], peer(d))
    for p, zs, rs, first, second, peer in parts:
        for d in FAR:
            arrived(r2.at[p, d - 1], rs2r.at[p, d - 1])
        total = sf[p]
        for d in range(3):
            total += r2[p, d].astype(f32)
        Z[p] = total

        @pl.when(is_gen)
        def _(p=p, total=total):
            yS[y, p] = total.astype(bf16)
            y_send(yS, y, p, 0)

        @pl.when(jnp.logical_not(is_gen))
        def _(p=p, total=total):
            gate = PR[4:5, own_cols(p)] + vec_ref[1:2, own_cols(p)]
            yF[y - 2, p] = (G1[p, x, z].astype(f32) + gate * total).astype(bf16)
            y_send(yF, y - 2, p, 1)

    arrived(HS, xr.at[0])
    for s in range(2):
        value, slope = gelu_parts(H[0] if s == 0 else HS[...])
        SL[s], VA[s] = slope, value

    @pl.when(is_gen)
    def _():
        for p in range(2):
            y_wait(yS, 1 - y, p, 0)
            make_x0(p)
            Z[p] = yS[0, p].astype(f32) + yS[1, p].astype(f32)

    dist = jnp.zeros((1, 1), f32)
    for p, g in ((0, g2a), (1, g2b)):
        @pl.when(is_gen)
        def _(p=p):
            y_wait(yF, 0, p, 1)
            y_wait(yF, 1, p, 1)

        @pl.when(jnp.logical_not(is_gen))
        def _(p=p):
            y_wait(yF, 3 - y, p, 1)

        fake, real, x0 = yF[0, p].astype(f32), yF[1, p].astype(f32), X0[p].astype(f32)
        gap = (fake - real).astype(bf16)
        Dv[p] = gap
        dist += jnp.sum(jnp.sum(jnp.abs(x0 - real), axis=0, keepdims=True), axis=1, keepdims=True)
        gate = PR[6:7, own_cols(p)] + vec_ref[1:2, own_cols(p)]
        critic = ((fake - x0) * 0.125 * gate).astype(bf16)
        block = jnp.where(y == 2, critic, gap)
        if p == 0:
            G2A[x, z] = block
            g2a.first()
        else:
            G2B[x, z, :, 0:PW] = block
    hi = dist.astype(bf16)
    mid = (dist - hi.astype(f32)).astype(bf16)
    low = (dist - hi.astype(f32) - mid.astype(f32)).astype(bf16)
    lane = lax.broadcasted_iota(jnp.int32, (RB, 128), 1)
    tile = jnp.where(lane == 0, hi.astype(f32), jnp.where(lane == 1, mid.astype(f32), low.astype(f32)))
    G2B[x, z, :, PW:] = tile.astype(bf16)
    g2b.first()
    g2a.second(0)
    g2b.second(0)

    @pl.when(y == 2)
    def _():
        for p in range(2):
            DX[xh, p] = Dv[p]
        send(DX.at[xh], DX.at[xh], dxs, dxr, xdev(2))

    gather_forward(g2a, g2b)

    def gap_piece(k, xl_, zz):
        col = 2 * (k // 2) + xl_
        return G2A[col, zz] if k % 2 == 0 else G2B[col, zz, :, 0:PW]

    def share(xl_, zz):
        def one(col):
            tile = G2B[col, zz, :, PW:].astype(f32)
            return (tile[0:1, 0:1] + tile[0:1, 1:2]) + tile[0:1, 2:3]

        return one(xl_) + one(2 + xl_)

    def inverse(l):
        return 1.0 / ((CS[0, l : l + 1, :] + CS[1, l : l + 1, :]) / (32.0 * D) + epsilon_gap)

    def scaled_rows(zz, xl_):
        rows = pl.ds(pl.multiple_of(zz * 32 + xl_ * RB, RB), RB)
        for k in range(4):
            cols = slice(k * PW, (k + 1) * PW)
            gate = PR[5:6, cols] + vec_ref[0:1, cols]
            factor = jnp.where(y == 2, jnp.ones_like(gate), gate * 0.125)
            DZ[rows, cols] = (gap_piece(k, xl_, zz).astype(f32) * factor).astype(bf16)

    for i, dz in enumerate((0, 1, 3, 2)):
        gather_group(g2a, g2b, dz)
        zz = turn(z, -dz)

        def both(j, carry, zz=zz):
            scaled_rows(zz, j)
            return carry

        lax.fori_loop(0, 2, both, 0, unroll=True)
        rows = pl.ds(pl.multiple_of(zz * 32, 32), 32)
        orows = pl.ds(pl.multiple_of(128 + zz * 32, 32), 32)
        send(DZ.at[rows], DZ.at[orows], dzs.at[i], dzr.at[i], sib)


    for l in range(8):
        CS[0, l : l + 1, :] = jnp.broadcast_to(share(l % 2, l // 2), (1, 128))
    send(CS.at[0], CS.at[1], scs.at[0], scr.at[0], sib)
    live = y < 3
    for i, dz in enumerate((0, 1, 3, 2)):
        orows = pl.ds(pl.multiple_of(128 + turn(z, -dz) * 32, 32), 32)
        arrived(DZ.at[orows], dzr.at[i])
    DA[:, 0:HU] = lax.dot_general(DZ[...], W[0], NT, preferred_element_type=f32)
    arrived(CS.at[1], scr.at[0])
    for l in range(8):
        inv = jnp.where(y == 2, 1.0, inverse(l)[:, 0:1])
        IV[l * RB : (l + 1) * RB, :] = jnp.broadcast_to(inv, (RB, 256))
    for s in range(2):
        rows = slice(s * 128, (s + 1) * 128)
        dh = jnp.where(live, DA[rows, :] * SL[s] * IV[...], 0.0)
        DA[rows, :] = dh
        dhb[rows, :] = dh.astype(bf16)

    arrived(XH.at[other], xr.at[2])

    SM[...] = jnp.zeros_like(SM)

    def small(i, carry):
        cols = pl.ds(pl.multiple_of(i * CW, CW), CW)
        du = jnp.dot(dhb[:, 0:HU], U[:, cols], preferred_element_type=f32)
        dx = du * XH[:, cols].astype(f32)
        p3 = 1.0 + PR[3:4, cols]
        rows = [jnp.zeros((8, CW), f32) for _ in range(4)]
        for l in range(8):
            starts = [l * RB + k for k in (0, 8, 128, 136)]
            plain = sum(du[k : k + 8] for k in starts)
            norm = sum(dx[k : k + 8] for k in starts)
            scale = p3 + E[l % 2, l // 2, :, cols]
            for k, term in enumerate((scale * norm, scale * plain, plain, norm)):
                rows[k] += term
        rows = [jnp.sum(row, axis=0, keepdims=True) for row in rows]
        SM[0:1, cols] = rows[0]
        SM[1:2, cols] = rows[1]
        SM[2:3, cols] = rows[2]
        SM[3:4, cols] = (1.0 + PR[0:1, cols]) * rows[3] + PR[1:2, cols] * rows[2]
        return carry

    lax.fori_loop(0, D // CW, small, 0, unroll=True)

    own_row = pl.ds(z * 2 + xl, 1)
    inv_own = (1.0 / ((CS[0, own_row, :] + CS[1, own_row, :]) / (32.0 * D) + epsilon_gap))[:, 0:1]
    for p in range(2):
        fake, x0 = yF[0, p].astype(f32), X0[p].astype(f32)
        cot = jnp.where(y == 2, fake - x0, Dv[p].astype(f32) * inv_own) * 0.125
        row = jnp.sum(cot * Z[p], axis=0, keepdims=True)
        SM[4:5, own_cols(p)] = jnp.where(jnp.logical_or(y == 0, y == 2), row, 0.0)

    for k in range(32):
        start = k * SW // 128 * 128
        window = SM[:, start : start + 256]
        off = k * SW - start
        if off:
            window = pltpu.roll(window, 256 - off, 1)
        f_, t_ = k // 4, k % 4
        row = f_ % 4 * 8
        T[t_ % 2, (t_ // 2) * 2 + f_ // 4, row : row + 8] = window

    T16[...] = T[...].astype(bf16)
    near = [(dx, dc) for dx in (2, 1, 3, 0) for dc in range(2) if dx + dc]
    for k, (dx, dc) in enumerate(near):
        c_ = c if dc == 0 else 1 - c
        send(T16.at[c_, turn(x, dx)], TX.at[k], t1s.at[k], t1r.at[k], device(turn(x, dx), y, z, c_))


    @pl.when(y == 2)
    def _():
        arrived(DX.at[1 - xh], dxr)
        for k in range(4):
            score_out[own_rows, k * PW : (k + 1) * PW] = DX[k // 2, k % 2].astype(f32) * inv_own

    @pl.when(y != 2)
    def _():
        for k in range(4):
            score_out[own_rows, k * PW : (k + 1) * PW] = gap_piece(k, xl, z).astype(f32) * inv_own

    send(score_out.at[own_rows], score_out.at[own_rows], scs.at[1], scr.at[1], sib)

    live_rows = jnp.where(live, IV[...], 0.0)
    for s in range(2):
        rows = slice(s * 128, (s + 1) * 128)
        value = VA[s]
        dht[:, rows] = DA[rows, :].T.astype(bf16)
        at[:, rows] = (value * live_rows).T.astype(bf16)
    arrived(uu.at[other], xr.at[1])

    def product(left, right, out):
        def step(i, carry):
            cols = pl.ds(pl.multiple_of(i * CW, CW), CW)
            out[:, cols] = jnp.dot(left[...], right[:, cols], preferred_element_type=f32)[0:HU]
            return carry

        lax.fori_loop(0, D // CW, step, 0, unroll=True)

    product(dht, uu, GU)
    for k in range(7):
        arrived(TX.at[k], t1r.at[k])
    total = T[c, x]
    for k in range(7):
        total += TX[k].astype(f32)
    for z_ in range(4):
        T3[z_] = total[z_ * 8 : z_ * 8 + 8]
    @pl.when(is_gen)
    def _():
        for k in range(4):
            d = FAR + (0,)
            send(T3.at[turn(z, d[k])], TZ.at[3 + k], t2s.at[3 + k], t2r.at[3 + k], device(x, twin, turn(z, d[k]), c))

    for k, d in enumerate(FAR):
        send(T3.at[turn(z, d)], TZ.at[k], t2s.at[k], t2r.at[k], zdev(d))

    for k in range(3):
        arrived(TZ.at[k], t2r.at[k])
    small_out[...] = T3[z] + TZ[0] + TZ[1] + TZ[2]

    @pl.when(is_gen)
    def _():
        for k in range(4):
            arrived(TZ.at[3 + k], t2r.at[3 + k])
            sent(TZ.at[3 + k], t2s.at[3 + k])
        small_out[...] = small_out[...] + (TZ[3] + TZ[4] + TZ[5] + TZ[6])

    arrived(score_out.at[pl.ds(pl.multiple_of((1 - c) * RB, RB), RB)], scr.at[1])
    sent(score_out.at[own_rows], scs.at[1])
    sent(CS.at[0], scs.at[0])
    for k in range(7):
        sent(TX.at[k], t1s.at[k])
    for k in range(3):
        sent(TZ.at[k], t2s.at[k])
    for g in (g1a, g1b, g2a, g2b):
        g.drain()
    sent(UT.at[0], wss.at[0])
    sent(down_ref.at[0], wss.at[1])
    for src, dst, k in shared:
        sent(src, xs.at[k])
    for p, zs, rs, first, second, peer in parts:
        for d in FAR:
            if p == 0:
                sent(rs.at[0], rsAs.at[d - 1])
            else:
                for xh_ in range(2):
                    sent(rs.at[0, pl.ds(0, 2)], rsBs.at[d - 1, xh_])
            sent(r2.at[p, 0], rs2s.at[p, d - 1])
    for i in range(4):
        sent(DZ.at[pl.ds(0, 32)], dzs.at[i])

    @pl.when(is_gen)
    def _():
        y_drain(yS, 0)

    @pl.when(jnp.logical_not(is_gen))
    def _():
        y_drain(yF, 1)
        for d in FAR:
            sent(E.at[0, 0], es.at[d - 1])
        sent(E.at[0], es.at[3])

    @pl.when(y == 2)
    def _():
        sent(DX.at[0], dxs)


def place_kernel(gu, at, dz, score, small, up_out, down_out, score_out, small_out, gd, sems, down_sems):
    cuts = ((0, 56), (56, 56), (112, 56), (168, 48))
    copies = [pltpu.make_async_copy(score, score_out, sems.at[0])]
    for k, (start, size) in enumerate(cuts):
        rows = pl.ds(start, size)
        copies.append(pltpu.make_async_copy(gu.at[rows], up_out.at[0, rows], sems.at[1 + k]))
    for cp in copies:
        cp.start()
    for k in range(5):
        small_out[k] = small[k : k + 1, 0:SW]
    for i in range(D // CW):
        cols = pl.ds(i * CW, CW)
        gd[:, cols] = jnp.dot(at[...], dz[:, cols], preferred_element_type=f32)[0:HU]
        cp = pltpu.make_async_copy(gd.at[:, cols], down_out.at[0, :, cols], down_sems.at[i])
        cp.start()
        copies.append(cp)
    for cp in copies:
        cp.wait()


def per_device(noise_in, noise, timesteps, up_weight, down_weight, small_params):
    dma = pltpu.SemaphoreType.DMA
    vm = pltpu.VMEM
    vmem = pl.BlockSpec(memory_space=pltpu.VMEM)
    hbm = pl.BlockSpec(memory_space=pl.ANY)
    scratch = [
        vm((4, D), f32),
        vm((32, D), bf16),
        vm((32, D), bf16),
        vm((256, D), bf16),
        vm((5, 3, D), f32),
        vm((8, D), f32),
        vm((HP, 256), bf16),
        vm((128, 256), f32),
        vm((HU, D), bf16),
        vm((2, D, HU), bf16),
        vm((2, HU, D), bf16),
        vm((2, 4, 1, D), f32),
        vm((2, 4, 4, RB, PW), bf16),
        vm((4, 4, RB, PW), bf16),
        vm((4, 4, RB, PW + 128), bf16),
        vm((2, 2, RB, PW), bf16),
        vm((256, D), bf16),
        vm((2, 128, HP), f32),
        vm((128, HP), f32),
        vm((2, 128, HP), f32),
        vm((2, 128, HP), f32),
        vm((2, 128, HP), bf16),
        vm((256, HP), f32),
        vm((256, HP), bf16),
        vm((4, 4, RB, PW), bf16),
        vm((4, 4, RB, PW), bf16),
        vm((3, 4, RB, PW), bf16),
        vm((3, 4, RB, PW), bf16),
        vm((2, RB, PW), f32),
        vm((2, 4, RB, PW), bf16),
        vm((2, 3, RB, PW), bf16),
        vm((2, RB, PW), f32),
        vm((2, 2, RB, PW), bf16),
        vm((2, 2, RB, PW), bf16),
        vm((2, RB, PW), bf16),
        vm((2, RB, PW), bf16),
        vm((2, 8, 128), f32),
        vm((8, D), f32),
        vm((2, 4, 32, 256), f32),
        vm((2, 4, 32, 256), bf16),
        vm((7, 32, 256), bf16),
        vm((4, 8, 256), f32),
        vm((7, 8, 256), f32),
        dma((5,)), dma((2,)), dma((2,)), dma((4,)), dma((4,)),
        dma((2, 3)), dma((2, 3)), dma((2, 4, 3)), dma((2, 4, 3)),
        dma((2, 3)), dma((2, 3)), dma((2, 4, 3)), dma((2, 4, 3)),
        dma((3,)), dma((3,)), dma((3, 2)), dma((3, 2)), dma((2, 3)), dma((2, 3)),
        dma((2, 2, 3)), dma((2, 2, 2)), dma((3,)), dma((3,)), dma(()), dma(()),
        dma((4,)), dma((4,)), dma((2,)), dma((2,)), dma((7,)), dma((7,)), dma((7,)), dma((7,)),
    ]
    parts = pl.pallas_call(
        chain_kernel,
        out_shape=[
            vm((HU, D), f32),
            vm((HP, 256), bf16),
            vm((256, D), bf16),
            vm((32, D), f32),
            vm((8, 256), f32),
        ],
        in_specs=[hbm, hbm, hbm, hbm, pl.BlockSpec(memory_space=pltpu.SMEM), hbm],
        out_specs=[vmem] * 5,
        scratch_shapes=scratch,
        compiler_params=pltpu.CompilerParams(
            collective_id=0, has_side_effects=True, vmem_limit_bytes=52 * 2**20
        ),
        name="chain",
    )(up_weight, down_weight, noise_in, noise, timesteps, jnp.transpose(small_params, (1, 0, 2)))
    up_grad, down_grad, score, small = pl.pallas_call(
        place_kernel,
        out_shape=[
            jax.ShapeDtypeStruct((1, HU, D), f32),
            jax.ShapeDtypeStruct((1, HU, D), f32),
            jax.ShapeDtypeStruct((32, D), f32),
            jax.ShapeDtypeStruct((5, 1, SW), f32),
        ],
        in_specs=[vmem] * 5,
        out_specs=[hbm, hbm, hbm, vmem],
        scratch_shapes=[vm((HU, D), f32), dma((5,)), dma((D // CW,))],
        compiler_params=pltpu.CompilerParams(vmem_limit_bytes=24 * 2**20),
        name="place",
    )(*parts)
    return (score, up_grad, down_grad, jnp.transpose(small, (1, 0, 2)))


def solution(mesh):
    in_specs = (
        P("fsdp", None),
        P("fsdp", None),
        P("fsdp"),
        P("group", ("fsdp", "tp"), None),
        P("group", ("fsdp", "tp"), None),
        P(),
    )
    out_specs = (
        P("fsdp", None),
        P("group", ("fsdp", "tp"), None),
        P("group", ("fsdp", "tp"), None),
        P("group", None, ("fsdp", "tp")),
    )
    return jax.shard_map(
        per_device, mesh=mesh, in_specs=in_specs, out_specs=out_specs, check_vma=False
    )
```

```python
import functools
import math

import jax
import jax.numpy as jnp
from jax import lax
from jax.experimental import pallas as pl
from jax.experimental.pallas import tpu as pltpu
from jax.sharding import PartitionSpec as P

MESH = pl.DeviceIdType.MESH
bf16, f32 = jnp.bfloat16, jnp.float32
gen_time = 999.0
epsilon_norm = 1e-06
epsilon_gap = 1e-05

D = 5120
HU = 216
HP = 256
RB = 16
PW = 1280
SW = 160
CW = 1024
NT = (((1,), (1,)), ((), ()))
FAR = (2, 1, 3)


def device(x, y, z, c):
    return (y, lax.rem(x, 2) * 4 + z, lax.div(x, 2) * 2 + c)


def turn(value, steps):
    return lax.rem(value + (steps % 4), 4)


def gelu_parts(h):
    k = math.sqrt(2.0 / math.pi)
    t = jnp.tanh(k * (h + 0.044715 * (h * h * h)))
    value = 0.5 * h * (1.0 + t)
    slope = 0.5 * (1.0 + t) + 0.5 * h * (1.0 - t * t) * (k * (1.0 + 3.0 * 0.044715 * (h * h)))
    return value, slope


def chain_kernel(
    up_ref, down_ref, nin_hbm, noi_hbm, time_ref, par_hbm,
    GU, at, DZ, score_out, small_out,
    vec_ref, nin_ref, noi_ref, uu, par_ref, PR, dht, IV, U, UT, W, E, G1, G2A, G2B, DX, XH, H, HS, SL, VA, act, DA, dhb,
    zsA, zsB, rsA, rsB, sf, ss2, r2, Z, yS, yF, X0, Dv, CS, SM, T, T16, TX, T3, TZ,
    loc, wss, wrs, es, er,
    a1s, a1r, a2s, a2r, b1s, b1r, b2s, b2r,
    rsAs, rsAr, rsBs, rsBr, rs2s, rs2r, ys, yr, xs, xr, dxs, dxr, dzs, dzr, scs, scr, t1s, t1r, t2s, t2r,
):
    y = lax.axis_index("group")
    fi = lax.axis_index("fsdp")
    ti = lax.axis_index("tp")
    xl, z = lax.div(fi, 4), lax.rem(fi, 4)
    xh, c = lax.div(ti, 2), lax.rem(ti, 2)
    x = xh * 2 + xl
    role = jnp.maximum(y - 1, 0)
    is_gen = y < 2
    pending = []

    def xdev(d):
        return device(turn(x, d), y, z, c)

    def zdev(d):
        return device(x, y, turn(z, d), c)

    sib = device(x, y, z, 1 - c)

    def send(src, dst, s, r, dev):
        cp = pltpu.make_async_remote_copy(
            src_ref=src, dst_ref=dst, send_sem=s, recv_sem=r, device_id=dev, device_id_type=MESH
        )
        cp.start()
        return cp

    def sent(src, s):
        pltpu.make_async_copy(src, src, s).wait()

    def arrived(dst, r):
        pltpu.make_async_copy(dst, dst, r).wait()

    early = [
        pltpu.make_async_copy(nin_hbm, nin_ref, loc.at[3]),
        pltpu.make_async_copy(noi_hbm, noi_ref, loc.at[4]),
    ]
    loads = [
        pltpu.make_async_copy(up_ref.at[0], U, loc.at[0]),
        pltpu.make_async_copy(down_ref.at[0], W.at[0], loc.at[1]),
        pltpu.make_async_copy(par_hbm, par_ref, loc.at[2]),
    ]
    for cp in early + loads:
        cp.start()

    barrier = pltpu.get_barrier_semaphore()
    peers = [xdev(d) for d in FAR] + [zdev(d) for d in FAR]
    peers += [device(x, turn(y, d), z, c) for d in FAR] + [sib]
    twin = y + 1 - 2 * lax.rem(y, 2)
    peers += [device(turn(x, d), y, z, 1 - c) for d in FAR]
    peers += [device(x, twin, turn(z, d), c) for d in FAR]
    for dev in peers:
        pl.semaphore_signal(barrier, inc=1, device_id=dev, device_id_type=MESH)
    pl.semaphore_wait(barrier, len(peers))
    for cp in early:
        cp.wait()

    def own_cols(p):
        return pl.ds(pl.multiple_of(xh * (2 * PW) + p * PW, 128), PW)

    own_rows = pl.ds(pl.multiple_of(c * RB, RB), RB)

    class Gather:
        def __init__(self, buf, order, s1s, s1r, s2s, s2r):
            self.buf, self.order = buf, order
            self.sems = (s1s, s1r, s2s, s2r)

        def block(self, d1, d2):
            if self.order == "xz":
                return self.buf.at[turn(x, -d1), turn(z, -d2)]
            return self.buf.at[turn(x, -d2), turn(z, -d1)]

        def peer(self, ring, d):
            return xdev(d) if (self.order == "xz") == (ring == 1) else zdev(d)

        def first(self, peers=FAR):
            own = self.block(0, 0)
            for d in peers:
                send(own, own, self.sems[0].at[d - 1], self.sems[1].at[d - 1], self.peer(1, d))

        def second(self, d1, peers=FAR):
            b = self.block(d1, 0)
            for d in peers:
                send(b, b, self.sems[2].at[d1, d - 1], self.sems[3].at[d1, d - 1], self.peer(2, d))

        def wait1(self, d1):
            arrived(self.block(d1, 0), self.sems[1].at[d1 - 1])

        def wait2(self, d1, d2):
            arrived(self.block(d1, d2), self.sems[3].at[d1, d2 - 1])

        def drain(self, halved=None):
            own = self.block(0, 0)
            for d in FAR:
                for d1 in range(-1, 4):
                    sem = self.sems[0].at[d - 1] if d1 < 0 else self.sems[2].at[d1, d - 1]
                    if halved is not None and d == 2 and d1 == (-1 if self.order == "xz" else 0):

                        @pl.when(jnp.logical_not(halved))
                        def _(sem=sem):
                            sent(own, sem)

                    else:
                        sent(own, sem)

    def gather_start(A, B):
        A.first()
        B.first()
        A.second(0)
        B.second(0)

    def gather_forward(A, B):
        for d in (1, 3, 2):
            A.wait1(d)
            A.second(d)
            B.wait1(d)
            B.second(d)

    def gather_group(A, B, dz):
        if dz == 0:
            for d in FAR:
                B.wait2(0, d)
        else:
            for d1 in range(4):
                A.wait2(d1, dz)
            for d in FAR:
                B.wait2(dz, d)

    g1a = Gather(G1.at[0], "xz", a1s.at[0], a1r.at[0], a2s.at[0], a2r.at[0])
    g1b = Gather(G1.at[1], "zx", b1s.at[0], b1r.at[0], b2s.at[0], b2r.at[0])
    g2a = Gather(G2A, "xz", a1s.at[1], a1r.at[1], a2s.at[1], a2r.at[1])
    g2b = Gather(G2B, "zx", b1s.at[1], b1r.at[1], b2s.at[1], b2r.at[1])

    @pl.when(is_gen)
    def _():
        for p in range(2):
            G1[p, x, z] = nin_ref[own_rows, own_cols(p)]
            cols = pl.ds(pl.multiple_of((1 - xh) * (2 * PW) + p * PW, 128), PW)
            G1[p, turn(x, 2), z] = nin_ref[own_rows, cols]
        g1a.first((1, 3))
        g1b.first()
        g1a.second(0)
        g1b.second(0, (1, 3))
        g1a.second(2)

    loads[0].wait()

    def transpose(i, carry):
        cols = pl.ds(pl.multiple_of(i * CW, CW), CW)
        UT[0, cols, :] = U[:, cols].T
        return carry

    lax.fori_loop(0, D // CW, transpose, 0)
    send(UT.at[0], UT.at[1], wss.at[0], wrs.at[0], sib)
    send(down_ref.at[0], W.at[1], wss.at[1], wrs.at[1], sib)
    loads[2].wait()
    for j in range(5):
        PR[j : j + 1, :] = par_ref[j, pl.ds(role, 1), :]
    PR[5:6, :] = par_ref[4, 0:1, :]
    PR[6:7, :] = par_ref[4, 1:2, :]

    step_value = time_ref[0].astype(f32)
    lane = lax.broadcasted_iota(jnp.int32, (2, D // 2), 1).astype(f32)
    row = lax.broadcasted_iota(jnp.int32, (2, D // 2), 0)
    angles = jnp.where(row == 0, gen_time, step_value) * jnp.exp(-math.log(10000.0) * lane / (D // 2))
    vec_ref[0:2, 0 : D // 2] = jnp.cos(angles)
    vec_ref[0:2, D // 2 : D] = jnp.sin(angles)
    turn_angle = jnp.full((1, 128), 0.5 * math.pi, f32) * step_value / 1000.0
    vec_ref[2:3, :] = jnp.broadcast_to(jnp.cos(turn_angle)[:, 0:1], (1, D))
    vec_ref[3:4, :] = jnp.broadcast_to(jnp.sin(turn_angle)[:, 0:1], (1, D))

    @pl.when(is_gen)
    def _():
        for l in range(8):
            E[l // 4, l % 4] = vec_ref[0:1, :]

    @pl.when(jnp.logical_not(is_gen))
    def _():
        E[xl, z] = vec_ref[1:2, :]
        own = E.at[xl, z]
        for d in FAR:
            send(own, own, es.at[d - 1], er.at[d - 1], zdev(d))
        for d in FAR:
            arrived(E.at[xl, turn(z, -d)], er.at[d - 1])
        send(E.at[xl], E.at[xl], es.at[3], er.at[3], xdev(1))
        arrived(E.at[1 - xl], er.at[3])

    H[...] = jnp.zeros_like(H)
    act[...] = jnp.zeros_like(act)
    DA[...] = jnp.zeros_like(DA)

    def make_x0(p):
        total = yS[0, p].astype(f32) + yS[1, p].astype(f32)
        gate = PR[5:6, own_cols(p)] + vec_ref[0:1, own_cols(p)]
        X0[p] = (nin_ref[own_rows, own_cols(p)].astype(f32) + gate * total).astype(bf16)

    def y_send(buf, slot, p, k):
        own = buf.at[slot, p]
        for i, to in enumerate((3 - y, turn(y, 2), twin)):
            send(own, own, ys.at[k, p, i], yr.at[k, p, slot], device(x, to, z, c))

    def y_wait(buf, slot, p, k):
        arrived(buf.at[slot, p], yr.at[k, p, slot])

    def y_drain(buf, k):
        for p in range(2):
            for d in FAR:
                sent(buf.at[0, 0], ys.at[k, p, d - 1])

    @pl.when(jnp.logical_not(is_gen))
    def _():
        for p, g in ((0, g1a), (1, g1b)):
            y_wait(yS, 0, p, 0)
            y_wait(yS, 1, p, 0)
            make_x0(p)
            cols = own_cols(p)
            noisy = vec_ref[2:3, cols] * X0[p].astype(f32) + vec_ref[3:4, cols] * noi_ref[own_rows, cols].astype(f32)
            G1[p, x, z] = noisy.astype(bf16)
            g.first()
        g1a.second(0)
        g1b.second(0)

    for d in (1, 3):
        g1a.wait1(d)
        g1a.second(d)
        g1b.wait1(d)
        g1b.second(d)

    @pl.when(jnp.logical_not(is_gen))
    def _():
        g1a.wait1(2)
        g1a.second(2)

    g1b.wait1(2)
    g1b.second(2)

    def norm_rows(zz, xl_):
        rows = pl.ds(pl.multiple_of(zz * 32 + xl_ * RB, RB), RB)

        def piece(k):
            return G1[k % 2, 2 * (k // 2) + xl_, zz].astype(f32)

        mean = sum(jnp.sum(piece(k), axis=1, keepdims=True) for k in range(4)) / D
        var = sum(jnp.sum(jnp.square(piece(k) - mean), axis=1, keepdims=True) for k in range(4)) / D
        rstd = lax.rsqrt(var + epsilon_norm)
        for k in range(4):
            cols = slice(k * PW, (k + 1) * PW)
            e = E[xl_, zz, :, cols]
            scale = 1.0 + PR[3:4, cols] + e
            gain = (1.0 + PR[0:1, cols]) * scale
            bias = PR[1:2, cols] * scale + (PR[2:3, cols] + e)
            xhat = (piece(k) - mean) * rstd
            uu[rows, cols] = (xhat * gain + bias).astype(bf16)
            XH[rows, cols] = xhat.astype(bf16)

    for dz in (0, 1, 3, 2):
        if dz:
            gather_group(g1a, g1b, dz)
        else:
            for d in (1, 3):
                g1b.wait2(0, d)

            @pl.when(jnp.logical_not(is_gen))
            def _():
                g1b.wait2(0, 2)

        zz = turn(z, -dz)

        def both(i, carry, zz=zz):
            norm_rows(zz, i)
            return carry

        lax.fori_loop(0, 2, both, 0, unroll=True)

    arrived(UT.at[1], wrs.at[0])
    for s in range(2):
        H[s, :, 0:HU] = jnp.dot(uu[0:128, :], UT[s], preferred_element_type=f32)
    for s in range(2):
        act[s] = gelu_parts(H[s])[0].astype(bf16)
    loads[1].wait()
    arrived(W.at[1], wrs.at[1])

    def z_piece(xh_, p):
        cols = slice((xh_ * 2 + p) * PW, (xh_ * 2 + p + 1) * PW)
        acc = jnp.dot(act[0, :, 0:HU], W[0, :, cols], preferred_element_type=f32)
        acc += jnp.dot(act[1, :, 0:HU], W[1, :, cols], preferred_element_type=f32)
        acc = acc.astype(bf16)
        for z_ in range(4):
            for xl_ in range(2):
                rows = acc[z_ * 32 + xl_ * RB : z_ * 32 + (xl_ + 1) * RB]
                if p == 0:
                    zsA[2 * xh_ + xl_, z_] = rows
                else:
                    zsB[z_, 2 * xh_ + xl_] = rows

    for xh_ in range(2):
        z_piece(xh_, 0)
        for xl_ in range(2):
            to = 2 * xh_ + xl_

            @pl.when(to != x)
            def _():
                d = lax.rem(to + 4 - x, 4)
                send(zsA.at[to], rsA.at[d - 1], rsAs.at[d - 1], rsAr.at[d - 1], device(to, y, z, c))

        z_piece(xh_, 1)
        two = pl.ds(2 * xh_, 2)
        for d in FAR:
            send(
                zsB.at[turn(z, d), two], rsB.at[d - 1, two],
                rsBs.at[d - 1, xh_], rsBr.at[d - 1, xh_], zdev(d),
            )

    half = pl.ds(0, 128)
    other = pl.ds(128, 128)
    shared = [
        (H.at[1], HS, 0),
        (uu.at[half], uu.at[other], 1),
        (XH.at[half], XH.at[other], 2),
    ]
    for src, dst, k in shared:
        send(src, dst, xs.at[k], xr.at[k], sib)

    parts = ((0, zsA, rsA, x, z, zdev), (1, zsB, rsB, z, x, xdev))
    for p, zs, rs, first, second, peer in parts:
        for d in FAR:
            if p == 0:
                arrived(rsA.at[d - 1], rsAr.at[d - 1])
            else:
                for xh_ in range(2):
                    arrived(rsB.at[d - 1, pl.ds(2 * xh_, 2)], rsBr.at[d - 1, xh_])

        for d in FAR + (0,):
            to = turn(second, d)
            total = zs[first, to].astype(f32)
            for k in range(3):
                total += rs[k, to].astype(f32)
            if d == 0:
                sf[p] = total
            else:
                ss2[p, to] = total.astype(bf16)
                send(ss2.at[p, to], r2.at[p, d - 1], rs2s.at[p, d - 1], rs2r.at[p, d - 1], peer(d))
    for p, zs, rs, first, second, peer in parts:
        for d in FAR:
            arrived(r2.at[p, d - 1], rs2r.at[p, d - 1])
        total = sf[p]
        for d in range(3):
            total += r2[p, d].astype(f32)
        Z[p] = total

        @pl.when(is_gen)
        def _(p=p, total=total):
            yS[y, p] = total.astype(bf16)
            y_send(yS, y, p, 0)

        @pl.when(jnp.logical_not(is_gen))
        def _(p=p, total=total):
            gate = PR[4:5, own_cols(p)] + vec_ref[1:2, own_cols(p)]
            yF[y - 2, p] = (G1[p, x, z].astype(f32) + gate * total).astype(bf16)
            y_send(yF, y - 2, p, 1)

    arrived(HS, xr.at[0])
    for s in range(2):
        value, slope = gelu_parts(H[0] if s == 0 else HS[...])
        SL[s], VA[s] = slope, value

    @pl.when(is_gen)
    def _():
        for p in range(2):
            y_wait(yS, 1 - y, p, 0)
            make_x0(p)
            Z[p] = yS[0, p].astype(f32) + yS[1, p].astype(f32)

    dist = jnp.zeros((1, 1), f32)
    for p, g in ((0, g2a), (1, g2b)):
        @pl.when(is_gen)
        def _(p=p):
            y_wait(yF, 0, p, 1)
            y_wait(yF, 1, p, 1)

        @pl.when(jnp.logical_not(is_gen))
        def _(p=p):
            y_wait(yF, 3 - y, p, 1)

        fake, real, x0 = yF[0, p].astype(f32), yF[1, p].astype(f32), X0[p].astype(f32)
        gap = (fake - real).astype(bf16)
        Dv[p] = gap
        dist += jnp.sum(jnp.sum(jnp.abs(x0 - real), axis=0, keepdims=True), axis=1, keepdims=True)
        gate = PR[6:7, own_cols(p)] + vec_ref[1:2, own_cols(p)]
        critic = ((fake - x0) * 0.125 * gate).astype(bf16)
        block = jnp.where(y == 2, critic, gap)
        if p == 0:
            G2A[x, z] = block
            g2a.first()
        else:
            G2B[x, z, :, 0:PW] = block
    hi = dist.astype(bf16)
    mid = (dist - hi.astype(f32)).astype(bf16)
    low = (dist - hi.astype(f32) - mid.astype(f32)).astype(bf16)
    lane = lax.broadcasted_iota(jnp.int32, (RB, 128), 1)
    tile = jnp.where(lane == 0, hi.astype(f32), jnp.where(lane == 1, mid.astype(f32), low.astype(f32)))
    G2B[x, z, :, PW:] = tile.astype(bf16)
    g2b.first()
    g2a.second(0)
    g2b.second(0)

    @pl.when(y == 2)
    def _():
        for p in range(2):
            DX[xh, p] = Dv[p]
        send(DX.at[xh], DX.at[xh], dxs, dxr, xdev(2))

    gather_forward(g2a, g2b)

    def gap_piece(k, xl_, zz):
        col = 2 * (k // 2) + xl_
        return G2A[col, zz] if k % 2 == 0 else G2B[col, zz, :, 0:PW]

    def share(xl_, zz):
        def one(col):
            tile = G2B[col, zz, :, PW:].astype(f32)
            return (tile[0:1, 0:1] + tile[0:1, 1:2]) + tile[0:1, 2:3]

        return one(xl_) + one(2 + xl_)

    def inverse(l):
        return 1.0 / ((CS[0, l : l + 1, :] + CS[1, l : l + 1, :]) / (32.0 * D) + epsilon_gap)

    def scaled_rows(zz, xl_):
        rows = pl.ds(pl.multiple_of(zz * 32 + xl_ * RB, RB), RB)
        for k in range(4):
            cols = slice(k * PW, (k + 1) * PW)
            gate = PR[5:6, cols] + vec_ref[0:1, cols]
            factor = jnp.where(y == 2, jnp.ones_like(gate), gate * 0.125)
            DZ[rows, cols] = (gap_piece(k, xl_, zz).astype(f32) * factor).astype(bf16)

    for i, dz in enumerate((0, 1, 3, 2)):
        gather_group(g2a, g2b, dz)
        zz = turn(z, -dz)

        def both(j, carry, zz=zz):
            scaled_rows(zz, j)
            return carry

        lax.fori_loop(0, 2, both, 0, unroll=True)
        rows = pl.ds(pl.multiple_of(zz * 32, 32), 32)
        orows = pl.ds(pl.multiple_of(128 + zz * 32, 32), 32)
        send(DZ.at[rows], DZ.at[orows], dzs.at[i], dzr.at[i], sib)


    for l in range(8):
        CS[0, l : l + 1, :] = jnp.broadcast_to(share(l % 2, l // 2), (1, 128))
    send(CS.at[0], CS.at[1], scs.at[0], scr.at[0], sib)
    live = y < 3
    for i, dz in enumerate((0, 1, 3, 2)):
        orows = pl.ds(pl.multiple_of(128 + turn(z, -dz) * 32, 32), 32)
        arrived(DZ.at[orows], dzr.at[i])
    DA[:, 0:HU] = lax.dot_general(DZ[...], W[0], NT, preferred_element_type=f32)
    arrived(CS.at[1], scr.at[0])
    for l in range(8):
        inv = jnp.where(y == 2, 1.0, inverse(l)[:, 0:1])
        IV[l * RB : (l + 1) * RB, :] = jnp.broadcast_to(inv, (RB, 256))
    for s in range(2):
        rows = slice(s * 128, (s + 1) * 128)
        dh = jnp.where(live, DA[rows, :] * SL[s] * IV[...], 0.0)
        DA[rows, :] = dh
        dhb[rows, :] = dh.astype(bf16)

    arrived(XH.at[other], xr.at[2])

    SM[...] = jnp.zeros_like(SM)

    def small(i, carry):
        cols = pl.ds(pl.multiple_of(i * CW, CW), CW)
        du = jnp.dot(dhb[:, 0:HU], U[:, cols], preferred_element_type=f32)
        dx = du * XH[:, cols].astype(f32)
        p3 = 1.0 + PR[3:4, cols]
        rows = [jnp.zeros((8, CW), f32) for _ in range(4)]
        for l in range(8):
            starts = [l * RB + k for k in (0, 8, 128, 136)]
            plain = sum(du[k : k + 8] for k in starts)
            norm = sum(dx[k : k + 8] for k in starts)
            scale = p3 + E[l % 2, l // 2, :, cols]
            for k, term in enumerate((scale * norm, scale * plain, plain, norm)):
                rows[k] += term
        rows = [jnp.sum(row, axis=0, keepdims=True) for row in rows]
        SM[0:1, cols] = rows[0]
        SM[1:2, cols] = rows[1]
        SM[2:3, cols] = rows[2]
        SM[3:4, cols] = (1.0 + PR[0:1, cols]) * rows[3] + PR[1:2, cols] * rows[2]
        return carry

    lax.fori_loop(0, D // CW, small, 0, unroll=True)

    own_row = pl.ds(z * 2 + xl, 1)
    inv_own = (1.0 / ((CS[0, own_row, :] + CS[1, own_row, :]) / (32.0 * D) + epsilon_gap))[:, 0:1]
    for p in range(2):
        fake, x0 = yF[0, p].astype(f32), X0[p].astype(f32)
        cot = jnp.where(y == 2, fake - x0, Dv[p].astype(f32) * inv_own) * 0.125
        row = jnp.sum(cot * Z[p], axis=0, keepdims=True)
        SM[4:5, own_cols(p)] = jnp.where(jnp.logical_or(y == 0, y == 2), row, 0.0)

    for k in range(32):
        start = k * SW // 128 * 128
        window = SM[:, start : start + 256]
        off = k * SW - start
        if off:
            window = pltpu.roll(window, 256 - off, 1)
        f_, t_ = k // 4, k % 4
        row = f_ % 4 * 8
        T[t_ % 2, (t_ // 2) * 2 + f_ // 4, row : row + 8] = window

    T16[...] = T[...].astype(bf16)
    near = [(dx, dc) for dx in (2, 1, 3, 0) for dc in range(2) if dx + dc]
    for k, (dx, dc) in enumerate(near):
        c_ = c if dc == 0 else 1 - c
        send(T16.at[c_, turn(x, dx)], TX.at[k], t1s.at[k], t1r.at[k], device(turn(x, dx), y, z, c_))


    @pl.when(y == 2)
    def _():
        arrived(DX.at[1 - xh], dxr)
        for k in range(4):
            score_out[own_rows, k * PW : (k + 1) * PW] = DX[k // 2, k % 2].astype(f32) * inv_own

    @pl.when(y != 2)
    def _():
        for k in range(4):
            score_out[own_rows, k * PW : (k + 1) * PW] = gap_piece(k, xl, z).astype(f32) * inv_own

    send(score_out.at[own_rows], score_out.at[own_rows], scs.at[1], scr.at[1], sib)

    live_rows = jnp.where(live, IV[...], 0.0)
    for s in range(2):
        rows = slice(s * 128, (s + 1) * 128)
        value = VA[s]
        dht[:, rows] = DA[rows, :].T.astype(bf16)
        at[:, rows] = (value * live_rows).T.astype(bf16)
    arrived(uu.at[other], xr.at[1])

    def product(left, right, out):
        def step(i, carry):
            cols = pl.ds(pl.multiple_of(i * CW, CW), CW)
            out[:, cols] = jnp.dot(left[...], right[:, cols], preferred_element_type=f32)[0:HU]
            return carry

        lax.fori_loop(0, D // CW, step, 0, unroll=True)

    product(dht, uu, GU)
    for k in range(7):
        arrived(TX.at[k], t1r.at[k])
    total = T[c, x]
    for k in range(7):
        total += TX[k].astype(f32)
    for z_ in range(4):
        T3[z_] = total[z_ * 8 : z_ * 8 + 8]
    @pl.when(is_gen)
    def _():
        for k in range(4):
            d = FAR + (0,)
            send(T3.at[turn(z, d[k])], TZ.at[3 + k], t2s.at[3 + k], t2r.at[3 + k], device(x, twin, turn(z, d[k]), c))

    for k, d in enumerate(FAR):
        send(T3.at[turn(z, d)], TZ.at[k], t2s.at[k], t2r.at[k], zdev(d))

    for k in range(3):
        arrived(TZ.at[k], t2r.at[k])
    small_out[...] = T3[z] + TZ[0] + TZ[1] + TZ[2]

    @pl.when(is_gen)
    def _():
        for k in range(4):
            arrived(TZ.at[3 + k], t2r.at[3 + k])
            sent(TZ.at[3 + k], t2s.at[3 + k])
        small_out[...] = small_out[...] + (TZ[3] + TZ[4] + TZ[5] + TZ[6])

    arrived(score_out.at[pl.ds(pl.multiple_of((1 - c) * RB, RB), RB)], scr.at[1])
    sent(score_out.at[own_rows], scs.at[1])
    sent(CS.at[0], scs.at[0])
    for k in range(7):
        sent(TX.at[k], t1s.at[k])
    for k in range(3):
        sent(TZ.at[k], t2s.at[k])
    for g in (g1a, g1b):
        g.drain(is_gen)
    for g in (g2a, g2b):
        g.drain()
    sent(UT.at[0], wss.at[0])
    sent(down_ref.at[0], wss.at[1])
    for src, dst, k in shared:
        sent(src, xs.at[k])
    for p, zs, rs, first, second, peer in parts:
        for d in FAR:
            if p == 0:
                sent(rs.at[0], rsAs.at[d - 1])
            else:
                for xh_ in range(2):
                    sent(rs.at[0, pl.ds(0, 2)], rsBs.at[d - 1, xh_])
            sent(r2.at[p, 0], rs2s.at[p, d - 1])
    for i in range(4):
        sent(DZ.at[pl.ds(0, 32)], dzs.at[i])

    @pl.when(is_gen)
    def _():
        y_drain(yS, 0)

    @pl.when(jnp.logical_not(is_gen))
    def _():
        y_drain(yF, 1)
        for d in FAR:
            sent(E.at[0, 0], es.at[d - 1])
        sent(E.at[0], es.at[3])

    @pl.when(y == 2)
    def _():
        sent(DX.at[0], dxs)


def place_kernel(gu, at, dz, score, small, up_out, down_out, score_out, small_out, gd, sems, down_sems):
    cuts = ((0, 56), (56, 56), (112, 56), (168, 48))
    copies = [pltpu.make_async_copy(score, score_out, sems.at[0])]
    for k, (start, size) in enumerate(cuts):
        rows = pl.ds(start, size)
        copies.append(pltpu.make_async_copy(gu.at[rows], up_out.at[0, rows], sems.at[1 + k]))
    for cp in copies:
        cp.start()
    for k in range(5):
        small_out[k] = small[k : k + 1, 0:SW]
    for i in range(D // CW):
        cols = pl.ds(i * CW, CW)
        gd[:, cols] = jnp.dot(at[...], dz[:, cols], preferred_element_type=f32)[0:HU]
        cp = pltpu.make_async_copy(gd.at[:, cols], down_out.at[0, :, cols], down_sems.at[i])
        cp.start()
        copies.append(cp)
    for cp in copies:
        cp.wait()


def per_device(noise_in, noise, timesteps, up_weight, down_weight, small_params):
    dma = pltpu.SemaphoreType.DMA
    vm = pltpu.VMEM
    vmem = pl.BlockSpec(memory_space=pltpu.VMEM)
    hbm = pl.BlockSpec(memory_space=pl.ANY)
    scratch = [
        vm((4, D), f32),
        vm((32, D), bf16),
        vm((32, D), bf16),
        vm((256, D), bf16),
        vm((5, 3, D), f32),
        vm((8, D), f32),
        vm((HP, 256), bf16),
        vm((128, 256), f32),
        vm((HU, D), bf16),
        vm((2, D, HU), bf16),
        vm((2, HU, D), bf16),
        vm((2, 4, 1, D), f32),
        vm((2, 4, 4, RB, PW), bf16),
        vm((4, 4, RB, PW), bf16),
        vm((4, 4, RB, PW + 128), bf16),
        vm((2, 2, RB, PW), bf16),
        vm((256, D), bf16),
        vm((2, 128, HP), f32),
        vm((128, HP), f32),
        vm((2, 128, HP), f32),
        vm((2, 128, HP), f32),
        vm((2, 128, HP), bf16),
        vm((256, HP), f32),
        vm((256, HP), bf16),
        vm((4, 4, RB, PW), bf16),
        vm((4, 4, RB, PW), bf16),
        vm((3, 4, RB, PW), bf16),
        vm((3, 4, RB, PW), bf16),
        vm((2, RB, PW), f32),
        vm((2, 4, RB, PW), bf16),
        vm((2, 3, RB, PW), bf16),
        vm((2, RB, PW), f32),
        vm((2, 2, RB, PW), bf16),
        vm((2, 2, RB, PW), bf16),
        vm((2, RB, PW), bf16),
        vm((2, RB, PW), bf16),
        vm((2, 8, 128), f32),
        vm((8, D), f32),
        vm((2, 4, 32, 256), f32),
        vm((2, 4, 32, 256), bf16),
        vm((7, 32, 256), bf16),
        vm((4, 8, 256), f32),
        vm((7, 8, 256), f32),
        dma((5,)), dma((2,)), dma((2,)), dma((4,)), dma((4,)),
        dma((2, 3)), dma((2, 3)), dma((2, 4, 3)), dma((2, 4, 3)),
        dma((2, 3)), dma((2, 3)), dma((2, 4, 3)), dma((2, 4, 3)),
        dma((3,)), dma((3,)), dma((3, 2)), dma((3, 2)), dma((2, 3)), dma((2, 3)),
        dma((2, 2, 3)), dma((2, 2, 2)), dma((3,)), dma((3,)), dma(()), dma(()),
        dma((4,)), dma((4,)), dma((2,)), dma((2,)), dma((7,)), dma((7,)), dma((7,)), dma((7,)),
    ]
    parts = pl.pallas_call(
        chain_kernel,
        out_shape=[
            vm((HU, D), f32),
            vm((HP, 256), bf16),
            vm((256, D), bf16),
            vm((32, D), f32),
            vm((8, 256), f32),
        ],
        in_specs=[hbm, hbm, hbm, hbm, pl.BlockSpec(memory_space=pltpu.SMEM), hbm],
        out_specs=[vmem] * 5,
        scratch_shapes=scratch,
        compiler_params=pltpu.CompilerParams(
            collective_id=0, has_side_effects=True, vmem_limit_bytes=52 * 2**20
        ),
        name="chain",
    )(up_weight, down_weight, noise_in, noise, timesteps, jnp.transpose(small_params, (1, 0, 2)))
    up_grad, down_grad, score, small = pl.pallas_call(
        place_kernel,
        out_shape=[
            jax.ShapeDtypeStruct((1, HU, D), f32),
            jax.ShapeDtypeStruct((1, HU, D), f32),
            jax.ShapeDtypeStruct((32, D), f32),
            jax.ShapeDtypeStruct((5, 1, SW), f32),
        ],
        in_specs=[vmem] * 5,
        out_specs=[hbm, hbm, hbm, vmem],
        scratch_shapes=[vm((HU, D), f32), dma((5,)), dma((D // CW,))],
        compiler_params=pltpu.CompilerParams(vmem_limit_bytes=24 * 2**20),
        name="place",
    )(*parts)
    return (score, up_grad, down_grad, jnp.transpose(small, (1, 0, 2)))


def solution(mesh):
    in_specs = (
        P("fsdp", None),
        P("fsdp", None),
        P("fsdp"),
        P("group", ("fsdp", "tp"), None),
        P("group", ("fsdp", "tp"), None),
        P(),
    )
    out_specs = (
        P("fsdp", None),
        P("group", ("fsdp", "tp"), None),
        P("group", ("fsdp", "tp"), None),
        P("group", None, ("fsdp", "tp")),
    )
    return jax.shard_map(
        per_device, mesh=mesh, in_specs=in_specs, out_specs=out_specs, check_vma=False
    )
```
